32 devices in a mesh: dp: 8 (over z, x), ns: 4 (over y, core).
Axes of the slice: x: 2, y: 2, z: 4, core: 2. Of those that a mesh axis runs over, the one named last changes fastest.
Arguments:
- patches: bfloat16 [32768, 768], P(('dp', 'ns')), may hold values from -6 to 6
- counts: int32 [32, 16], P(('dp', 'ns')), may hold values from 0 to 576, as said below
- owners: int32 [32, 16], P(('dp', 'ns')), may hold values from 0 to 7, as said below
- pooled_cot: bfloat16 [512, 768], P(('dp', 'ns')), may hold values from -96 to 96
- patch_cot: bfloat16 [32768, 768], P(('dp', 'ns')), may hold values from -6 to 6
- master_qkv: float32 [2304, 768], P('ns'), may hold values from -0.21875 to 0.21875
- master_out: float32 [768, 768], P('ns'), may hold values from -0.4375 to 0.4375
- master_up: float32 [3072, 768], P('ns'), may hold values from -0.21875 to 0.21875
- master_down: float32 [3072, 768], P('ns'), may hold values from -0.109375 to 0.109375
- mom_qkv: float32 [2304, 768], P('ns')
- mom_out: float32 [768, 768], P('ns')
- mom_up: float32 [3072, 768], P('ns')
- mom_down: float32 [3072, 768], P('ns')
- vectors: float32 [10176], replicated
- vec_first: float32 [10176], replicated
- vec_second: float32 [10176], replicated, may hold values from 6553 to 27852
Outputs:
- out_patches: bfloat16 [32768, 768], P(('dp', 'ns'))
- pooled_rows: bfloat16 [512, 768], P(('dp', 'ns'))
- patch_grad: float32 [32768, 768], P(('dp', 'ns'))
- grad_qkv: float32 [2304, 768], P('ns')
- grad_out: float32 [768, 768], P('ns')
- grad_up: float32 [3072, 768], P('ns')
- grad_down: float32 [3072, 768], P('ns')
- moment_qkv: float32 [2304, 768], P('ns')
- moment_out: float32 [768, 768], P('ns')
- moment_up: float32 [3072, 768], P('ns')
- moment_down: float32 [3072, 768], P('ns')
- new_qkv: float32 [2304, 768], P('ns')
- new_out: float32 [768, 768], P('ns')
- new_up: float32 [3072, 768], P('ns')
- new_down: float32 [3072, 768], P('ns')
- copy_qkv: bfloat16 [2304, 768], P('ns')
- copy_out: bfloat16 [768, 768], P('ns')
- copy_up: bfloat16 [3072, 768], P('ns')
- copy_down: bfloat16 [3072, 768], P('ns')
- vector_grad: float32 [10176], replicated
- vector_first: float32 [10176], replicated
- vector_second: float32 [10176], replicated
- vector_new: float32 [10176], replicated
The draws below stay inside these ranges and needn't reach their ends.
Inputs may be any that keep to these rules, and one draw needn't show every extreme that they name: `counts`: row 4 * i + j lists the images of the device at index i along dp and j along ns in the order of its slots: at most one of 576 patches, and only first in its row, the others of 64, then zeros. The first 2 entries of every row are nonzero, a row sums to at most 1024, and some row sums to exactly 1024. `owners`: in a row no value stands more than 2 times. The first 2 entries of a row are equal, and this value is the same in all rows of one index along ns.
All inputs are finite; a program needn't handle non-finite values.
Results may differ from the reference program's by a relative error of at most 0.04.
Values may be sent and summed in bfloat16 or wider, within the bound.
No kernel may reach another device: no remote copies, remote signals or barrier semaphores. Data moves between devices by JAX's collectives and lax.ppermute only.
A program may use at most 320 MiB of HBM per device.

```python
import math
import jax
import jax.numpy as jnp
from jax import lax

D = 768
HEADS = 12
HD = 64
FF = 3072
SLOTS = 1024
SMALL_P = 64
BIG_P = 576
ITERS = 4
STEP = 10
IMG_DEV = 16
SENDCAP = 2
TOKENS = 32768
NV = 10176
N_DP = 8
N_NS = 4


def draw_counts(key, part):
    key = jax.random.fold_in(key, 11)
    big_key, jitter_key, full_key = jax.random.split(key, 3)
    row_total = N_DP * N_NS
    dp_index = jnp.arange(row_total, dtype=jnp.int32) // N_NS
    base_count = IMG_DEV * (N_DP - 1 + 2 * dp_index) // (3 * (N_DP - 1))
    jitter = jax.random.randint(jitter_key, (row_total,), -1, 2)
    has_big = jax.random.randint(big_key, (row_total,), 0, N_DP) < dp_index
    full_row = jnp.arange(row_total, dtype=jnp.int32) == jax.random.randint(full_key, (), 0, row_total)
    most_small = (SLOTS - BIG_P) // SMALL_P
    with_big = jnp.clip(base_count - BIG_P // SMALL_P + jitter, SENDCAP - 1, most_small)
    without_big = jnp.clip(base_count + jitter, SENDCAP, IMG_DEV)
    has_big = has_big & jnp.logical_not(full_row)
    small_count = jnp.where(has_big, with_big, jnp.where(full_row, IMG_DEV, without_big))[:, None]
    position = jnp.arange(IMG_DEV, dtype=jnp.int32)[None, :]
    big_rows = jnp.where(position == 0, BIG_P, jnp.where(position <= small_count, SMALL_P, 0))
    drawn_rows = jnp.where(position < small_count, SMALL_P, 0)
    return jnp.where(has_big[:, None], big_rows, drawn_rows).astype(jnp.int32)


def draw_owners(key, part):
    key = jax.random.fold_in(key, 23)
    row_total = N_DP * N_NS
    hot_key, rest_key = jax.random.split(key)
    hot_owner = jax.random.randint(hot_key, (N_NS,), 0, N_DP)
    ns_index = jnp.arange(row_total, dtype=jnp.int32) % N_NS
    row_keys = jax.random.split(rest_key, row_total)

    def one_row(row_key, chosen):
        order_key, shuffle_key = jax.random.split(row_key)
        ordering = jnp.concatenate([jnp.arange(SENDCAP, dtype=jnp.int32), SENDCAP + jax.random.permutation(order_key, IMG_DEV - SENDCAP).astype(jnp.int32)])
        groups = ordering // SENDCAP
        shuffle = jnp.concatenate([jnp.zeros((1,), jnp.int32), 1 + jax.random.permutation(shuffle_key, N_DP - 1).astype(jnp.int32)])
        return (chosen + shuffle[groups]) % N_DP
    return jax.vmap(one_row)(row_keys, hot_owner[ns_index]).astype(jnp.int32)


def momentum_scale(noise_draw, column_key):
    row_count = noise_draw.shape[0]
    position = jnp.arange(row_count, dtype=jnp.float32) / (row_count - 1)
    row_factor = 10.0 ** position
    column_factor = 10.0 ** jax.random.uniform(column_key, (D,), jnp.float32)
    return (noise_draw * row_factor[:, None] * column_factor[None, :] * (0.05 * math.sqrt(TOKENS))).astype(jnp.float32)


def draw_mom_qkv(key, part):
    key = jax.random.fold_in(key, 31)
    noise_key, column_key = jax.random.split(key)
    noise_draw = jax.random.normal(noise_key, (3 * D, D), jnp.float32)
    return momentum_scale(noise_draw, column_key)


def draw_mom_out(key, part):
    key = jax.random.fold_in(key, 37)
    noise_key, column_key = jax.random.split(key)
    noise_draw = jax.random.normal(noise_key, (D, D), jnp.float32)
    return momentum_scale(noise_draw, column_key)


def draw_mom_up(key, part):
    key = jax.random.fold_in(key, 41)
    noise_key, column_key = jax.random.split(key)
    noise_draw = jax.random.normal(noise_key, (FF, D), jnp.float32)
    return momentum_scale(noise_draw, column_key)


def draw_mom_down(key, part):
    key = jax.random.fold_in(key, 43)
    noise_key, column_key = jax.random.split(key)
    noise_draw = jax.random.normal(noise_key, (FF, D), jnp.float32)
    return momentum_scale(noise_draw, column_key)


def draw_vectors(key, part):
    key = jax.random.fold_in(key, 47)
    widths = [D, D, 3 * D, HD, HD, HD, D, D, D, FF, D]
    gain_marks = [1.0, 0.0, 0.0, 1.0, 0.0, 1.0, 0.0, 1.0, 0.0, 0.0, 0.0]
    gain_flag = jnp.concatenate([jnp.full((width,), mark, jnp.float32) for width, mark in zip(widths, gain_marks)])
    noise_draw = jax.random.normal(key, (NV,), jnp.float32)
    return (gain_flag * (1.0 + 0.1 * noise_draw) + (1.0 - gain_flag) * 0.2 * noise_draw).astype(jnp.float32)


def draw_vec_first(key, part):
    key = jax.random.fold_in(key, 53)
    return (0.2 * math.sqrt(TOKENS) * jax.random.normal(key, (NV,), jnp.float32)).astype(jnp.float32)


def steps_of(key, shape, shards, smallest, high):
    level = 1.0
    for dim, blocks in shards:
        heights = jax.random.uniform(jax.random.fold_in(jax.random.fold_in(key, 6), dim), (blocks,), jnp.float32, smallest / len(shards), high / len(shards))
        level = level * jnp.repeat(jnp.exp(heights), shape[dim] // blocks).reshape((-1,) + (1,) * (len(shape) - 1 - dim))
    return level


def normal_values(rng, dims, scale, reach, cuts=(), held_as=jnp.bfloat16):
    values = jax.random.normal(rng, dims, jnp.float32) * scale
    if len(cuts) > 0:
        values = steps_of(rng, dims, cuts, -0.22, 0.18) * values
    return jnp.clip(values, min=-reach, max=reach).astype(held_as)


def setup_inputs(seed: int = 0) -> dict:
    splits = jax.random.split(jax.random.key(seed), 17)
    return {
        "patches": normal_values(splits[0], (TOKENS, D), 1.0, 6.0, ((0, 32),)),
        "counts": draw_counts(jax.random.fold_in(splits[16], 71), 0),
        "owners": draw_owners(jax.random.fold_in(splits[16], 71), 0),
        "pooled_cot": normal_values(splits[3], (N_DP * N_NS * N_DP * SENDCAP, D), (SMALL_P // 4), 96.0, ((0, 32),)),
        "patch_cot": normal_values(splits[4], (TOKENS, D), 1.0, 6.0, ((0, 32),)),
        "master_qkv": normal_values(splits[5], (3 * D, D), D ** -0.5, 0.21875, ((0, 4),), jnp.float32),
        "master_out": normal_values(splits[6], (D, D), (D // 4) ** -0.5, 0.4375, ((0, 4),), jnp.float32),
        "master_up": normal_values(splits[7], (FF, D), D ** -0.5, 0.21875, ((0, 4),), jnp.float32),
        "master_down": normal_values(splits[8], (FF, D), FF ** -0.5, 0.109375, ((0, 4),), jnp.float32),
        "mom_qkv": draw_mom_qkv(jax.random.fold_in(splits[16], 71), 0),
        "mom_out": draw_mom_out(jax.random.fold_in(splits[16], 71), 0),
        "mom_up": draw_mom_up(jax.random.fold_in(splits[16], 71), 0),
        "mom_down": draw_mom_down(jax.random.fold_in(splits[16], 71), 0),
        "vectors": draw_vectors(jax.random.fold_in(splits[16], 71), 0),
        "vec_first": draw_vec_first(jax.random.fold_in(splits[16], 71), 0),
        "vec_second": jnp.clip(jnp.exp(jax.random.uniform(splits[15], (NV,), jnp.float32, math.log(6553.0), math.log(27852.0))), 6553.0, 27852.0),
    }


@jax.custom_vjp
def low(v):
    return lax.optimization_barrier(v.astype(jnp.bfloat16)).astype(jnp.float32)

@jax.custom_vjp
def low_back(v):
    return v

def low_keep(v):
    return (low(v), None)

def low_pass(kept, grad):
    return (grad,)

def back_keep(v):
    return (v, None)

def back_low(kept, grad):
    return (low(grad),)
low.defvjp(low_keep, low_pass)
low_back.defvjp(back_keep, back_low)
HIGHEST = lax.Precision.HIGHEST
NS_A = 3.4445
NS_B = -4.775
NS_C = 2.0315
MUON_RATE = 0.8
MUON_DECAY = 0.5
MUON_SHRINK = 0.01
ADAM_RATE = 0.5
BETA_ONE = 0.9
BETA_TWO = 0.95
MASKED = -1e+30

def layer_norm(values, gain_vec, bias_vec):
    row_mean = lax.optimization_barrier(jnp.mean(values, axis=-1, keepdims=True))
    centred = values - row_mean
    variance = lax.optimization_barrier(jnp.mean(centred * centred, axis=-1, keepdims=True))
    return centred * lax.rsqrt(variance + 1e-06) * gain_vec + bias_vec

def gelu_exact(values):
    return jax.nn.gelu(values, approximate=False)

def split_vectors(vectors):
    widths = [D, D, 3 * D, HD, HD, HD, D, D, D, FF, D]
    pieces = []
    start = 0
    for width in widths:
        pieces.append(vectors[start:start + width])
        start = start + width
    return pieces

def segment_of(counts_row, slot_count):
    image_ends = jnp.cumsum(counts_row).astype(jnp.int32)
    position = jnp.arange(slot_count, dtype=jnp.int32)
    return lax.optimization_barrier(jnp.sum((image_ends[None, :] <= position[:, None]).astype(jnp.int32), axis=1))

def owner_slots(owners_row, capacity):
    image_total = owners_row.shape[0]
    ordering = jnp.arange(image_total, dtype=jnp.int32)
    earlier = (owners_row[None, :] == owners_row[:, None]) & (ordering[None, :] < ordering[:, None])
    same_before = lax.optimization_barrier(jnp.sum(earlier.astype(jnp.int32), axis=1))
    return owners_row * capacity + same_before

def device_forward(inputs, w_qkv, w_out, w_up, w_down, vectors, counts_row, owners_row):
    gain_one, bias_one, bias_qkv, gain_query, bias_query, gain_key, bias_out, gain_two, bias_two, bias_up, bias_down = split_vectors(vectors)
    slot_count = inputs.shape[0]
    segment = segment_of(counts_row, slot_count)
    first_low = low(layer_norm(inputs, gain_one, bias_one))
    qkv = low_back(jnp.dot(first_low, w_qkv.T, precision=HIGHEST) + bias_qkv)
    queries = qkv[:, :D].reshape(slot_count, HEADS, HD)
    key_rows = qkv[:, D:2 * D].reshape(slot_count, HEADS, HD)
    value_rows = qkv[:, 2 * D:].reshape(slot_count, HEADS, HD)
    query_low = low(layer_norm(queries, gain_query, bias_query))
    key_low = low(layer_norm(key_rows, gain_key, 0.0))
    value_low = low(value_rows)
    block_rows = min(512, slot_count)
    block_count = slot_count // block_rows
    query_blocks = query_low.reshape(block_count, block_rows, HEADS, HD)
    segment_blocks = segment.reshape(block_count, block_rows)

    def attend(operands):
        query_block, segment_block = operands
        scores = low_back(jnp.einsum('qhe,khe->hqk', query_block, key_low, precision=HIGHEST) * 0.125)
        allowed = segment_block[:, None] == segment[None, :]
        scores = jnp.where(allowed[None], scores, MASKED)
        attn_prob = low(jax.nn.softmax(scores, axis=-1))
        return jnp.einsum('hqk,khe->qhe', attn_prob, value_low, precision=HIGHEST)
    attended = lax.map(jax.checkpoint(attend), (query_blocks, segment_blocks)).reshape(slot_count, D)
    attn_low = low(low_back(attended))
    branch = low_back(jnp.dot(attn_low, w_out.T, precision=HIGHEST) + bias_out)
    middle = inputs + branch
    second_low = low(layer_norm(middle, gain_two, bias_two))
    pre_act = low_back(jnp.dot(second_low, w_up.T, precision=HIGHEST) + bias_up)
    hidden_low = low(gelu_exact(pre_act))
    mixed_rows = low_back(jnp.dot(hidden_low, w_down, precision=HIGHEST) + bias_down)
    result_rows = middle + mixed_rows
    image_ids = jnp.arange(IMG_DEV, dtype=jnp.int32)
    picker = (segment[None, :] == image_ids[:, None]).astype(jnp.float32)
    image_sizes = jnp.maximum(counts_row, 1).astype(jnp.float32)[:, None]
    pooled = low(jnp.dot(picker, result_rows, precision=HIGHEST) / image_sizes)
    targets = owner_slots(owners_row, SENDCAP)
    routing = (jnp.arange(N_DP * SENDCAP, dtype=jnp.int32)[:, None] == targets[None, :]).astype(jnp.float32)
    outgoing = jnp.dot(routing, pooled, precision=HIGHEST).reshape(N_DP, SENDCAP, D)
    return (result_rows, outgoing)

def muon(gradient, momentum, master):
    moment = MUON_DECAY * momentum + gradient
    norm_value = jnp.sqrt(jnp.sum(moment * moment))
    orthogonal = low(moment / (norm_value + 1e-07))
    row_count = gradient.shape[0]
    for iteration in range(ITERS):
        row_blocks = orthogonal.reshape(N_NS, row_count // N_NS, D)
        partial_value = low(jnp.einsum('nrd,nre->nde', row_blocks, row_blocks, precision=HIGHEST))
        gram_sum = lax.optimization_barrier(jnp.sum(partial_value, axis=0))
        gram_low = low(gram_sum)
        squared = jnp.dot(gram_low, gram_low, precision=HIGHEST)
        mixer_low = low(NS_B * gram_sum + NS_C * squared)
        orthogonal = low(NS_A * orthogonal + jnp.dot(orthogonal, mixer_low, precision=HIGHEST))
    step_scale = MUON_RATE * math.sqrt(max(1.0, row_count / D))
    new_master = master * (1.0 - MUON_RATE * MUON_SHRINK) - step_scale * orthogonal
    return (moment, new_master, new_master.astype(jnp.bfloat16))

def reference(patches, counts, owners, pooled_cot, patch_cot, master_qkv, master_out, master_up, master_down, mom_qkv, mom_out, mom_up, mom_down, vectors, vec_first, vec_second):
    device_total = N_DP * N_NS
    inputs = patches.astype(jnp.float32).reshape(device_total, SLOTS, D)
    w_qkv = low(master_qkv)
    w_out = low(master_out)
    w_up = low(master_up)
    w_down = low(master_down)

    def forward(inputs, w_qkv, w_out, w_up, w_down, vectors):

        def one_device(operands):
            rows_in, counts_row, owners_row = operands
            return device_forward(rows_in, w_qkv, w_out, w_up, w_down, vectors, counts_row, owners_row)
        outputs, outgoing = lax.map(jax.checkpoint(one_device), (inputs, counts, owners))
        arranged = outgoing.reshape(N_DP, N_NS, N_DP, SENDCAP, D).transpose(2, 1, 0, 3, 4)
        return (outputs, arranged.reshape(device_total * N_DP * SENDCAP, D))
    segments = jax.vmap(lambda counts_row: segment_of(counts_row, SLOTS))(counts)
    live_mask = (segments < IMG_DEV).astype(jnp.float32)[:, :, None]
    (outputs, arrived), pullback = jax.vjp(forward, inputs, w_qkv, w_out, w_up, w_down, vectors)
    cot_rows = live_mask * patch_cot.astype(jnp.float32).reshape(device_total, SLOTS, D)
    patch_grad, grad_qkv, grad_out, grad_up, grad_down, vector_grad = pullback((cot_rows, pooled_cot.astype(jnp.float32)))
    moment_qkv, new_qkv, copy_qkv = muon(grad_qkv, mom_qkv, master_qkv)
    moment_out, new_out, copy_out = muon(grad_out, mom_out, master_out)
    moment_up, new_up, copy_up = muon(grad_up, mom_up, master_up)
    moment_down, new_down, copy_down = muon(grad_down, mom_down, master_down)
    vector_first = BETA_ONE * vec_first + (1.0 - BETA_ONE) * vector_grad
    vector_second = BETA_TWO * vec_second + (1.0 - BETA_TWO) * vector_grad * vector_grad
    first_hat = vector_first / (1.0 - BETA_ONE ** STEP)
    second_hat = vector_second / (1.0 - BETA_TWO ** STEP)
    vector_new = vectors - ADAM_RATE * first_hat / (jnp.sqrt(second_hat) + 1e-08)
    return (outputs.reshape(device_total * SLOTS, D).astype(jnp.bfloat16), arrived.astype(jnp.bfloat16), patch_grad.reshape(device_total * SLOTS, D), grad_qkv, grad_out, grad_up, grad_down, moment_qkv, moment_out, moment_up, moment_down, new_qkv, new_out, new_up, new_down, copy_qkv, copy_out, copy_up, copy_down, vector_grad, vector_first, vector_second, vector_new)
```

```python
import functools
import math

import jax
import jax.numpy as jnp
from jax import lax
from jax.experimental import pallas as pl
from jax.experimental.pallas import tpu as pltpu
from jax.sharding import PartitionSpec as P

D = 768
HD = 64
FF = 3072
ITERS = 4
STEP = 10


NS_A = 3.4445
NS_B = -4.775
NS_C = 2.0315
MUON_RATE = 0.8
MUON_DECAY = 0.5
MUON_SHRINK = 0.01
ADAM_RATE = 0.5
BETA_ONE = 0.9
BETA_TWO = 0.95
MASKED = -1e30


def split_vectors(vectors):
    widths = [D, D, 3 * D, HD, HD, HD, D, D, D, FF, D]
    pieces = []
    start = 0
    for width in widths:
        pieces.append(vectors[start : start + width])
        start = start + width
    return pieces


def owner_slots(owners_row, capacity):
    image_total = owners_row.shape[0]
    ordering = jnp.arange(image_total, dtype=jnp.int32)
    earlier = (owners_row[None, :] == owners_row[:, None]) & (ordering[None, :] < ordering[:, None])
    same_before = jnp.sum(earlier.astype(jnp.int32), axis=1)
    return owners_row * capacity + same_before


def xor_pairs(count, bit):
    return [(index, index ^ (1 << bit)) for index in range(count)]


def swap(value, axis, bit):
    return lax.ppermute(value, axis, xor_pairs(lax.axis_size(axis), bit))


def bit_of(axis, bit):
    return (lax.axis_index(axis) >> bit) & 1


def bits_in(axis):
    return (lax.axis_size(axis) - 1).bit_length()


def add_low(first, second):
    return (first.astype(jnp.float32) + second.astype(jnp.float32)).astype(jnp.bfloat16)


def sum_rows(blocks):
    value = blocks
    for bit in range(bits_in("ns")):
        mine = bit_of("ns", bit)
        pairs = value.reshape(value.shape[0] // 2, 2, *value.shape[1:])
        keep = lax.dynamic_index_in_dim(pairs, mine, 1, keepdims=False)
        send = lax.dynamic_index_in_dim(pairs, 1 - mine, 1, keepdims=False)
        value = add_low(keep, swap(send, "ns", bit))
    value = value[0]
    halved = min(2, bits_in("dp"))
    for bit in range(halved):
        mine = bit_of("dp", bit)
        pairs = value.reshape(2, value.shape[0] // 2, D)
        keep = lax.dynamic_index_in_dim(pairs, mine, 0, keepdims=False)
        send = lax.dynamic_index_in_dim(pairs, 1 - mine, 0, keepdims=False)
        value = add_low(keep, swap(send, "dp", bit))
    for bit in range(halved, bits_in("dp")):
        value = add_low(value, swap(value, "dp", bit))
    for bit in reversed(range(halved)):
        mine = bit_of("dp", bit)
        other = swap(value, "dp", bit)
        low_half = jnp.where(mine == 0, value, other)
        high_half = jnp.where(mine == 0, other, value)
        value = jnp.concatenate([low_half, high_half], axis=0)
    return value


def sum_everywhere(value):
    for axis in ("ns", "dp"):
        for bit in range(bits_in(axis)):
            value = value + swap(value, axis, bit)
    return value


def sum_gram(gram):
    gram = gram + swap(gram, "ns", 0)
    count = bits_in("ns")
    if count == 1:
        return gram
    mine = bit_of("ns", 0)
    half = lax.dynamic_index_in_dim(gram.reshape(2, D // 2, D), mine, 0, keepdims=False)
    for bit in range(1, count):
        half = half + swap(half, "ns", bit)
    other = swap(half, "ns", 0)
    low_half = jnp.where(mine == 0, half, other)
    high_half = jnp.where(mine == 0, other, half)
    return jnp.concatenate([low_half, high_half], axis=0)


def split_low(value):
    high = lax.reduce_precision(value, 8, 7)
    return high.astype(jnp.bfloat16), (value - high).astype(jnp.bfloat16)


def dot32(first, second):
    return jnp.dot(first, second, preferred_element_type=jnp.float32)


def orthogonalise(moment_low, gram_raw):
    scale = 1.0 / (jnp.sqrt(jnp.trace(gram_raw)) + 1e-07)
    gram = gram_raw * (scale * scale)
    rows = moment_low
    for iteration in range(ITERS):
        gram_high, gram_rest = split_low(gram)
        mixer = (NS_B * gram + NS_C * dot32(gram_high, gram_high)).astype(jnp.bfloat16)
        renewed = NS_A * rows.astype(jnp.float32) + dot32(rows, mixer)
        if iteration == 0:
            renewed = renewed * scale
        if iteration == ITERS - 1:
            return renewed
        rows = renewed.astype(jnp.bfloat16)
        middle = NS_A * gram + dot32(gram_high, mixer) + dot32(gram_rest, mixer)
        middle_high, middle_rest = split_low(middle)
        gram = NS_A * middle + dot32(mixer, middle_high) + dot32(mixer, middle_rest)


LOW = jnp.bfloat16
F32 = jnp.float32
HEADS = D // HD
BIG = 576
SMALL = 64
TILE = 256
VMEM_LIMIT = 60 * 1024 * 1024


def mm(first, second, first_dim=1, second_dim=0):
    return lax.dot_general(
        first,
        second,
        (((first_dim,), (second_dim,)), ((), ())),
        preferred_element_type=F32,
    )


def split_value(value):
    high = value.astype(LOW)
    return high, (value - high.astype(F32)).astype(LOW)


def normalise(values):
    row_mean = jnp.mean(values, axis=-1, keepdims=True)
    centred = values - row_mean
    scale = lax.rsqrt(jnp.mean(centred * centred, axis=-1, keepdims=True) + 1e-06)
    return centred * scale, scale


def norm_back(unit, scale, unit_grad):
    return scale * (
        unit_grad
        - jnp.mean(unit_grad, axis=-1, keepdims=True)
        - unit * jnp.mean(unit_grad * unit, axis=-1, keepdims=True)
    )


def column_sum(values):
    return jnp.sum(values, axis=0, keepdims=True)


def params(**extra):
    return pltpu.CompilerParams(vmem_limit_bytes=VMEM_LIMIT, **extra)


def whole(shape):
    return pl.BlockSpec(shape, lambda *_: (0,) * len(shape))


def rows_of(width, tile=TILE):
    return pl.BlockSpec((tile, width), lambda i, *_: (i, 0))


def lanes_of(height, tile=TILE):
    return pl.BlockSpec((height, tile), lambda i, *_: (0, i))


def shape_of(shape, dtype):
    return jax.ShapeDtypeStruct(shape, dtype)


def project_kernel(x_ref, w_ref, g_ref, b_ref, bias_ref, gq_ref, bq_ref, gk_ref,
                   h_ref, qkv_ref, unit_ref, scale_ref):
    unit, _ = normalise(x_ref[...].astype(F32))
    h_low = (unit * g_ref[...] + b_ref[...]).astype(LOW)
    h_ref[...] = h_low
    for part in range(3):
        rows = pl.ds(part * D, D)
        value = mm(w_ref[rows, :], h_low, 1, 1) + bias_ref[rows, :]
        if part == 2:
            qkv_ref[2] = value.astype(LOW)
            continue
        heads = value.reshape(HEADS, HD, value.shape[1])
        centred = heads - jnp.mean(heads, axis=1, keepdims=True)
        scale = lax.rsqrt(jnp.mean(centred * centred, axis=1, keepdims=True) + 1e-06)
        unit_heads = centred * scale
        scale_ref[part] = scale
        unit_ref[part] = unit_heads.reshape(D, -1).astype(LOW)
        if part == 0:
            result = unit_heads * gq_ref[...][None] + bq_ref[...][None]
            result = result.astype(LOW) * LOW(0.125)
        else:
            result = (unit_heads * gk_ref[...][None]).astype(LOW)
        qkv_ref[part] = result.reshape(D, -1)


def project(patches, w_qkv, gain_one, bias_one, bias_qkv, gain_query, bias_query, gain_key):
    slots = patches.shape[0]
    return pl.pallas_call(
        project_kernel,
        grid=(slots // TILE,),
        in_specs=[rows_of(D), whole((3 * D, D)), whole((1, D)), whole((1, D)),
                  whole((3 * D, 1)), whole((HD, 1)), whole((HD, 1)), whole((HD, 1))],
        out_specs=[rows_of(D),
                   pl.BlockSpec((3, D, TILE), lambda i: (0, 0, i)),
                   pl.BlockSpec((2, D, TILE), lambda i: (0, 0, i)),
                   pl.BlockSpec((2, HEADS, 1, TILE), lambda i: (0, 0, 0, i))],
        out_shape=[shape_of((slots, D), LOW), shape_of((3, D, slots), LOW),
                   shape_of((2, D, slots), LOW), shape_of((2, HEADS, 1, slots), F32)],
        compiler_params=params(),
        name="project",
    )(patches, w_qkv, gain_one[None], bias_one[None], bias_qkv[:, None],
      gain_query[:, None], bias_query[:, None], gain_key[:, None])


def used_slots(counts_ref):
    total = counts_ref[0]
    for k in range(1, counts_ref.shape[0]):
        total = total + counts_ref[k]
    return total


def pair_mask(tile_start, used, has_big):
    same = (has_big & (tile_start + SMALL < BIG)) | (tile_start >= used)
    row_half = lax.broadcasted_iota(jnp.int32, (128, 128), 0) // SMALL
    column_half = lax.broadcasted_iota(jnp.int32, (128, 128), 1) // SMALL
    return (row_half == column_half) | same


def soft_columns(scores):
    peak = jnp.max(scores, axis=0, keepdims=True)
    exponent = jnp.exp(scores - peak)
    total = jnp.sum(exponent, axis=0, keepdims=True)
    return exponent.astype(LOW), total, peak + jnp.log(total)


def attend_kernel(group, counts_ref, qkv_ref, out_ref, log_ref):
    used = used_slots(counts_ref)
    has_big = counts_ref[0] == BIG
    slots = out_ref.shape[1]

    def head_rows(index):
        return pl.ds(index * HD, HD)

    for tile in range(slots // 128):
        span = pl.ds(tile * 128, 128)
        mask = pair_mask(tile * 128, used, has_big)
        for index in range(group):
            q = qkv_ref[0, head_rows(index), span]
            k = qkv_ref[1, head_rows(index), span]
            v = qkv_ref[2, head_rows(index), span]
            scores = jnp.where(mask, mm(k, q, 0, 0), MASKED)
            weights, total, log_total = soft_columns(scores)
            out_ref[head_rows(index), span] = (mm(v, weights) / total).astype(LOW)
            log_ref[index, :, span] = log_total

    @pl.when(has_big)
    def _():
        for index in range(group):
            k = qkv_ref[1, head_rows(index), 0:640]
            v = qkv_ref[2, head_rows(index), 0:640]
            for start, width in ((0, 256), (256, 256), (512, 128)):
                span = pl.ds(start, width)
                q = qkv_ref[0, head_rows(index), span]
                scores = mm(k, q, 0, 0)[:BIG]
                weights, total, log_total = soft_columns(scores)
                weights = jnp.concatenate([weights, jnp.zeros((640 - BIG, width), LOW)], axis=0)
                result = mm(v, weights) / total
                if width == 128:
                    lane = lax.broadcasted_iota(jnp.int32, (1, width), 1)
                    inside = lane < BIG - start
                    result = jnp.where(inside, result, out_ref[head_rows(index), span].astype(F32))
                    log_total = jnp.where(inside, log_total, log_ref[index, :, span])
                out_ref[head_rows(index), span] = result.astype(LOW)
                log_ref[index, :, span] = log_total

    for first in range(0, slots - 128, 256):

        @pl.when((used >= first) & (used < first + 256) & (used < slots - 128))
        def _():
            for index in range(group):
                k = qkv_ref[1, head_rows(index), first:slots]
                v = qkv_ref[2, head_rows(index), first:slots]

                def columns(chunk, carry):
                    span = pl.ds(pl.multiple_of(chunk * 256, 256), 256)
                    q = qkv_ref[0, head_rows(index), span]
                    scores = mm(k, q, 0, 0)
                    key_slot = first + lax.broadcasted_iota(jnp.int32, (256, 256), 0)
                    top = jnp.where(key_slot >= used, scores[:256], MASKED)
                    if slots - first > 256:
                        top = jnp.concatenate([top, scores[256:]], axis=0)
                    weights, total, log_total = soft_columns(top)
                    slot = chunk * 256 + lax.broadcasted_iota(jnp.int32, (1, 256), 1)
                    inside = slot >= used
                    result = mm(v, weights) / total
                    old = out_ref[head_rows(index), span].astype(F32)
                    out_ref[head_rows(index), span] = jnp.where(inside, result, old).astype(LOW)
                    log_ref[index, :, span] = jnp.where(inside, log_total, log_ref[index, :, span])
                    return carry

                lax.fori_loop(first // 256, slots // 256, columns, 0)


def attend(counts, qkv, group=2):
    slots = qkv.shape[2]
    return pl.pallas_call(
        functools.partial(attend_kernel, group),
        grid_spec=pltpu.PrefetchScalarGridSpec(
            num_scalar_prefetch=1,
            grid=(HEADS // group,),
            in_specs=[pl.BlockSpec((3, group * HD, slots), lambda h, c: (0, h, 0))],
            out_specs=[pl.BlockSpec((group * HD, slots), lambda h, c: (h, 0)),
                       pl.BlockSpec((group, 1, slots), lambda h, c: (h, 0, 0))],
        ),
        out_shape=[shape_of((D, slots), LOW), shape_of((HEADS, 1, slots), F32)],
        compiler_params=params(),
        name="attend",
    )(counts, qkv)


def attend_back_kernel(group, counts_ref, qkv_ref, attn_ref, log_ref, grad_ref, unit_ref,
                       scale_ref, gq_ref, gk_ref,
                       dqkv_ref, bias_ref, gain_q_ref, bias_q_ref, gain_k_ref, dq_s, dk_s, dv_s):
    used = used_slots(counts_ref)
    has_big = counts_ref[0] == BIG
    slots = attn_ref.shape[1]

    @pl.when(pl.program_id(0) == 0)
    def _():
        gain_q_ref[...] = jnp.zeros_like(gain_q_ref)
        bias_q_ref[...] = jnp.zeros_like(bias_q_ref)
        gain_k_ref[...] = jnp.zeros_like(gain_k_ref)

    def head_rows(index):
        return pl.ds(index * HD, HD)

    def delta_of(index, span):
        return column_sum(
            grad_ref[head_rows(index), span].astype(F32)
            * attn_ref[head_rows(index), span].astype(F32)
        )

    for tile in range(slots // 128):
        span = pl.ds(tile * 128, 128)
        mask = pair_mask(tile * 128, used, has_big)
        for index in range(group):
            rows = head_rows(index)
            q, k, v = (qkv_ref[part, rows, span] for part in range(3))
            grad = grad_ref[rows, span]
            scores = mm(k, q, 0, 0)
            probs = jnp.exp(jnp.where(mask, scores - log_ref[index, :, span], MASKED))
            score_low = (probs * (mm(v, grad, 0, 0) - delta_of(index, span))).astype(LOW)
            dv_s[rows, span] = mm(grad, probs.astype(LOW), 1, 1)
            dk_s[rows, span] = mm(q, score_low, 1, 1)
            dq_s[rows, span] = mm(k, score_low)

    @pl.when(has_big)
    def _():
        for index in range(group):
            rows = head_rows(index)
            wide = pl.ds(0, 640)
            q, k, v = (qkv_ref[part, rows, wide] for part in range(3))
            dk = jnp.zeros((HD, 640), F32)
            dv = jnp.zeros((HD, 640), F32)
            for start, width in ((0, 256), (256, 256), (512, 128)):
                span = pl.ds(start, width)
                q_part = qkv_ref[0, rows, span]
                grad = grad_ref[rows, span]
                scores = mm(k, q_part, 0, 0)[:BIG]
                probs = jnp.exp(scores - log_ref[index, :, span])
                if width == 128:
                    lane = lax.broadcasted_iota(jnp.int32, (1, width), 1)
                    probs = jnp.where(lane < BIG - start, probs, 0.0)
                score_low = (
                    probs * (mm(v, grad, 0, 0)[:BIG] - delta_of(index, span))
                ).astype(LOW)
                blank = jnp.zeros((640 - BIG, width), LOW)
                score_low = jnp.concatenate([score_low, blank], axis=0)
                probs_low = jnp.concatenate([probs.astype(LOW), blank], axis=0)
                dv = dv + mm(grad, probs_low, 1, 1)
                dk = dk + mm(q_part, score_low, 1, 1)
                dq = mm(k, score_low)
                if width == 128:
                    dq = jnp.where(lane < BIG - start, dq, dq_s[rows, span])
                dq_s[rows, span] = dq
            inside = lax.broadcasted_iota(jnp.int32, (1, 640), 1) < BIG
            dk_s[rows, wide] = jnp.where(inside, dk, dk_s[rows, wide])
            dv_s[rows, wide] = jnp.where(inside, dv, dv_s[rows, wide])

    for index in range(group):
        rows = head_rows(index)
        for part, store, gain_ref in ((0, dq_s, gq_ref), (1, dk_s, gk_ref)):
            unit = unit_ref[part, rows, :].astype(F32)
            grad = store[rows, :]
            if part == 0:
                grad = grad * 0.125
                bias_q_ref[...] += jnp.sum(grad, axis=1, keepdims=True)
                gain_q_ref[...] += jnp.sum(grad * unit, axis=1, keepdims=True)
            else:
                gain_k_ref[...] += jnp.sum(grad * unit, axis=1, keepdims=True)
            unit_grad = grad * gain_ref[...]
            result = scale_ref[part, index] * (
                unit_grad
                - jnp.mean(unit_grad, axis=0, keepdims=True)
                - unit * jnp.mean(unit_grad * unit, axis=0, keepdims=True)
            )
            result = result.astype(LOW)
            dqkv_ref[part, rows, :] = result
            bias_ref[part, rows, :] = jnp.sum(result.astype(F32), axis=1, keepdims=True)
        result = dv_s[rows, :].astype(LOW)
        dqkv_ref[2, rows, :] = result
        bias_ref[2, rows, :] = jnp.sum(result.astype(F32), axis=1, keepdims=True)


def attend_back(counts, qkv, attn, log_total, attn_grad, unit, scale, gain_query, gain_key, group=2):
    slots = qkv.shape[2]
    head_block = pl.BlockSpec((group * HD, slots), lambda h, c: (h, 0))
    column = pl.BlockSpec((HD, 1), lambda h, c: (0, 0))
    return pl.pallas_call(
        functools.partial(attend_back_kernel, group),
        grid_spec=pltpu.PrefetchScalarGridSpec(
            num_scalar_prefetch=1,
            grid=(HEADS // group,),
            in_specs=[pl.BlockSpec((3, group * HD, slots), lambda h, c: (0, h, 0)),
                      head_block,
                      pl.BlockSpec((group, 1, slots), lambda h, c: (h, 0, 0)),
                      head_block,
                      pl.BlockSpec((2, group * HD, slots), lambda h, c: (0, h, 0)),
                      pl.BlockSpec((2, group, 1, slots), lambda h, c: (0, h, 0, 0)),
                      column, column],
            out_specs=[pl.BlockSpec((3, group * HD, slots), lambda h, c: (0, h, 0)),
                       pl.BlockSpec((3, group * HD, 1), lambda h, c: (0, h, 0)),
                       column, column, column],
            scratch_shapes=[pltpu.VMEM((group * HD, slots), F32)] * 3,
        ),
        out_shape=[shape_of((3, D, slots), LOW), shape_of((3, D, 1), F32),
                   shape_of((HD, 1), F32), shape_of((HD, 1), F32), shape_of((HD, 1), F32)],
        compiler_params=params(),
        name="attend_back",
    )(counts, qkv, attn, log_total, attn_grad, unit, scale, gain_query[:, None], gain_key[:, None])


def segment_picker(counts_ref, first, width):
    images = counts_ref.shape[0]
    slot = first + lax.broadcasted_iota(jnp.int32, (images, width), 1)
    image = lax.broadcasted_iota(jnp.int32, (images, width), 0)
    start = jnp.int32(0)
    picked = jnp.zeros((images, width), jnp.bool_)
    for k in range(images):
        end = start + counts_ref[k]
        picked = picked | ((image == k) & (slot >= start) & (slot < end))
        start = end
    return picked.astype(F32), start


def image_sizes(counts_ref):
    images = counts_ref.shape[0]
    image = lax.broadcasted_iota(jnp.int32, (images, 1), 0)
    sizes = jnp.zeros((images, 1), F32)
    for k in range(images):
        sizes = jnp.where(image == k, jnp.maximum(counts_ref[k], 1).astype(F32), sizes)
    return sizes


def middle_kernel(counts_ref, x_ref, attn_ref, w_ref, bias_ref, g_ref, b_ref, cot_ref, image_ref,
                  x2_ref, h_ref, dy_ref, mix_ref):
    x2 = x_ref[...].astype(F32) + mm(attn_ref[...], w_ref[...], 0, 1) + bias_ref[...]
    x2_ref[...] = x2
    unit, _ = normalise(x2)
    h_ref[...] = (unit * g_ref[...] + b_ref[...]).astype(LOW)
    tile = x_ref.shape[0]
    first = pl.program_id(0) * tile
    picker, used = segment_picker(counts_ref, first, tile)
    picker = picker.astype(LOW)
    image_grad = image_ref[...].astype(F32) / image_sizes(counts_ref)
    dy = jnp.zeros(x2.shape, F32)
    rest = image_grad
    for _ in range(3):
        high, rest = split_value32(rest)
        dy = dy + mm(picker, high, 0, 0)
    slot = first + lax.broadcasted_iota(jnp.int32, (tile, 1), 0)
    dy = dy + jnp.where(slot < used, cot_ref[...].astype(F32), 0.0)
    dy_ref[...] = dy
    mix_ref[...] = dy.astype(LOW)


def split_value32(value):
    high = value.astype(LOW)
    return high, value - high.astype(F32)


def middle(counts, patches, attn, w_out, bias_out, gain_two, bias_two, patch_cot, image_cot):
    slots = patches.shape[0]
    images = counts.shape[0]
    return pl.pallas_call(
        middle_kernel,
        grid_spec=pltpu.PrefetchScalarGridSpec(
            num_scalar_prefetch=1,
            grid=(slots // TILE,),
            in_specs=[rows_of(D), lanes_of(D), whole((D, D)), whole((1, D)), whole((1, D)),
                      whole((1, D)), rows_of(D), whole((images, D))],
            out_specs=[rows_of(D)] * 4,
        ),
        out_shape=[shape_of((slots, D), F32), shape_of((slots, D), LOW),
                   shape_of((slots, D), F32), shape_of((slots, D), LOW)],
        compiler_params=params(),
        name="middle",
    )(counts, patches, attn, w_out, bias_out[None], gain_two[None], bias_two[None], patch_cot, image_cot)


def feed_kernel(x2_ref, h_ref, mix_ref, up_ref, down_ref, bias_ref, bias_down_ref,
                y_ref, dh_ref, grad_up_ref, grad_down_ref, bias_grad_ref):
    first = pl.program_id(0) == 0

    @pl.when(first)
    def _():
        y_ref[...] = x2_ref[...] + bias_down_ref[...]
        dh_ref[...] = jnp.zeros_like(dh_ref)

    up, down = up_ref[...], down_ref[...]
    slots = h_ref.shape[0]
    grad_up = jnp.zeros(up.shape, F32)
    grad_down = jnp.zeros(up.shape, F32)
    bias_grad = jnp.zeros((1, up.shape[0]), F32)
    for start in range(0, slots, TILE):
        span = pl.ds(start, TILE)
        h, mix = h_ref[span, :], mix_ref[span, :]
        u = mm(h, up, 1, 1) + bias_ref[...]
        gate = 0.5 * (1.0 + lax.erf(u * (0.5**0.5)))
        slope = gate + u * (jnp.exp(-0.5 * u * u) * ((0.5 / math.pi) ** 0.5))
        hidden = (u * gate).astype(LOW)
        pre = (mm(mix, down, 1, 1) * slope).astype(LOW)
        y_ref[span, :] += mm(hidden, down)
        dh_ref[span, :] += mm(pre, up)
        grad_up = grad_up + mm(pre, h, 0, 0)
        grad_down = grad_down + mm(hidden, mix, 0, 0)
        bias_grad = bias_grad + column_sum(pre.astype(F32))
    grad_up_ref[...] = grad_up.astype(LOW)
    grad_down_ref[...] = grad_down.astype(LOW)
    bias_grad_ref[...] = bias_grad


def feed(x2, h2, mix, w_up, w_down, bias_up, bias_down, block=256):
    slots = x2.shape[0]
    units = w_up.shape[0]
    return pl.pallas_call(
        feed_kernel,
        grid=(units // block,),
        in_specs=[whole((slots, D)), whole((slots, D)), whole((slots, D)),
                  rows_of(D, block), rows_of(D, block),
                  pl.BlockSpec((1, block), lambda i: (0, i)), whole((1, D))],
        out_specs=[whole((slots, D)), whole((slots, D)), rows_of(D, block), rows_of(D, block),
                   pl.BlockSpec((1, block), lambda i: (0, i))],
        out_shape=[shape_of((slots, D), F32), shape_of((slots, D), F32),
                   shape_of((units, D), LOW), shape_of((units, D), LOW),
                   shape_of((1, units), F32)],
        compiler_params=params(),
        name="feed",
    )(x2, h2, mix, w_up, w_down, bias_up[None], bias_down[None])


def after_kernel(counts_ref, y_ref, x2_ref, dh_ref, dy_ref, attn_ref, w_ref, g_ref,
                 out_ref, pooled_ref, dx2_ref, dattn_ref, grad_out_ref,
                 gain_ref, bias_ref, out_bias_ref, down_bias_ref, pool_s, grad_s):
    step = pl.program_id(0)

    @pl.when(step == 0)
    def _():
        pool_s[...] = jnp.zeros_like(pool_s)
        grad_s[...] = jnp.zeros_like(grad_s)
        for ref in (gain_ref, bias_ref, out_bias_ref, down_bias_ref):
            ref[...] = jnp.zeros_like(ref)

    y = y_ref[...]
    tile = y.shape[0]
    out_ref[...] = y.astype(LOW)
    picker, _ = segment_picker(counts_ref, step * tile, tile)
    picker = picker.astype(LOW)
    rest = y
    pooled = pool_s[...]
    for _ in range(3):
        high, rest = split_value32(rest)
        pooled = pooled + mm(picker, high)
    pool_s[...] = pooled
    pooled_ref[...] = (pooled / image_sizes(counts_ref)).astype(LOW)
    unit, scale = normalise(x2_ref[...])
    dh = dh_ref[...]
    gain_ref[...] += column_sum(dh * unit)
    bias_ref[...] += column_sum(dh)
    dy = dy_ref[...]
    down_bias_ref[...] += column_sum(dy.astype(LOW).astype(F32))
    dx2 = dy + norm_back(unit, scale, dh * g_ref[...])
    dx2_ref[...] = dx2
    da = dx2.astype(LOW)
    out_bias_ref[...] += column_sum(da.astype(F32))
    dattn_ref[...] = mm(w_ref[...], da, 0, 1).astype(LOW)
    grad = grad_s[...] + mm(da, attn_ref[...], 0, 1)
    grad_s[...] = grad
    grad_out_ref[...] = grad.astype(LOW)


def after(counts, y, x2, dh2, dy, attn, w_out, gain_two):
    slots = y.shape[0]
    images = counts.shape[0]
    line = whole((1, D))
    return pl.pallas_call(
        after_kernel,
        grid_spec=pltpu.PrefetchScalarGridSpec(
            num_scalar_prefetch=1,
            grid=(slots // TILE,),
            in_specs=[rows_of(D), rows_of(D), rows_of(D), rows_of(D), lanes_of(D),
                      whole((D, D)), line],
            out_specs=[rows_of(D), whole((images, D)), rows_of(D), lanes_of(D), whole((D, D)),
                       line, line, line, line],
            scratch_shapes=[pltpu.VMEM((images, D), F32), pltpu.VMEM((D, D), F32)],
        ),
        out_shape=[shape_of((slots, D), LOW), shape_of((images, D), LOW),
                   shape_of((slots, D), F32), shape_of((D, slots), LOW), shape_of((D, D), LOW)]
        + [shape_of((1, D), F32)] * 4,
        compiler_params=params(),
        name="after",
    )(counts, y, x2, dh2, dy, attn, w_out, gain_two[None])


def first_back_kernel(x_ref, dqkv_ref, w_ref, g_ref, dx2_ref, out_ref, gain_ref, bias_ref):
    @pl.when(pl.program_id(0) == 0)
    def _():
        gain_ref[...] = jnp.zeros_like(gain_ref)
        bias_ref[...] = jnp.zeros_like(bias_ref)

    dh = mm(dqkv_ref[...], w_ref[...], 0, 0)
    unit, scale = normalise(x_ref[...].astype(F32))
    gain_ref[...] += column_sum(dh * unit)
    bias_ref[...] += column_sum(dh)
    out_ref[...] = dx2_ref[...] + norm_back(unit, scale, dh * g_ref[...])


def first_back(patches, dqkv, w_qkv, gain_one, dx2):
    slots = patches.shape[0]
    line = whole((1, D))
    return pl.pallas_call(
        first_back_kernel,
        grid=(slots // TILE,),
        in_specs=[rows_of(D), lanes_of(3 * D), whole((3 * D, D)), line, rows_of(D)],
        out_specs=[rows_of(D), line, line],
        out_shape=[shape_of((slots, D), F32), shape_of((1, D), F32), shape_of((1, D), F32)],
        compiler_params=params(),
        name="first_back",
    )(patches, dqkv, w_qkv, gain_one[None], dx2)


def per_device(
    patches,
    counts,
    owners,
    pooled_cot,
    patch_cot,
    master_qkv,
    master_out,
    master_up,
    master_down,
    mom_qkv,
    mom_out,
    mom_up,
    mom_down,
    vectors,
    vec_first,
    vec_second,
):
    dp_count = lax.axis_size("dp")
    ns_count = lax.axis_size("ns")
    slot_count = patches.shape[0]
    image_total = counts.shape[1]
    capacity = pooled_cot.shape[0] // dp_count
    w_qkv, w_out, w_up, w_down = (
        lax.all_gather(master_qkv.astype(jnp.bfloat16), "ns", axis=0, tiled=True),
        lax.all_gather(master_out.astype(jnp.bfloat16), "ns", axis=0, tiled=True),
        lax.all_gather(master_up.astype(jnp.bfloat16), "ns", axis=0, tiled=True),
        lax.all_gather(master_down.astype(jnp.bfloat16), "ns", axis=0, tiled=True),
    )
    (
        gain_one,
        bias_one,
        bias_qkv,
        gain_query,
        bias_query,
        gain_key,
        bias_out,
        gain_two,
        bias_two,
        bias_up,
        bias_down,
    ) = split_vectors(vectors)
    returned = lax.all_to_all(
        pooled_cot.reshape(dp_count, capacity, D), "dp", split_axis=0, concat_axis=0, tiled=True
    ).reshape(dp_count * capacity, D)
    targets = owner_slots(owners[0], capacity)
    routing = (
        jnp.arange(dp_count * capacity, dtype=jnp.int32)[:, None] == targets[None, :]
    ).astype(jnp.bfloat16)
    image_cot = dot32(routing.T, returned).astype(jnp.bfloat16)
    sizes = counts[0]
    first_low, qkv, unit, scale = project(
        patches, w_qkv, gain_one, bias_one, bias_qkv, gain_query, bias_query, gain_key
    )
    attn, log_total = attend(sizes, qkv)
    x2, second_low, row_grad, mixed_low = middle(
        sizes, patches, attn, w_out, bias_out, gain_two, bias_two, patch_cot, image_cot
    )
    y, second_grad, grad_up, grad_down, up_bias_grad = feed(
        x2, second_low, mixed_low, w_up, w_down, bias_up, bias_down
    )
    (
        out_patches,
        pooled,
        middle_grad,
        attn_grad,
        grad_out,
        gain_two_grad,
        bias_two_grad,
        out_bias_grad,
        down_bias_grad,
    ) = after(sizes, y, x2, second_grad, row_grad, attn, w_out, gain_two)
    outgoing = dot32(routing, pooled).astype(jnp.bfloat16).reshape(dp_count, capacity, D)
    arrived = lax.all_to_all(outgoing, "dp", split_axis=0, concat_axis=0, tiled=True)
    pooled_rows = arrived.reshape(dp_count * capacity, D)
    dqkv, qkv_bias_grad, gain_query_grad, bias_query_grad, gain_key_grad = attend_back(
        sizes, qkv, attn, log_total, attn_grad, unit, scale, gain_query, gain_key
    )
    dqkv = dqkv.reshape(3 * D, slot_count)
    grad_qkv = dot32(dqkv, first_low).astype(jnp.bfloat16)
    patch_grad, gain_one_grad, bias_one_grad = first_back(
        patches, dqkv, w_qkv, gain_one, middle_grad
    )
    vector_local = jnp.concatenate(
        [
            piece.reshape(-1)
            for piece in (
                gain_one_grad,
                bias_one_grad,
                qkv_bias_grad,
                gain_query_grad,
                bias_query_grad,
                gain_key_grad,
                out_bias_grad,
                gain_two_grad,
                bias_two_grad,
                up_bias_grad,
                down_bias_grad,
            )
        ]
    )
    gradients = (grad_qkv, grad_out, grad_up, grad_down)
    moments = (mom_qkv, mom_out, mom_up, mom_down)
    masters = (master_qkv, master_out, master_up, master_down)
    grad_parts, moment_parts, new_masters = [None] * 4, [None] * 4, [None] * 4
    for kind_index in (3, 2, 1, 0):
        gradient = gradients[kind_index].astype(jnp.bfloat16)
        length = gradient.shape[0] // ns_count
        total = sum_rows(gradient.reshape(ns_count, length, D)).astype(jnp.float32)
        moment = MUON_DECAY * moments[kind_index] + total
        moment_low = moment.astype(jnp.bfloat16)
        gram_raw = sum_gram(
            jnp.einsum("rd,re->de", moment_low, moment_low, preferred_element_type=jnp.float32)
        )
        ortho = orthogonalise(moment_low, gram_raw)
        step_scale = MUON_RATE * math.sqrt(max(1.0, length * ns_count / D))
        grad_parts[kind_index] = total
        moment_parts[kind_index] = moment
        new_masters[kind_index] = (
            masters[kind_index] * (1.0 - MUON_RATE * MUON_SHRINK) - step_scale * ortho
        )
    vector_size = vector_local.shape[0]
    padded = -(-vector_size // 1024) * 1024
    vector_grad = sum_everywhere(
        jnp.pad(vector_local, (0, padded - vector_size)).reshape(-1, 128)
    ).reshape(-1)[:vector_size]
    vector_first = BETA_ONE * vec_first + (1.0 - BETA_ONE) * vector_grad
    vector_second = BETA_TWO * vec_second + (1.0 - BETA_TWO) * vector_grad * vector_grad
    first_hat = vector_first / (1.0 - BETA_ONE**STEP)
    second_hat = vector_second / (1.0 - BETA_TWO**STEP)
    vector_new = vectors - ADAM_RATE * first_hat / (jnp.sqrt(second_hat) + 1e-08)
    return (
        out_patches,
        pooled_rows,
        patch_grad,
        grad_parts[0],
        grad_parts[1],
        grad_parts[2],
        grad_parts[3],
        moment_parts[0],
        moment_parts[1],
        moment_parts[2],
        moment_parts[3],
        new_masters[0],
        new_masters[1],
        new_masters[2],
        new_masters[3],
        new_masters[0].astype(jnp.bfloat16),
        new_masters[1].astype(jnp.bfloat16),
        new_masters[2].astype(jnp.bfloat16),
        new_masters[3].astype(jnp.bfloat16),
        vector_grad,
        vector_first,
        vector_second,
        vector_new,
    )


def solution(mesh):
    placed = (
        P(("dp", "ns"), None),
        P(("dp", "ns"), None),
        P(("dp", "ns"), None),
        P(("dp", "ns"), None),
        P(("dp", "ns"), None),
        P("ns", None),
        P("ns", None),
        P("ns", None),
        P("ns", None),
        P("ns", None),
        P("ns", None),
        P("ns", None),
        P("ns", None),
        P(),
        P(),
        P(),
    )
    return jax.shard_map(
        per_device,
        mesh=mesh,
        in_specs=placed,
        out_specs=(
            P(("dp", "ns"), None),
            P(("dp", "ns"), None),
            P(("dp", "ns"), None),
            P("ns", None),
            P("ns", None),
            P("ns", None),
            P("ns", None),
            P("ns", None),
            P("ns", None),
            P("ns", None),
            P("ns", None),
            P("ns", None),
            P("ns", None),
            P("ns", None),
            P("ns", None),
            P("ns", None),
            P("ns", None),
            P("ns", None),
            P("ns", None),
            P(),
            P(),
            P(),
            P(),
        ),
        check_vma=False,
    )
```

```python
import functools
import math

import jax
import jax.numpy as jnp
from jax import lax
from jax.experimental import pallas as pl
from jax.experimental.pallas import tpu as pltpu
from jax.sharding import PartitionSpec as P

D = 768
HD = 64
FF = 3072
ITERS = 4
STEP = 10


NS_A = 3.4445
NS_B = -4.775
NS_C = 2.0315
MUON_RATE = 0.8
MUON_DECAY = 0.5
MUON_SHRINK = 0.01
ADAM_RATE = 0.5
BETA_ONE = 0.9
BETA_TWO = 0.95
MASKED = -1e30


def owner_slots(owners_row, capacity):
    image_total = owners_row.shape[0]
    ordering = jnp.arange(image_total, dtype=jnp.int32)
    earlier = (owners_row[None, :] == owners_row[:, None]) & (ordering[None, :] < ordering[:, None])
    same_before = jnp.sum(earlier.astype(jnp.int32), axis=1)
    return owners_row * capacity + same_before


def swap(value, axis, bit):
    count = lax.axis_size(axis)
    return lax.ppermute(value, axis, [(index, index ^ (1 << bit)) for index in range(count)])


def bit_of(axis, bit):
    return (lax.axis_index(axis) >> bit) & 1


def bits_in(axis):
    return (lax.axis_size(axis) - 1).bit_length()


def tie(values, earlier):
    return lax.optimization_barrier((values, earlier))


def add_low(first, second):
    return (first.astype(jnp.float32) + second.astype(jnp.float32)).astype(jnp.bfloat16)


def halves(value, axis, bit, dim=0):
    mine = bit_of(axis, bit)
    shape = value.shape
    pairs = value.reshape(*shape[:dim], 2, shape[dim] // 2, *shape[dim + 1 :])
    keep = lax.dynamic_index_in_dim(pairs, mine, dim, keepdims=False)
    send = lax.dynamic_index_in_dim(pairs, 1 - mine, dim, keepdims=False)
    return keep, send


def joined(value, other, axis, bit, dim=0):
    mine = bit_of(axis, bit)
    low_half = jnp.where(mine == 0, value, other)
    high_half = jnp.where(mine == 0, other, value)
    return jnp.concatenate([low_half, high_half], axis=dim)


class Chain:
    def __init__(self, steps):
        self.steps = steps
        self.result = None
        self.pending = next(steps)

    def advance(self, came):
        try:
            self.pending = self.steps.send(came)
        except StopIteration as stop:
            self.pending = None
            self.result = stop.value


def meet(*chains, also=()):
    live = [chain for chain in chains if chain.pending is not None]
    cames, also = lax.optimization_barrier((tuple(chain.pending for chain in live), also))
    for chain, came in zip(live, cames):
        chain.advance(came)
    return also


def finish(*chains):
    while any(chain.pending is not None for chain in chains):
        meet(*chains)


def rest_of_dp(value, dim, split):
    first = 1
    split = split and bits_in("dp") > 2
    if split:
        keep, send = halves(value, "dp", 1, dim)
        value = add_low(keep, (yield swap(send, "dp", 1)))
        first = 2
    for bit in range(first, bits_in("dp")):
        value = add_low(value, (yield swap(value, "dp", bit)))
    if split:
        value = joined(value, (yield swap(value, "dp", 1)), "dp", 1, dim)
    other = yield swap(value, "dp", 0)
    return value, other


def sum_up(kept, sent):
    value = add_low(kept, (yield swap(sent, "ns", 1)))
    keep, send = halves(value, "dp", 0)
    return add_low(keep, (yield swap(send, "dp", 0)))


def sum_down(kept, sent):
    keep, send = halves(jnp.stack([kept, sent]), "dp", 0, 1)
    value = add_low(keep, (yield swap(send, "dp", 0)))
    return add_low(value[0], (yield swap(value[1], "ns", 1)))


def sum_blocks(value, split):
    for bit in range(bits_in("ns")):
        mine = bit_of("ns", bit)
        pairs = value.reshape(value.shape[0] // 2, 2, *value.shape[1:])
        keep = lax.dynamic_index_in_dim(pairs, mine, 1, keepdims=False)
        send = lax.dynamic_index_in_dim(pairs, 1 - mine, 1, keepdims=False)
        value = add_low(keep, (yield swap(send, "ns", bit)))
    keep, send = halves(value[0], "dp", 0)
    value = add_low(keep, (yield swap(send, "dp", 0)))
    return (yield from rest_of_dp(value, 0, split))


def sum_vector(value):
    for axis in ("ns", "dp"):
        count = lax.axis_size(axis)
        for bit in range(0, bits_in(axis), 2):
            masks = [1 << bit]
            if bit + 1 < bits_in(axis):
                masks += [2 << bit, 3 << bit]
            came = yield tuple(
                lax.ppermute(value, axis, [(index, index ^ mask) for index in range(count)])
                for mask in masks
            )
            value = value + came[0]
            if len(came) == 3:
                value = value + (came[1] + came[2])
    return value


def sum_gram(gram):
    gram = gram + (yield swap(gram, "ns", 0))
    keep, _ = halves(gram, "ns", 0)
    for bit in range(1, bits_in("ns")):
        keep = keep + (yield swap(keep, "ns", bit))
    other = yield swap(keep, "ns", 0)
    return (keep[None], 0), (other[None], 0)


def by_distance(table):
    place = lax.axis_index("ns")
    return [
        lax.dynamic_index_in_dim(table, place ^ distance, 0, keepdims=True)
        for distance in range(table.shape[0])
    ]


def dot32(first, second):
    return jnp.dot(first, second, preferred_element_type=jnp.float32)


LOW = jnp.bfloat16
F32 = jnp.float32
HEADS = D // HD
BIG = 576
SMALL = 64
TILE = 256
MIB = 1024 * 1024
COST_SCALE = 1e9


def mm(first, second, first_dim=1, second_dim=0):
    return lax.dot_general(
        first,
        second,
        (((first_dim,), (second_dim,)), ((), ())),
        preferred_element_type=F32,
    )


def split_value(value):
    high = value.astype(LOW)
    return high, (value - high.astype(F32)).astype(LOW)


def normalise(values):
    row_mean = jnp.mean(values, axis=-1, keepdims=True)
    centred = values - row_mean
    scale = lax.rsqrt(jnp.mean(centred * centred, axis=-1, keepdims=True) + 1e-06)
    return centred * scale, scale


def norm_back(unit, scale, unit_grad):
    return scale * (
        unit_grad
        - jnp.mean(unit_grad, axis=-1, keepdims=True)
        - unit * jnp.mean(unit_grad * unit, axis=-1, keepdims=True)
    )


def column_sum(values):
    return jnp.sum(values, axis=0, keepdims=True)


def params(mebibytes):
    return pltpu.CompilerParams(vmem_limit_bytes=mebibytes * MIB)


def cost(micros, nbytes):
    return pl.CostEstimate(flops=int(micros * COST_SCALE), bytes_accessed=int(nbytes * COST_SCALE * 1e-9), transcendentals=0)


def whole(shape):
    return pl.BlockSpec(shape, lambda *_: (0,) * len(shape))


def once(shape):
    return pl.BlockSpec(shape, lambda *_: (0,) * len(shape), pipeline_mode=pl.Buffered(1))


def rows_of(width, tile=TILE):
    return pl.BlockSpec((tile, width), lambda i, *_: (i, 0))


def lanes_of(height, tile=TILE):
    return pl.BlockSpec((height, tile), lambda i, *_: (0, i))


STARTS = {}
WIDTHS = dict(gain_one=D, bias_one=D, bias_qkv=3 * D, gain_query=HD, bias_query=HD, gain_key=HD,
              bias_out=D, gain_two=D, bias_two=D, bias_up=FF, bias_down=D)
for part_name, part_width in WIDTHS.items():
    STARTS[part_name] = sum(WIDTHS[other] for other in STARTS)


def vector_row(ref, name):
    start = STARTS[name]
    return ref[:, start : start + WIDTHS[name]]


def to_column(row):
    return jnp.broadcast_to(row, (8, row.shape[1])).T[:, :1]


def to_row(column):
    return jnp.broadcast_to(column, (column.shape[0], 128)).T[:1]


def qkv_part(block):
    return pl.BlockSpec(
        (block.shape[0] - out_rows(block), D), lambda *_: (0, 0), pipeline_mode=pl.Buffered(1)
    )


def out_part(block):
    return pl.BlockSpec((out_rows(block), D), lambda *_: (3, 0), pipeline_mode=pl.Buffered(1))


def out_rows(block):
    return block.shape[0] // 4


def place_blocks(place_ref, refs, store):
    rows = refs[0].shape[0]
    for distance, ref in enumerate(refs):
        start = pl.multiple_of((place_ref[0] ^ distance) * rows, rows)
        store[pl.ds(start, rows), :] = ref[...]


def shape_of(shape, dtype):
    return jax.ShapeDtypeStruct(shape, dtype)


def project_kernel(place_ref, x_ref, w0, w1, w2, w3, vec_ref,
                   h_ref, qkv_ref, unit_ref, scale_ref, w_s, col_s):
    @pl.when(pl.program_id(0) == 0)
    def _():
        place_blocks(place_ref, (w0, w1, w2, w3), w_s)
        start = STARTS["bias_qkv"]
        row = vec_ref[:, start : start + 3 * D + 256]
        col_s[...] = to_column(row)

    unit, _ = normalise(x_ref[...].astype(F32))
    h_low = (unit * vector_row(vec_ref, "gain_one") + vector_row(vec_ref, "bias_one")).astype(LOW)
    h_ref[...] = h_low
    gain_q = col_s[pl.ds(3 * D, HD), :]
    bias_q = col_s[pl.ds(3 * D + HD, HD), :]
    gain_k = col_s[pl.ds(3 * D + 2 * HD, HD), :]
    for part in range(3):
        rows = pl.ds(part * D, D)
        value = mm(w_s[rows, :], h_low, 1, 1) + col_s[rows, :]
        if part == 2:
            qkv_ref[2] = value.astype(LOW)
            continue
        heads = value.reshape(HEADS, HD, value.shape[1])
        centred = heads - jnp.mean(heads, axis=1, keepdims=True)
        scale = lax.rsqrt(jnp.mean(centred * centred, axis=1, keepdims=True) + 1e-06)
        unit_heads = centred * scale
        scale_ref[part] = scale
        unit_ref[part] = unit_heads.reshape(D, -1).astype(LOW)
        if part == 0:
            result = unit_heads * gain_q[None] + bias_q[None]
            result = result.astype(LOW) * LOW(0.125)
        else:
            result = (unit_heads * gain_k[None]).astype(LOW)
        qkv_ref[part] = result.reshape(D, -1)


def project(place, patches, w_blocks, vectors):
    slots = patches.shape[0]
    return pl.pallas_call(
        project_kernel,
        grid_spec=pltpu.PrefetchScalarGridSpec(
            num_scalar_prefetch=1,
            grid=(slots // TILE,),
            in_specs=[rows_of(D)] + [qkv_part(w_blocks[0])] * 4 + [once(vectors.shape)],
            out_specs=[rows_of(D),
                       pl.BlockSpec((3, D, TILE), lambda i, p: (0, 0, i)),
                       pl.BlockSpec((2, D, TILE), lambda i, p: (0, 0, i)),
                       pl.BlockSpec((2, HEADS, 1, TILE), lambda i, p: (0, 0, 0, i))],
            scratch_shapes=[pltpu.VMEM((3 * D, D), LOW), pltpu.VMEM((3 * D + 256, 1), F32)],
        ),
        out_shape=[shape_of((slots, D), LOW), shape_of((3, D, slots), LOW),
                   shape_of((2, D, slots), LOW), shape_of((2, HEADS, 1, slots), F32)],
        compiler_params=params(24),
        cost_estimate=cost(10, 16e6),
        name="project",
    )(place, patches, *w_blocks, vectors)


def used_slots(counts_ref):
    total = counts_ref[0]
    for k in range(1, counts_ref.shape[0]):
        total = total + counts_ref[k]
    return total


def pair_mask(tile_start, used, has_big):
    same = (has_big & (tile_start + SMALL < BIG)) | (tile_start >= used)
    row_half = lax.broadcasted_iota(jnp.int32, (128, 128), 0) // SMALL
    column_half = lax.broadcasted_iota(jnp.int32, (128, 128), 1) // SMALL
    return (row_half == column_half) | same


def soft_columns(scores):
    peak = jnp.max(scores, axis=0, keepdims=True)
    exponent = jnp.exp(scores - peak)
    total = jnp.sum(exponent, axis=0, keepdims=True)
    return exponent.astype(LOW), total, peak + jnp.log(total)


def pair_mask_row(slots, used, has_big):
    row_half = lax.broadcasted_iota(jnp.int32, (128, slots), 0) // SMALL
    slot = lax.broadcasted_iota(jnp.int32, (128, slots), 1)
    column_half = slot // SMALL % 2
    start = slot // 128 * 128
    same = (has_big & (start + SMALL < BIG)) | (start >= used)
    return (row_half == column_half) | same


def attend_kernel(group, counts_ref, qkv_ref, out_ref, log_ref):
    used = used_slots(counts_ref)
    has_big = counts_ref[0] == BIG
    slots = out_ref.shape[1]
    heads = [pl.ds(index * HD, HD) for index in range(group)]

    def narrow(first, last):
        tiles = [slice(start, start + 128) for start in range(first, last, 128)]
        mask = pair_mask_row(slots, used, has_big)[:, first:last]
        span = slice(first, last)
        all_scores = []
        for rows in heads:
            all_scores.append(jnp.concatenate(
                [mm(qkv_ref[1, rows, tile], qkv_ref[0, rows, tile], 0, 0) for tile in tiles], axis=1
            ))
        for index, rows in enumerate(heads):
            scores = jnp.where(mask, all_scores[index], MASKED)
            weights, total, log_total = soft_columns(scores)
            result = jnp.concatenate(
                [mm(qkv_ref[2, rows, tile], weights[:, tile.start - first : tile.stop - first])
                 for tile in tiles], axis=1
            )
            out_ref[rows, span] = (result / total).astype(LOW)
            log_ref[index, :, span] = log_total

    @pl.when(jnp.logical_not(has_big))
    def _():
        narrow(0, 512)

    narrow(512, slots)

    @pl.when(has_big)
    def _():
        for start, width in ((0, 256), (256, 256), (512, 128)):
            span = pl.ds(start, width)
            all_scores = [
                mm(qkv_ref[1, rows, 0:640], qkv_ref[0, rows, span], 0, 0)[:BIG] for rows in heads
            ]
            for index, rows in enumerate(heads):
                weights, total, log_total = soft_columns(all_scores[index])
                weights = jnp.concatenate([weights, jnp.zeros((640 - BIG, width), LOW)], axis=0)
                result = mm(qkv_ref[2, rows, 0:640], weights) / total
                if width == 128:
                    lane = lax.broadcasted_iota(jnp.int32, (1, width), 1)
                    inside = lane < BIG - start
                    result = jnp.where(inside, result, out_ref[rows, span].astype(F32))
                    log_total = jnp.where(inside, log_total, log_ref[index, :, span])
                out_ref[rows, span] = result.astype(LOW)
                log_ref[index, :, span] = log_total

    for first in range(0, slots - 128, 256):

        @pl.when((used >= first) & (used < first + 256) & (used < slots - 128))
        def _():
            def columns(chunk, carry):
                span = pl.ds(pl.multiple_of(chunk * 256, 256), 256)
                slot = chunk * 256 + lax.broadcasted_iota(jnp.int32, (1, 256), 1)
                inside = slot >= used
                key_slot = first + lax.broadcasted_iota(jnp.int32, (256, 256), 0)
                all_scores = [
                    mm(qkv_ref[1, rows, first:slots], qkv_ref[0, rows, span], 0, 0)
                    for rows in heads
                ]
                for index, rows in enumerate(heads):
                    scores = all_scores[index]
                    top = jnp.where(key_slot >= used, scores[:256], MASKED)
                    if slots - first > 256:
                        top = jnp.concatenate([top, scores[256:]], axis=0)
                    weights, total, log_total = soft_columns(top)
                    result = mm(qkv_ref[2, rows, first:slots], weights) / total
                    old = out_ref[rows, span].astype(F32)
                    out_ref[rows, span] = jnp.where(inside, result, old).astype(LOW)
                    log_ref[index, :, span] = jnp.where(inside, log_total, log_ref[index, :, span])
                return carry

            lax.fori_loop(first // 256, slots // 256, columns, 0)


def attend(counts, qkv, group=2):
    slots = qkv.shape[2]
    return pl.pallas_call(
        functools.partial(attend_kernel, group),
        grid_spec=pltpu.PrefetchScalarGridSpec(
            num_scalar_prefetch=1,
            grid=(HEADS // group,),
            in_specs=[pl.BlockSpec((3, group * HD, slots), lambda h, c: (0, h, 0))],
            out_specs=[pl.BlockSpec((group * HD, slots), lambda h, c: (h, 0)),
                       pl.BlockSpec((group, 1, slots), lambda h, c: (h, 0, 0))],
        ),
        out_shape=[shape_of((D, slots), LOW), shape_of((HEADS, 1, slots), F32)],
        compiler_params=params(16),
        cost_estimate=cost(28, 7000000.0),
        name="attend",
    )(counts, qkv)


def attend_back_kernel(group, counts_ref, qkv_ref, attn_ref, log_ref, grad_ref, unit_ref,
                       scale_ref, vec_ref, _, dqkv_ref, bias_ref, gains_ref, dq_s, dk_s, dv_s):
    used = used_slots(counts_ref)
    has_big = counts_ref[0] == BIG
    slots = attn_ref.shape[1]
    start = STARTS["gain_query"]
    columns = to_column(vec_ref[:, start : start + 256])
    gain_q, gain_k = columns[:HD], columns[2 * HD : 3 * HD]

    @pl.when(pl.program_id(0) == 0)
    def _():
        gains_ref[...] = jnp.zeros_like(gains_ref)

    def head_rows(index):
        return pl.ds(index * HD, HD)

    def delta_of(index, span):
        return column_sum(
            grad_ref[head_rows(index), span].astype(F32)
            * attn_ref[head_rows(index), span].astype(F32)
        )

    def narrow(first, last):
        tiles = [slice(start, start + 128) for start in range(first, last, 128)]
        mask = pair_mask_row(slots, used, has_big)[:, first:last]
        span = slice(first, last)

        def wide(product):
            return jnp.concatenate([product(tile) for tile in tiles], axis=1)

        def inner(tile):
            return slice(tile.start - first, tile.stop - first)

        all_scores, all_grads = [], []
        for index in range(group):
            rows = head_rows(index)
            all_scores.append(wide(
                lambda tile: mm(qkv_ref[1, rows, tile], qkv_ref[0, rows, tile], 0, 0)))
            all_grads.append(wide(
                lambda tile: mm(qkv_ref[2, rows, tile], grad_ref[rows, tile], 0, 0)))
        for index in range(group):
            rows = head_rows(index)
            scores = all_scores[index] - log_ref[index, :, span]
            probs = jnp.exp(jnp.where(mask, scores, MASKED))
            score_low = (probs * (all_grads[index] - delta_of(index, span))).astype(LOW)
            probs_low = probs.astype(LOW)
            dv_s[rows, span] = wide(
                lambda tile: mm(grad_ref[rows, tile], probs_low[:, inner(tile)], 1, 1))
            dk_s[rows, span] = wide(
                lambda tile: mm(qkv_ref[0, rows, tile], score_low[:, inner(tile)], 1, 1))
            dq_s[rows, span] = wide(
                lambda tile: mm(qkv_ref[1, rows, tile], score_low[:, inner(tile)]))

    @pl.when(jnp.logical_not(has_big))
    def _():
        narrow(0, 512)

    @pl.when(used > 512)
    def _():
        narrow(512, slots)

    @pl.when(used <= 512)
    def _():
        for store in (dq_s, dk_s, dv_s):
            store[:, 512:slots] = jnp.zeros((store.shape[0], slots - 512), F32)

    @pl.when(has_big)
    def _():
        wide = pl.ds(0, 640)
        dk = [jnp.zeros((HD, 640), F32)] * group
        dv = [jnp.zeros((HD, 640), F32)] * group
        for start, width in ((0, 256), (256, 256), (512, 128)):
            span = pl.ds(start, width)
            lane = lax.broadcasted_iota(jnp.int32, (1, width), 1)
            all_scores, all_grads = [], []
            for index in range(group):
                rows = head_rows(index)
                all_scores.append(mm(qkv_ref[1, rows, wide], qkv_ref[0, rows, span], 0, 0)[:BIG])
                all_grads.append(mm(qkv_ref[2, rows, wide], grad_ref[rows, span], 0, 0)[:BIG])
            for index in range(group):
                rows = head_rows(index)
                probs = jnp.exp(all_scores[index] - log_ref[index, :, span])
                if width == 128:
                    probs = jnp.where(lane < BIG - start, probs, 0.0)
                score_low = (probs * (all_grads[index] - delta_of(index, span))).astype(LOW)
                blank = jnp.zeros((640 - BIG, width), LOW)
                score_low = jnp.concatenate([score_low, blank], axis=0)
                probs_low = jnp.concatenate([probs.astype(LOW), blank], axis=0)
                dv[index] = dv[index] + mm(grad_ref[rows, span], probs_low, 1, 1)
                dk[index] = dk[index] + mm(qkv_ref[0, rows, span], score_low, 1, 1)
                dq = mm(qkv_ref[1, rows, wide], score_low)
                if width == 128:
                    dq = jnp.where(lane < BIG - start, dq, dq_s[rows, span])
                dq_s[rows, span] = dq
        inside = lax.broadcasted_iota(jnp.int32, (1, 640), 1) < BIG
        for index in range(group):
            rows = head_rows(index)
            dk_s[rows, wide] = jnp.where(inside, dk[index], dk_s[rows, wide])
            dv_s[rows, wide] = jnp.where(inside, dv[index], dv_s[rows, wide])

    sums = [jnp.zeros((HD, 1), F32)] * 3
    biases = [[], [], []]
    for index in range(group):
        rows = head_rows(index)
        for part, store, gain in ((0, dq_s, gain_q), (1, dk_s, gain_k)):
            unit = unit_ref[part, rows, :].astype(F32)
            grad = store[rows, :]
            if part == 0:
                grad = grad * 0.125
                sums[0] = sums[0] + jnp.sum(grad * unit, axis=1, keepdims=True)
                sums[1] = sums[1] + jnp.sum(grad, axis=1, keepdims=True)
            else:
                sums[2] = sums[2] + jnp.sum(grad * unit, axis=1, keepdims=True)
            unit_grad = grad * gain
            result = scale_ref[part, index] * (
                unit_grad
                - jnp.mean(unit_grad, axis=0, keepdims=True)
                - unit * jnp.mean(unit_grad * unit, axis=0, keepdims=True)
            )
            result = result.astype(LOW)
            dqkv_ref[part, rows, :] = result
            biases[part].append(jnp.sum(result.astype(F32), axis=1, keepdims=True))
        result = dv_s[rows, :].astype(LOW)
        dqkv_ref[2, rows, :] = result
        biases[2].append(jnp.sum(result.astype(F32), axis=1, keepdims=True))
    for part in range(3):
        bias_ref[part] = to_row(jnp.concatenate(biases[part], axis=0))
    blank = jnp.zeros((HD, 1), F32)
    gains_ref[:, 0:128] += to_row(jnp.concatenate(sums[:2], axis=0))
    gains_ref[:, 128:256] += to_row(jnp.concatenate([sums[2], blank], axis=0))


def attend_back(counts, qkv, attn, log_total, attn_grad, unit, scale, vectors, earlier, half,
                group=2):
    slots = qkv.shape[2]
    steps = HEADS // group // 2
    first = half * steps
    head_block = pl.BlockSpec((group * HD, slots), lambda h, c: (h + first, 0))
    dqkv_block = pl.BlockSpec((3, group * HD, slots), lambda h, c: (0, h + first, 0))
    held = pl.BlockSpec(memory_space=pl.ANY)
    extra = [vectors if earlier is None else earlier]
    return pl.pallas_call(
        functools.partial(attend_back_kernel, group),
        grid_spec=pltpu.PrefetchScalarGridSpec(
            num_scalar_prefetch=1,
            grid=(steps,),
            in_specs=[dqkv_block,
                      head_block,
                      pl.BlockSpec((group, 1, slots), lambda h, c: (h + first, 0, 0)),
                      head_block,
                      pl.BlockSpec((2, group * HD, slots), lambda h, c: (0, h + first, 0)),
                      pl.BlockSpec((2, group, 1, slots), lambda h, c: (0, h + first, 0, 0)),
                      whole(vectors.shape), held],
            out_specs=[dqkv_block,
                       pl.BlockSpec((3, 1, group * HD), lambda h, c: (0, 0, h)),
                       whole((1, 256))],
            scratch_shapes=[pltpu.VMEM((group * HD, slots), F32)] * 3,
        ),
        out_shape=[shape_of((3, D, slots), LOW), shape_of((3, 1, D // 2), F32),
                   shape_of((1, 256), F32)],
        input_output_aliases={} if earlier is None else {8: 0},
        compiler_params=params(20),
        cost_estimate=cost(14, 8e6),
        name="attend_back",
    )(counts, qkv, attn, log_total, attn_grad, unit, scale, vectors, *extra)


def segment_picker(counts_ref, first, width):
    images = counts_ref.shape[0]
    slot = first + lax.broadcasted_iota(jnp.int32, (images, width), 1)
    image = lax.broadcasted_iota(jnp.int32, (images, width), 0)
    start = jnp.int32(0)
    picked = jnp.zeros((images, width), jnp.bool_)
    for k in range(images):
        end = start + counts_ref[k]
        picked = picked | ((image == k) & (slot >= start) & (slot < end))
        start = end
    return picked.astype(F32), start


def image_sizes(counts_ref):
    images = counts_ref.shape[0]
    image = lax.broadcasted_iota(jnp.int32, (images, 1), 0)
    sizes = jnp.zeros((images, 1), F32)
    for k in range(images):
        sizes = jnp.where(image == k, jnp.maximum(counts_ref[k], 1).astype(F32), sizes)
    return sizes


def middle_kernel(counts_ref, place_ref, x_ref, attn_ref, w0, w1, w2, w3, vec_ref, cot_ref,
                  image_ref, x2_ref, h_ref, dy_ref, mix_ref, w_s):
    @pl.when(pl.program_id(0) == 0)
    def _():
        place_blocks(place_ref, (w0, w1, w2, w3), w_s)

    x2 = x_ref[...].astype(F32) + mm(attn_ref[...], w_s[...], 0, 1) + vector_row(vec_ref, "bias_out")
    x2_ref[...] = x2
    unit, _ = normalise(x2)
    h_ref[...] = (
        unit * vector_row(vec_ref, "gain_two") + vector_row(vec_ref, "bias_two")
    ).astype(LOW)
    tile = x_ref.shape[0]
    first = pl.program_id(0) * tile
    picker, used = segment_picker(counts_ref, first, tile)
    picker = picker.astype(LOW)
    image_grad = image_ref[...].astype(F32) / image_sizes(counts_ref)
    dy = jnp.zeros(x2.shape, F32)
    rest = image_grad
    for _ in range(3):
        high, rest = split_value32(rest)
        dy = dy + mm(picker, high, 0, 0)
    slot = first + lax.broadcasted_iota(jnp.int32, (tile, 1), 0)
    dy = dy + jnp.where(slot < used, cot_ref[...].astype(F32), 0.0)
    dy_ref[...] = dy
    mix_ref[...] = dy.astype(LOW)


def split_value32(value):
    high = value.astype(LOW)
    return high, value - high.astype(F32)


def middle(counts, place, patches, attn, w_blocks, vectors, patch_cot, image_cot):
    slots = patches.shape[0]
    images = counts.shape[0]
    return pl.pallas_call(
        middle_kernel,
        grid_spec=pltpu.PrefetchScalarGridSpec(
            num_scalar_prefetch=2,
            grid=(slots // TILE,),
            in_specs=[rows_of(D), lanes_of(D)] + [out_part(w_blocks[0])] * 4
            + [whole(vectors.shape), rows_of(D), whole((images, D))],
            out_specs=[rows_of(D)] * 4,
            scratch_shapes=[pltpu.VMEM((D, D), LOW)],
        ),
        out_shape=[shape_of((slots, D), F32), shape_of((slots, D), LOW),
                   shape_of((slots, D), F32), shape_of((slots, D), LOW)],
        compiler_params=params(20),
        cost_estimate=cost(9, 20e6),
        name="middle",
    )(counts, place, patches, attn, *w_blocks, vectors, patch_cot, image_cot)


def feed_kernel(distances, start_y, y_in_ref, dh_in_ref, h_ref, mix_ref, up_a, down_a, up_b,
                down_b, bias_ref, vec_ref,
                y_ref, dh_ref, grad_a, grad_b, bias_grad_a, bias_grad_b):
    @pl.when(pl.program_id(0) == 0)
    def _():
        if start_y:
            y_ref[...] = y_in_ref[...] + vector_row(vec_ref, "bias_down")
            dh_ref[...] = jnp.zeros_like(dh_ref)
        else:
            y_ref[...] = y_in_ref[...]
            dh_ref[...] = dh_in_ref[...]

    slots = h_ref.shape[0]
    for distance, up_ref, down_ref, grad_ref, bias_grad_ref in (
        (distances[0], up_a, down_a, grad_a, bias_grad_a),
        (distances[1], up_b, down_b, grad_b, bias_grad_b),
    ):
        up, down = up_ref[...], down_ref[...]
        h, mix = h_ref[...], mix_ref[...]
        u = mm(up, h, 1, 1) + to_column(bias_ref[distance : distance + 1])
        back = mm(down, mix, 1, 1)
        gate = 0.5 * (1.0 + lax.erf(u * (0.5**0.5)))
        slope = gate + u * (jnp.exp(-0.5 * u * u) * ((0.5 / math.pi) ** 0.5))
        hidden = (u * gate).astype(LOW)
        pre = (back * slope).astype(LOW)
        y_ref[...] += mm(hidden, down, 0, 0)
        dh_ref[...] += mm(pre, up, 0, 0)
        grad_up = mm(pre, h)
        grad_down = mm(hidden, mix)
        bias_grad = to_row(jnp.sum(pre.astype(F32), axis=1, keepdims=True))
        grad_ref[0] = grad_up.astype(LOW)
        grad_ref[1] = grad_down.astype(LOW)
        bias_grad_ref[...] = bias_grad


def feed(distances, y, dh2, h2, mix, pair_a, pair_b, bias_table, vectors, block=256):
    slots = y.shape[0]
    units = pair_a.shape[1]
    start_y = dh2 is None
    if start_y:
        dh2 = y
    up = pl.BlockSpec((None, block, D), lambda i: (0, i, 0))
    down = pl.BlockSpec((None, block, D), lambda i: (1, i, 0))
    bias = pl.BlockSpec((1, block), lambda i: (0, i))
    both = pl.BlockSpec((2, block, D), lambda i: (0, i, 0))
    dh_spec = pl.BlockSpec((8, D), lambda i: (0, 0)) if start_y else once((slots, D))
    return pl.pallas_call(
        functools.partial(feed_kernel, distances, start_y),
        grid=(units // block,),
        in_specs=[once((slots, D)), dh_spec, once((slots, D)), once((slots, D)),
                  up, down, up, down, pl.BlockSpec((bias_table.shape[0], block), lambda i: (0, i)),
                  whole(vectors.shape)],
        out_specs=[once((slots, D)), once((slots, D)), both, both, bias, bias],
        out_shape=[shape_of((slots, D), F32), shape_of((slots, D), F32),
                   shape_of((2, units, D), LOW), shape_of((2, units, D), LOW),
                   shape_of((1, units), F32), shape_of((1, units), F32)],
        compiler_params=params(26),
        cost_estimate=cost(24, 25e6),
        name="feed",
    )(y, dh2, h2, mix, pair_a, pair_a, pair_b, pair_b, bias_table, vectors)


def after_kernel(counts_ref, place_ref, y_ref, x2_ref, dh_ref, dy_ref, attn_ref, w0, w1, w2, w3,
                 vec_ref, out_ref, pooled_ref, dx2_ref, dattn_ref, grad_out_ref, sums_ref,
                 pool_s, grad_s, w_s):
    step = pl.program_id(0)

    @pl.when(step == 0)
    def _():
        pool_s[...] = jnp.zeros_like(pool_s)
        grad_s[...] = jnp.zeros_like(grad_s)
        sums_ref[...] = jnp.zeros_like(sums_ref)
        place_blocks(place_ref, (w0, w1, w2, w3), w_s)

    y = y_ref[...]
    tile = y.shape[0]
    out_ref[...] = y.astype(LOW)
    picker, _ = segment_picker(counts_ref, step * tile, tile)
    picker = picker.astype(LOW)
    rest = y
    pooled = pool_s[...]
    for _ in range(3):
        high, rest = split_value32(rest)
        pooled = pooled + mm(picker, high)
    pool_s[...] = pooled
    pooled_ref[...] = (pooled / image_sizes(counts_ref)).astype(LOW)
    unit, scale = normalise(x2_ref[...])
    dh = dh_ref[...]
    sums_ref[0:1] += column_sum(dh * unit)
    sums_ref[1:2] += column_sum(dh)
    dy = dy_ref[...]
    sums_ref[3:4] += column_sum(dy.astype(LOW).astype(F32))
    dx2 = dy + norm_back(unit, scale, dh * vector_row(vec_ref, "gain_two"))
    dx2_ref[...] = dx2
    da = dx2.astype(LOW)
    sums_ref[2:3] += column_sum(da.astype(F32))
    dattn_ref[...] = mm(w_s[...], da, 0, 1).astype(LOW)
    grad = grad_s[...] + mm(da, attn_ref[...], 0, 1)
    grad_s[...] = grad
    grad_out_ref[...] = grad.astype(LOW)


def after(counts, place, y, x2, dh2, dy, attn, w_blocks, vectors):
    slots = y.shape[0]
    images = counts.shape[0]
    return pl.pallas_call(
        after_kernel,
        grid_spec=pltpu.PrefetchScalarGridSpec(
            num_scalar_prefetch=2,
            grid=(slots // TILE,),
            in_specs=[rows_of(D), rows_of(D), rows_of(D), rows_of(D), lanes_of(D)]
            + [out_part(w_blocks[0])] * 4 + [whole(vectors.shape)],
            out_specs=[rows_of(D), whole((images, D)), rows_of(D), lanes_of(D), whole((D, D)),
                       whole((8, D))],
            scratch_shapes=[pltpu.VMEM((images, D), F32), pltpu.VMEM((D, D), F32),
                            pltpu.VMEM((D, D), LOW)],
        ),
        out_shape=[shape_of((slots, D), LOW), shape_of((images, D), LOW),
                   shape_of((slots, D), F32), shape_of((D, slots), LOW), shape_of((D, D), LOW),
                   shape_of((8, D), F32)],
        compiler_params=params(28),
        cost_estimate=cost(12, 25e6),
        name="after",
    )(counts, place, y, x2, dh2, dy, attn, *w_blocks, vectors)


def first_back_kernel(place_ref, x_ref, dqkv_ref, w0, w1, w2, w3, vec_ref, dx2_ref,
                      out_ref, sums_ref, w_s):
    @pl.when(pl.program_id(0) == 0)
    def _():
        sums_ref[...] = jnp.zeros_like(sums_ref)
        place_blocks(place_ref, (w0, w1, w2, w3), w_s)

    dh = mm(dqkv_ref[...], w_s[...], 0, 0)
    unit, scale = normalise(x_ref[...].astype(F32))
    sums_ref[0:1] += column_sum(dh * unit)
    sums_ref[1:2] += column_sum(dh)
    out_ref[...] = dx2_ref[...] + norm_back(unit, scale, dh * vector_row(vec_ref, "gain_one"))


def first_back(place, patches, dqkv, w_blocks, vectors, dx2):
    slots = patches.shape[0]
    return pl.pallas_call(
        first_back_kernel,
        grid_spec=pltpu.PrefetchScalarGridSpec(
            num_scalar_prefetch=1,
            grid=(slots // TILE,),
            in_specs=[rows_of(D), lanes_of(3 * D)] + [qkv_part(w_blocks[0])] * 4
            + [whole(vectors.shape), rows_of(D)],
            out_specs=[rows_of(D), whole((8, D))],
            scratch_shapes=[pltpu.VMEM((3 * D, D), LOW)],
        ),
        out_shape=[shape_of((slots, D), F32), shape_of((8, D), F32)],
        compiler_params=params(22),
        cost_estimate=cost(10, 17e6),
        name="first_back",
    )(place, patches, dqkv, *w_blocks, vectors, dx2)


SIDE = 256
GRID_BLOCKS = [(i, j) for i in range(D // SIDE) for j in range(i, D // SIDE)]


def moment_kernel(half_ref, own_ref, other_ref, mom_ref, grad_ref, moment_ref, gram_ref):
    rows = own_ref.shape[0]
    for ref, place in ((own_ref, half_ref[0]), (other_ref, 1 - half_ref[0])):
        span = pl.ds(pl.multiple_of(place * rows, rows), rows)
        grad = ref[...].astype(F32)
        grad_ref[span, :] = grad
        moment_ref[span, :] = MUON_DECAY * mom_ref[span, :] + grad
    moment_low = moment_ref[...].astype(LOW)
    for index, (i, j) in enumerate(GRID_BLOCKS):
        gram_ref[index] = mm(
            moment_low[:, i * SIDE : (i + 1) * SIDE], moment_low[:, j * SIDE : (j + 1) * SIDE], 0, 0
        )


def one_of(stack, index):
    return pl.BlockSpec(
        (None,) + stack.shape[1:],
        lambda i: (index,) + (0,) * (stack.ndim - 1),
        pipeline_mode=pl.Buffered(1),
    )


def moment_and_gram(half, own, other, mom):
    rows = mom.shape[0]
    blocks = len(GRID_BLOCKS)
    out_shape = [shape_of((rows, D), F32), shape_of((rows, D), F32),
                 shape_of((blocks, SIDE, SIDE), F32)]
    (own, own_index), (other, other_index) = own, other
    return pl.pallas_call(
        moment_kernel,
        grid=(1,),
        in_specs=[pl.BlockSpec(memory_space=pltpu.SMEM), one_of(own, own_index),
                  one_of(other, other_index), once((rows, D))],
        out_specs=[once(leaf.shape) for leaf in out_shape],
        out_shape=out_shape,
        compiler_params=params(16),
        cost_estimate=cost(4, rows * D * 14 + blocks * SIDE * SIDE * 4),
        name="moment",
    )(half, own, other, mom)


def muon_kernel(step_scale, half_ref, own_ref, other_ref, moment_ref, master_ref,
                new_ref, copy_ref, gram_s, low_s, rest_s, mix_s, rows_s, gram_ref):
    count = own_ref.shape[0]
    for index in range(count):
        gram_ref[half_ref[0] * count + index] = own_ref[index]
        gram_ref[(1 - half_ref[0]) * count + index] = other_ref[index]
    spans = [slice(i * SIDE, (i + 1) * SIDE) for i in range(D // SIDE)]

    def put(refs, i, j, blocks):
        for ref, block in zip(refs, blocks):
            ref[spans[i], spans[j]] = block
            if i != j:
                ref[spans[j], spans[i]] = block.T

    total = jnp.zeros((1, 1), F32)
    row = lax.broadcasted_iota(jnp.int32, (SIDE, SIDE), 0)
    column = lax.broadcasted_iota(jnp.int32, (SIDE, SIDE), 1)
    for index, (i, j) in enumerate(GRID_BLOCKS):
        if i == j:
            kept = jnp.where(row == column, gram_ref[index], 0.0)
            total = total + jnp.sum(jnp.sum(kept, axis=0, keepdims=True), axis=1, keepdims=True)
    scale = 1.0 / (jnp.sqrt(total) + 1e-07)
    square = scale * scale
    for index, (i, j) in enumerate(GRID_BLOCKS):
        block = gram_ref[index] * square
        put((gram_s,), i, j, (block,))
        put((low_s, rest_s), i, j, split_value(block))
    rows_s[...] = moment_ref[...].astype(LOW)
    for iteration in range(ITERS):
        careful = iteration == 0
        for i, j in GRID_BLOCKS:
            squared = mm(low_s[spans[i], :], low_s[:, spans[j]])
            put((mix_s,), i, j, ((NS_B * gram_s[spans[i], spans[j]] + NS_C * squared).astype(LOW),))
        if iteration == ITERS - 1:
            break
        middle_blocks = []
        for i in range(D // SIDE):
            for j in range(0 if careful else i, D // SIDE):
                block = NS_A * gram_s[spans[i], spans[j]] + mm(low_s[spans[i], :], mix_s[:, spans[j]])
                if careful:
                    block = block + mm(rest_s[spans[i], :], mix_s[:, spans[j]])
                middle_blocks.append((i, j, block))
        for i, j, block in middle_blocks:
            gram_s[spans[i], spans[j]] = block
            if careful:
                low_s[spans[i], spans[j]], rest_s[spans[i], spans[j]] = split_value(block)
            else:
                put((low_s,), i, j, (block.astype(LOW),))
        renewed = NS_A * rows_s[...].astype(F32) + mm(rows_s[...], mix_s[...])
        if careful:
            renewed = renewed * scale
        rows_s[...] = renewed.astype(LOW)
        gram_blocks = []
        for i, j in GRID_BLOCKS:
            block = NS_A * gram_s[spans[i], spans[j]] + mm(mix_s[spans[i], :], low_s[:, spans[j]])
            if careful:
                block = block + mm(mix_s[spans[i], :], rest_s[:, spans[j]])
            gram_blocks.append((i, j, block))
        for i, j, block in gram_blocks:
            gram_s[spans[i], spans[j]] = block
            put((low_s,), i, j, (block.astype(LOW),))
    renewed = NS_A * rows_s[...].astype(F32) + mm(rows_s[...], mix_s[...])
    new = master_ref[...] * (1.0 - MUON_RATE * MUON_SHRINK) - step_scale * renewed
    new_ref[...] = new
    copy_ref[...] = new.astype(LOW)


def muon(half, own, other, moment, master, step_scale):
    rows = moment.shape[0]
    (own, own_index), (other, other_index) = own, other
    out_shape = [shape_of((rows, D), F32), shape_of((rows, D), LOW)]
    return pl.pallas_call(
        functools.partial(muon_kernel, step_scale),
        grid=(1,),
        in_specs=[pl.BlockSpec(memory_space=pltpu.SMEM), one_of(own, own_index),
                  one_of(other, other_index), once((rows, D)), once((rows, D))],
        out_specs=[once(leaf.shape) for leaf in out_shape],
        out_shape=out_shape,
        scratch_shapes=[pltpu.VMEM((D, D), F32), pltpu.VMEM((D, D), LOW), pltpu.VMEM((D, D), LOW),
                        pltpu.VMEM((D, D), LOW), pltpu.VMEM((rows, D), LOW),
                        pltpu.VMEM((len(GRID_BLOCKS), SIDE, SIDE), F32)],
        compiler_params=params(30),
        cost_estimate=cost(18, rows * D * 14),
        name="muon",
    )(half, own, other, moment, master)


def per_device(
    patches,
    counts,
    owners,
    pooled_cot,
    patch_cot,
    master_qkv,
    master_out,
    master_up,
    master_down,
    mom_qkv,
    mom_out,
    mom_up,
    mom_down,
    vectors,
    vec_first,
    vec_second,
):
    dp_count = lax.axis_size("dp")
    ns_count = lax.axis_size("ns")
    slot_count = patches.shape[0]
    image_total = counts.shape[1]
    capacity = pooled_cot.shape[0] // dp_count
    low = jnp.bfloat16
    place = lax.axis_index("ns").astype(jnp.int32).reshape(1)
    half_dp = bit_of("dp", 0).astype(jnp.int32).reshape(1)
    half_ns = bit_of("ns", 0).astype(jnp.int32).reshape(1)

    own_first = jnp.concatenate([master_qkv, master_out]).astype(low)
    w_first = (own_first, swap(own_first, "ns", 0), swap(own_first, "ns", 1))
    row = vectors.reshape(1, -1)
    bias_start = STARTS["bias_up"]
    bias_table = jnp.concatenate(
        by_distance(vectors[bias_start : bias_start + FF].reshape(ns_count, -1)), axis=0
    )
    returned = lax.all_to_all(
        pooled_cot.reshape(dp_count, capacity, D), "dp", split_axis=0, concat_axis=0, tiled=True
    ).reshape(dp_count * capacity, D)
    targets = owner_slots(owners[0], capacity)
    routing = (
        jnp.arange(dp_count * capacity, dtype=jnp.int32)[:, None] == targets[None, :]
    ).astype(low)
    image_cot = dot32(routing.T, returned).astype(low)
    sizes = counts[0]
    own_pair = jnp.stack([master_up, master_down]).astype(low)
    far_first, (own_pair, image_cot) = tie(w_first[2], (own_pair, image_cot))
    w_first = (w_first[0], w_first[1], far_first, swap(far_first, "ns", 0))
    own_pair, _ = tie(own_pair, far_first)
    near_pair, next_pair, far_pair = own_pair, swap(own_pair, "ns", 0), swap(own_pair, "ns", 1)
    first_low, qkv, unit, scale = project(place, patches, w_first, row)
    attn, log_total = attend(sizes, qkv)
    attn, far_pair = tie(attn, far_pair)
    pairs = (near_pair, next_pair, far_pair, swap(far_pair, "ns", 0))
    x2, second_low, row_grad, mixed_low = middle(
        sizes, place, patches, attn, w_first, row, patch_cot, image_cot
    )
    y, second_grad, grad_3, grad_1, bias_3, bias_1 = feed(
        (3, 1), x2, None, second_low, mixed_low, pairs[3], pairs[1], bias_table, row
    )
    came_3, came_1 = swap(grad_3, "ns", 0), swap(grad_1, "ns", 0)
    y, second_grad, grad_2, grad_0, bias_2, bias_0 = feed(
        (2, 0), y, second_grad, second_low, mixed_low, pairs[2], pairs[0], bias_table, row
    )
    sent, kept = add_low(grad_2, came_3), add_low(grad_0, came_1)
    up, down = Chain(sum_up(kept[0], sent[0])), Chain(sum_down(kept[1], sent[1]))
    y, (sent, kept) = tie(y, (sent, kept))
    out_patches, pooled, middle_grad, attn_grad, grad_out, sums_two = after(
        sizes, place, y, x2, second_grad, row_grad, attn, w_first, row
    )
    out = Chain(sum_blocks(grad_out.reshape(ns_count, -1, D), False))
    dqkv, bias_a, gains_a = attend_back(
        sizes, qkv, attn, log_total, attn_grad, unit, scale, row, None, 0
    )
    dqkv = meet(up, down, out, also=dqkv)
    dqkv, bias_b, gains_b = attend_back(
        sizes, qkv, attn, log_total, attn_grad, unit, scale, row, dqkv, 1
    )
    outgoing = dot32(routing, pooled).astype(low).reshape(dp_count, capacity, D)
    dqkv = meet(up, down, out, also=dqkv.reshape(3 * D, slot_count))
    pair = Chain(rest_of_dp(jnp.stack([up.result, down.result]), 1, True))
    grad_qkv = dot32(dqkv, first_low).astype(low)
    three = Chain(sum_blocks(grad_qkv.reshape(ns_count, -1, D), True))
    meet(three)
    middle_grad = meet(pair, out, also=middle_grad)
    patch_grad, sums_one = first_back(place, patches, dqkv, w_first, row, middle_grad)
    sums_one, patch_grad = meet(three, also=(sums_one, patch_grad))
    gains = gains_a + gains_b
    up_bias_grad = by_distance(jnp.concatenate([bias_0, bias_1, bias_2, bias_3], axis=0))
    vector_local = jnp.concatenate(
        [
            sums_one[0:1],
            sums_one[1:2],
            jnp.concatenate([bias_a, bias_b], axis=2).reshape(1, 3 * D),
            gains[:, : 3 * HD],
            sums_two[2:3],
            sums_two[0:1],
            sums_two[1:2],
            *up_bias_grad,
            sums_two[3:4],
        ],
        axis=1,
    )
    vector_size = vector_local.shape[1]
    padded = -(-vector_size // 1024) * 1024
    vector = Chain(sum_vector(
        jnp.pad(vector_local, ((0, 0), (0, padded - vector_size))).reshape(-1, 128)
    ))
    moments = (mom_qkv, mom_out, mom_up, mom_down)
    masters = (master_qkv, master_out, master_up, master_down)
    grad_parts, moment_parts = [None] * 4, [None] * 4
    new_masters, copies = [None] * 4, [None] * 4

    def momentum(kind, own, other):
        grad_parts[kind], moment_parts[kind], gram = moment_and_gram(
            half_dp, own, other, moments[kind]
        )
        return Chain(sum_gram(gram))

    def iterate(kind, halves_of_gram):
        rows = moments[kind].shape[0] * ns_count
        step_scale = MUON_RATE * math.sqrt(max(1.0, rows / D))
        new_masters[kind], copies[kind] = muon(
            half_ns, *halves_of_gram, moment_parts[kind], masters[kind], step_scale
        )

    meet(pair, out, vector)
    meet(three)
    meet(pair, out, vector)
    outgoing = meet(three, out, also=outgoing)
    finish(out)
    gram_out = momentum(1, *((half[None], 0) for half in out.result))
    arrived = lax.all_to_all(outgoing, "dp", split_axis=0, concat_axis=0, tiled=True)
    pooled_rows = arrived.reshape(dp_count * capacity, D)
    pooled_rows = meet(three, gram_out, vector, also=pooled_rows)
    finish(vector)
    finish(pair)
    gram_up = momentum(2, *((half, 0) for half in pair.result))
    gram_down = momentum(3, *((half, 1) for half in pair.result))
    meet(three, gram_out)
    meet(gram_up)
    finish(three)
    gram_three = momentum(0, *((half[None], 0) for half in three.result))
    meet(gram_down, gram_out)
    finish(gram_out)
    iterate(1, gram_out.result)
    new_masters[1] = meet(gram_up, gram_three, also=new_masters[1])
    finish(gram_up)
    iterate(2, gram_up.result)
    new_masters[2] = meet(gram_down, also=new_masters[2])
    finish(gram_down)
    iterate(3, gram_down.result)
    new_masters[3] = meet(gram_three, also=new_masters[3])
    finish(gram_three)
    iterate(0, gram_three.result)
    vector_grad = vector.result.reshape(-1)[:vector_size]
    vector_first = BETA_ONE * vec_first + (1.0 - BETA_ONE) * vector_grad
    vector_second = BETA_TWO * vec_second + (1.0 - BETA_TWO) * vector_grad * vector_grad
    first_hat = vector_first / (1.0 - BETA_ONE**STEP)
    second_hat = vector_second / (1.0 - BETA_TWO**STEP)
    vector_new = vectors - ADAM_RATE * first_hat / (jnp.sqrt(second_hat) + 1e-08)
    return (
        out_patches,
        pooled_rows,
        patch_grad,
        grad_parts[0],
        grad_parts[1],
        grad_parts[2],
        grad_parts[3],
        moment_parts[0],
        moment_parts[1],
        moment_parts[2],
        moment_parts[3],
        new_masters[0],
        new_masters[1],
        new_masters[2],
        new_masters[3],
        *copies,
        vector_grad,
        vector_first,
        vector_second,
        vector_new,
    )


def solution(mesh):
    placed = (
        P(("dp", "ns"), None),
        P(("dp", "ns"), None),
        P(("dp", "ns"), None),
        P(("dp", "ns"), None),
        P(("dp", "ns"), None),
        P("ns", None),
        P("ns", None),
        P("ns", None),
        P("ns", None),
        P("ns", None),
        P("ns", None),
        P("ns", None),
        P("ns", None),
        P(),
        P(),
        P(),
    )
    return jax.shard_map(
        per_device,
        mesh=mesh,
        in_specs=placed,
        out_specs=(
            P(("dp", "ns"), None),
            P(("dp", "ns"), None),
            P(("dp", "ns"), None),
            P("ns", None),
            P("ns", None),
            P("ns", None),
            P("ns", None),
            P("ns", None),
            P("ns", None),
            P("ns", None),
            P("ns", None),
            P("ns", None),
            P("ns", None),
            P("ns", None),
            P("ns", None),
            P("ns", None),
            P("ns", None),
            P("ns", None),
            P("ns", None),
            P(),
            P(),
            P(),
            P(),
        ),
        check_vma=False,
    )
```

```python
import functools
import math

import jax
import jax.numpy as jnp
from jax import lax
from jax.experimental import pallas as pl
from jax.experimental.pallas import tpu as pltpu
from jax.sharding import PartitionSpec as P

D = 768
HD = 64
FF = 3072
ITERS = 4
STEP = 10


NS_A = 3.4445
NS_B = -4.775
NS_C = 2.0315
MUON_RATE = 0.8
MUON_DECAY = 0.5
MUON_SHRINK = 0.01
ADAM_RATE = 0.5
BETA_ONE = 0.9
BETA_TWO = 0.95
MASKED = -1e30


def owner_slots(owners_row, capacity):
    image_total = owners_row.shape[0]
    ordering = jnp.arange(image_total, dtype=jnp.int32)
    earlier = (owners_row[None, :] == owners_row[:, None]) & (ordering[None, :] < ordering[:, None])
    same_before = jnp.sum(earlier.astype(jnp.int32), axis=1)
    return owners_row * capacity + same_before


def exchange(value, axis, mask):
    count = lax.axis_size(axis)
    return lax.ppermute(value, axis, [(index, index ^ mask) for index in range(count)])


def swap(value, axis, bit):
    return exchange(value, axis, 1 << bit)


def step(value, axis, bit):
    return value, axis, (1 << bit,)


def bit_of(axis, bit):
    return (lax.axis_index(axis) >> bit) & 1


def bits_in(axis):
    return (lax.axis_size(axis) - 1).bit_length()


def tie(values, earlier):
    return lax.optimization_barrier((values, earlier))


def add_low(first, second):
    return (first.astype(jnp.float32) + second.astype(jnp.float32)).astype(jnp.bfloat16)


def halves(value, axis, bit, dim=0):
    mine = bit_of(axis, bit)
    shape = value.shape
    pairs = value.reshape(*shape[:dim], 2, shape[dim] // 2, *shape[dim + 1 :])
    keep = lax.dynamic_index_in_dim(pairs, mine, dim, keepdims=False)
    send = lax.dynamic_index_in_dim(pairs, 1 - mine, dim, keepdims=False)
    return keep, send


def joined(value, other, axis, bit, dim=0):
    mine = bit_of(axis, bit)
    low_half = jnp.where(mine == 0, value, other)
    high_half = jnp.where(mine == 0, other, value)
    return jnp.concatenate([low_half, high_half], axis=dim)


class Chain:
    def __init__(self, steps):
        self.steps = steps
        self.result = None
        self.advance(None)

    def advance(self, came):
        try:
            self.sent, axis, masks, *self.held = self.steps.send(came)
            self.pending = tuple(exchange(self.sent, axis, mask) for mask in masks)
        except StopIteration as stop:
            self.sent = self.pending = None
            self.result = stop.value


def meet(*chains, also=()):
    live = [chain for chain in chains if chain.pending is not None]
    cames, also = lax.optimization_barrier((tuple(chain.pending for chain in live), also))
    for chain, came in zip(live, cames):
        chain.advance(came if len(came) > 1 else came[0])
    return also


def finish(*chains):
    while any(chain.pending is not None for chain in chains):
        meet(*chains)


def rest_of_dp(value, dim, split):
    value = yield from rest_summed(value, dim, split)
    other = yield step(value, "dp", 0)
    return value, other


def rest_summed(value, dim, split):
    first = 1
    split = split and bits_in("dp") > 2
    if split:
        keep, send = halves(value, "dp", 1, dim)
        value = add_low(keep, (yield step(send, "dp", 1)))
        first = 2
    for bit in range(first, bits_in("dp")):
        value = add_low(value, (yield step(value, "dp", bit)))
    if split:
        value = joined(value, (yield step(value, "dp", 1)), "dp", 1, dim)
    return value


def sum_pair(value):
    value = yield from rest_summed(value, 1, True)
    role = bit_of("dp", 0)
    mine = lax.dynamic_index_in_dim(value, role, 0, keepdims=False)
    theirs = lax.dynamic_index_in_dim(value, 1 - role, 0, keepdims=False)
    first = yield (*step(theirs, "dp", 0), "first")
    held = (mine, first)
    second = yield (*step(tie(mine, first)[0], "dp", 0), held)
    return value, first, second


def sum_up(kept, sent):
    value = add_low(kept, (yield step(sent, "ns", 1)))
    keep, send = halves(value, "dp", 0)
    return add_low(keep, (yield step(send, "dp", 0)))


def sum_down(kept, sent):
    keep, send = halves(jnp.stack([kept, sent]), "dp", 0, 1)
    value = add_low(keep, (yield step(send, "dp", 0)))
    return add_low(value[0], (yield step(value[1], "ns", 1)))


def sum_blocks(value, split):
    for bit in range(bits_in("ns")):
        mine = bit_of("ns", bit)
        pairs = value.reshape(value.shape[0] // 2, 2, *value.shape[1:])
        keep = lax.dynamic_index_in_dim(pairs, mine, 1, keepdims=False)
        send = lax.dynamic_index_in_dim(pairs, 1 - mine, 1, keepdims=False)
        value = add_low(keep, (yield step(send, "ns", bit)))
    keep, send = halves(value[0], "dp", 0)
    value = add_low(keep, (yield step(send, "dp", 0)))
    return (yield from rest_of_dp(value, 0, split))


def sum_vector(value):
    for axis in ("ns", "dp"):
        for bit in range(0, bits_in(axis), 2):
            masks = [1 << bit]
            if bit + 1 < bits_in(axis):
                masks += [2 << bit, 3 << bit]
            came = yield value, axis, masks
            if len(masks) == 1:
                value = value + came
            else:
                value = (value + came[0]) + (came[1] + came[2])
    return value


def sum_gram(gram):
    gram = gram + (yield step(gram, "ns", 0))
    keep, _ = halves(gram, "ns", 0)
    for bit in range(1, bits_in("ns")):
        keep = keep + (yield step(keep, "ns", bit))
    other = yield step(keep, "ns", 0)
    return (keep[None], 0), (other[None], 0)


def by_distance(table):
    place = lax.axis_index("ns")
    return [
        lax.dynamic_index_in_dim(table, place ^ distance, 0, keepdims=True)
        for distance in range(table.shape[0])
    ]


def dot32(first, second):
    return jnp.dot(first, second, preferred_element_type=jnp.float32)


LOW = jnp.bfloat16
F32 = jnp.float32
HEADS = D // HD
BIG = 576
SMALL = 64
TILE = 256
MIB = 1024 * 1024
COST_SCALE = 1e9


def mm(first, second, first_dim=1, second_dim=0):
    return lax.dot_general(
        first,
        second,
        (((first_dim,), (second_dim,)), ((), ())),
        preferred_element_type=F32,
    )


def split_value(value):
    high = value.astype(LOW)
    return high, (value - high.astype(F32)).astype(LOW)


def normalise(values):
    row_mean = jnp.mean(values, axis=-1, keepdims=True)
    centred = values - row_mean
    scale = lax.rsqrt(jnp.mean(centred * centred, axis=-1, keepdims=True) + 1e-06)
    return centred * scale, scale


def norm_back(unit, scale, unit_grad):
    return scale * (
        unit_grad
        - jnp.mean(unit_grad, axis=-1, keepdims=True)
        - unit * jnp.mean(unit_grad * unit, axis=-1, keepdims=True)
    )


def column_sum(values):
    return jnp.sum(values, axis=0, keepdims=True)


def params(mebibytes):
    return pltpu.CompilerParams(vmem_limit_bytes=mebibytes * MIB)


def cost(micros, nbytes):
    return pl.CostEstimate(flops=int(micros * COST_SCALE), bytes_accessed=int(nbytes * COST_SCALE * 1e-9), transcendentals=0)


def whole(shape):
    return pl.BlockSpec(shape, lambda *_: (0,) * len(shape))


def once(shape):
    return pl.BlockSpec(shape, lambda *_: (0,) * len(shape), pipeline_mode=pl.Buffered(1))


def rows_of(width, tile=TILE):
    return pl.BlockSpec((tile, width), lambda i, *_: (i, 0))


def lanes_of(height, tile=TILE):
    return pl.BlockSpec((height, tile), lambda i, *_: (0, i))


STARTS = {}
WIDTHS = dict(gain_one=D, bias_one=D, bias_qkv=3 * D, gain_query=HD, bias_query=HD, gain_key=HD,
              bias_out=D, gain_two=D, bias_two=D, bias_up=FF, bias_down=D)
for part_name, part_width in WIDTHS.items():
    STARTS[part_name] = sum(WIDTHS[other] for other in STARTS)


def vector_row(ref, name):
    start = STARTS[name]
    return ref[:, start : start + WIDTHS[name]]


def to_column(row):
    return jnp.broadcast_to(row, (8, row.shape[1])).T[:, :1]


def to_row(column):
    return jnp.broadcast_to(column, (column.shape[0], 128)).T[:1]


def qkv_part(block):
    return pl.BlockSpec(
        (block.shape[0] - out_rows(block), D), lambda *_: (0, 0), pipeline_mode=pl.Buffered(1)
    )


def out_part(block):
    return pl.BlockSpec((out_rows(block), D), lambda *_: (3, 0), pipeline_mode=pl.Buffered(1))


def out_rows(block):
    return block.shape[0] // 4


def place_blocks(place_ref, refs, store):
    rows = refs[0].shape[0]
    for distance, ref in enumerate(refs):
        start = pl.multiple_of((place_ref[0] ^ distance) * rows, rows)
        store[pl.ds(start, rows), :] = ref[...]


def shape_of(shape, dtype):
    return jax.ShapeDtypeStruct(shape, dtype)


def project_kernel(place_ref, x_ref, w0, w1, w2, w3, vec_ref,
                   h_ref, qkv_ref, unit_ref, scale_ref, w_s, col_s):
    @pl.when(pl.program_id(0) == 0)
    def _():
        place_blocks(place_ref, (w0, w1, w2, w3), w_s)
        start = STARTS["bias_qkv"]
        row = vec_ref[:, start : start + 3 * D + 256]
        col_s[...] = to_column(row)

    unit, _ = normalise(x_ref[...].astype(F32))
    h_low = (unit * vector_row(vec_ref, "gain_one") + vector_row(vec_ref, "bias_one")).astype(LOW)
    h_ref[...] = h_low
    gain_q = col_s[pl.ds(3 * D, HD), :]
    bias_q = col_s[pl.ds(3 * D + HD, HD), :]
    gain_k = col_s[pl.ds(3 * D + 2 * HD, HD), :]
    for part in range(3):
        rows = pl.ds(part * D, D)
        value = mm(w_s[rows, :], h_low, 1, 1) + col_s[rows, :]
        if part == 2:
            qkv_ref[2] = value.astype(LOW)
            continue
        heads = value.reshape(HEADS, HD, value.shape[1])
        centred = heads - jnp.mean(heads, axis=1, keepdims=True)
        scale = lax.rsqrt(jnp.mean(centred * centred, axis=1, keepdims=True) + 1e-06)
        unit_heads = centred * scale
        scale_ref[part] = scale
        unit_ref[part] = unit_heads.reshape(D, -1).astype(LOW)
        if part == 0:
            result = unit_heads * gain_q[None] + bias_q[None]
            result = result.astype(LOW) * LOW(0.125)
        else:
            result = (unit_heads * gain_k[None]).astype(LOW)
        qkv_ref[part] = result.reshape(D, -1)


def project(place, patches, w_blocks, vectors):
    slots = patches.shape[0]
    return pl.pallas_call(
        project_kernel,
        grid_spec=pltpu.PrefetchScalarGridSpec(
            num_scalar_prefetch=1,
            grid=(slots // TILE,),
            in_specs=[rows_of(D)] + [qkv_part(w_blocks[0])] * 4 + [once(vectors.shape)],
            out_specs=[rows_of(D),
                       pl.BlockSpec((3, D, TILE), lambda i, p: (0, 0, i)),
                       pl.BlockSpec((2, D, TILE), lambda i, p: (0, 0, i)),
                       pl.BlockSpec((2, HEADS, 1, TILE), lambda i, p: (0, 0, 0, i))],
            scratch_shapes=[pltpu.VMEM((3 * D, D), LOW), pltpu.VMEM((3 * D + 256, 1), F32)],
        ),
        out_shape=[shape_of((slots, D), LOW), shape_of((3, D, slots), LOW),
                   shape_of((2, D, slots), LOW), shape_of((2, HEADS, 1, slots), F32)],
        compiler_params=params(24),
        cost_estimate=cost(10, 16e6),
        name="project",
    )(place, patches, *w_blocks, vectors)


def used_slots(counts_ref):
    total = counts_ref[0]
    for k in range(1, counts_ref.shape[0]):
        total = total + counts_ref[k]
    return total


def pair_mask(tile_start, used, has_big):
    same = (has_big & (tile_start + SMALL < BIG)) | (tile_start >= used)
    row_half = lax.broadcasted_iota(jnp.int32, (128, 128), 0) // SMALL
    column_half = lax.broadcasted_iota(jnp.int32, (128, 128), 1) // SMALL
    return (row_half == column_half) | same


def soft_columns(scores):
    peak = jnp.max(scores, axis=0, keepdims=True)
    exponent = jnp.exp(scores - peak)
    total = jnp.sum(exponent, axis=0, keepdims=True)
    return exponent.astype(LOW), total, peak + jnp.log(total)


def pair_mask_row(slots, used, has_big):
    row_half = lax.broadcasted_iota(jnp.int32, (128, slots), 0) // SMALL
    slot = lax.broadcasted_iota(jnp.int32, (128, slots), 1)
    column_half = slot // SMALL % 2
    start = slot // 128 * 128
    same = (has_big & (start + SMALL < BIG)) | (start >= used)
    return (row_half == column_half) | same


def attend_kernel(group, counts_ref, qkv_ref, out_ref, log_ref):
    used = used_slots(counts_ref)
    has_big = counts_ref[0] == BIG
    slots = out_ref.shape[1]
    heads = [pl.ds(index * HD, HD) for index in range(group)]

    def narrow(first, last):
        tiles = [slice(start, start + 128) for start in range(first, last, 128)]
        mask = pair_mask_row(slots, used, has_big)[:, first:last]
        span = slice(first, last)
        all_scores = []
        for rows in heads:
            all_scores.append(jnp.concatenate(
                [mm(qkv_ref[1, rows, tile], qkv_ref[0, rows, tile], 0, 0) for tile in tiles], axis=1
            ))
        for index, rows in enumerate(heads):
            scores = jnp.where(mask, all_scores[index], MASKED)
            weights, total, log_total = soft_columns(scores)
            result = jnp.concatenate(
                [mm(qkv_ref[2, rows, tile], weights[:, tile.start - first : tile.stop - first])
                 for tile in tiles], axis=1
            )
            out_ref[rows, span] = (result / total).astype(LOW)
            log_ref[index, :, span] = log_total

    @pl.when(jnp.logical_not(has_big))
    def _():
        narrow(0, 512)

    narrow(512, slots)

    @pl.when(has_big)
    def _():
        for start, width in ((0, 256), (256, 256), (512, 128)):
            span = pl.ds(start, width)
            all_scores = [
                mm(qkv_ref[1, rows, 0:640], qkv_ref[0, rows, span], 0, 0)[:BIG] for rows in heads
            ]
            for index, rows in enumerate(heads):
                weights, total, log_total = soft_columns(all_scores[index])
                weights = jnp.concatenate([weights, jnp.zeros((640 - BIG, width), LOW)], axis=0)
                result = mm(qkv_ref[2, rows, 0:640], weights) / total
                if width == 128:
                    lane = lax.broadcasted_iota(jnp.int32, (1, width), 1)
                    inside = lane < BIG - start
                    result = jnp.where(inside, result, out_ref[rows, span].astype(F32))
                    log_total = jnp.where(inside, log_total, log_ref[index, :, span])
                out_ref[rows, span] = result.astype(LOW)
                log_ref[index, :, span] = log_total

    for first in range(0, slots - 128, 256):

        @pl.when((used >= first) & (used < first + 256) & (used < slots - 128))
        def _():
            def columns(chunk, carry):
                span = pl.ds(pl.multiple_of(chunk * 256, 256), 256)
                slot = chunk * 256 + lax.broadcasted_iota(jnp.int32, (1, 256), 1)
                inside = slot >= used
                key_slot = first + lax.broadcasted_iota(jnp.int32, (256, 256), 0)
                all_scores = [
                    mm(qkv_ref[1, rows, first:slots], qkv_ref[0, rows, span], 0, 0)
                    for rows in heads
                ]
                for index, rows in enumerate(heads):
                    scores = all_scores[index]
                    top = jnp.where(key_slot >= used, scores[:256], MASKED)
                    if slots - first > 256:
                        top = jnp.concatenate([top, scores[256:]], axis=0)
                    weights, total, log_total = soft_columns(top)
                    result = mm(qkv_ref[2, rows, first:slots], weights) / total
                    old = out_ref[rows, span].astype(F32)
                    out_ref[rows, span] = jnp.where(inside, result, old).astype(LOW)
                    log_ref[index, :, span] = jnp.where(inside, log_total, log_ref[index, :, span])
                return carry

            lax.fori_loop(first // 256, slots // 256, columns, 0)


def attend(counts, qkv, group=2):
    slots = qkv.shape[2]
    return pl.pallas_call(
        functools.partial(attend_kernel, group),
        grid_spec=pltpu.PrefetchScalarGridSpec(
            num_scalar_prefetch=1,
            grid=(HEADS // group,),
            in_specs=[pl.BlockSpec((3, group * HD, slots), lambda h, c: (0, h, 0))],
            out_specs=[pl.BlockSpec((group * HD, slots), lambda h, c: (h, 0)),
                       pl.BlockSpec((group, 1, slots), lambda h, c: (h, 0, 0))],
        ),
        out_shape=[shape_of((D, slots), LOW), shape_of((HEADS, 1, slots), F32)],
        compiler_params=params(16),
        cost_estimate=cost(28, 7000000.0),
        name="attend",
    )(counts, qkv)


def attend_back_kernel(group, counts_ref, qkv_ref, attn_ref, log_ref, grad_ref, unit_ref,
                       scale_ref, vec_ref, _, dqkv_ref, bias_ref, gains_ref, dq_s, dk_s, dv_s):
    used = used_slots(counts_ref)
    has_big = counts_ref[0] == BIG
    slots = attn_ref.shape[1]
    start = STARTS["gain_query"]
    columns = to_column(vec_ref[:, start : start + 256])
    gain_q, gain_k = columns[:HD], columns[2 * HD : 3 * HD]

    @pl.when(pl.program_id(0) == 0)
    def _():
        gains_ref[...] = jnp.zeros_like(gains_ref)

    def head_rows(index):
        return pl.ds(index * HD, HD)

    def delta_of(index, span):
        return column_sum(
            grad_ref[head_rows(index), span].astype(F32)
            * attn_ref[head_rows(index), span].astype(F32)
        )

    def narrow(first, last):
        tiles = [slice(start, start + 128) for start in range(first, last, 128)]
        mask = pair_mask_row(slots, used, has_big)[:, first:last]
        span = slice(first, last)

        def wide(product):
            return jnp.concatenate([product(tile) for tile in tiles], axis=1)

        def inner(tile):
            return slice(tile.start - first, tile.stop - first)

        all_scores, all_grads = [], []
        for index in range(group):
            rows = head_rows(index)
            all_scores.append(wide(
                lambda tile: mm(qkv_ref[1, rows, tile], qkv_ref[0, rows, tile], 0, 0)))
            all_grads.append(wide(
                lambda tile: mm(qkv_ref[2, rows, tile], grad_ref[rows, tile], 0, 0)))
        for index in range(group):
            rows = head_rows(index)
            scores = all_scores[index] - log_ref[index, :, span]
            probs = jnp.exp(jnp.where(mask, scores, MASKED))
            score_low = (probs * (all_grads[index] - delta_of(index, span))).astype(LOW)
            probs_low = probs.astype(LOW)
            dv_s[rows, span] = wide(
                lambda tile: mm(grad_ref[rows, tile], probs_low[:, inner(tile)], 1, 1))
            dk_s[rows, span] = wide(
                lambda tile: mm(qkv_ref[0, rows, tile], score_low[:, inner(tile)], 1, 1))
            dq_s[rows, span] = wide(
                lambda tile: mm(qkv_ref[1, rows, tile], score_low[:, inner(tile)]))

    @pl.when(jnp.logical_not(has_big))
    def _():
        narrow(0, 512)

    @pl.when(used > 512)
    def _():
        narrow(512, slots)

    @pl.when(used <= 512)
    def _():
        for store in (dq_s, dk_s, dv_s):
            store[:, 512:slots] = jnp.zeros((store.shape[0], slots - 512), F32)

    @pl.when(has_big)
    def _():
        wide = pl.ds(0, 640)
        dk = [jnp.zeros((HD, 640), F32)] * group
        dv = [jnp.zeros((HD, 640), F32)] * group
        for start, width in ((0, 256), (256, 256), (512, 128)):
            span = pl.ds(start, width)
            lane = lax.broadcasted_iota(jnp.int32, (1, width), 1)
            all_scores, all_grads = [], []
            for index in range(group):
                rows = head_rows(index)
                all_scores.append(mm(qkv_ref[1, rows, wide], qkv_ref[0, rows, span], 0, 0)[:BIG])
                all_grads.append(mm(qkv_ref[2, rows, wide], grad_ref[rows, span], 0, 0)[:BIG])
            for index in range(group):
                rows = head_rows(index)
                probs = jnp.exp(all_scores[index] - log_ref[index, :, span])
                if width == 128:
                    probs = jnp.where(lane < BIG - start, probs, 0.0)
                score_low = (probs * (all_grads[index] - delta_of(index, span))).astype(LOW)
                blank = jnp.zeros((640 - BIG, width), LOW)
                score_low = jnp.concatenate([score_low, blank], axis=0)
                probs_low = jnp.concatenate([probs.astype(LOW), blank], axis=0)
                dv[index] = dv[index] + mm(grad_ref[rows, span], probs_low, 1, 1)
                dk[index] = dk[index] + mm(qkv_ref[0, rows, span], score_low, 1, 1)
                dq = mm(qkv_ref[1, rows, wide], score_low)
                if width == 128:
                    dq = jnp.where(lane < BIG - start, dq, dq_s[rows, span])
                dq_s[rows, span] = dq
        inside = lax.broadcasted_iota(jnp.int32, (1, 640), 1) < BIG
        for index in range(group):
            rows = head_rows(index)
            dk_s[rows, wide] = jnp.where(inside, dk[index], dk_s[rows, wide])
            dv_s[rows, wide] = jnp.where(inside, dv[index], dv_s[rows, wide])

    sums = [jnp.zeros((HD, 1), F32)] * 3
    biases = [[], [], []]
    for index in range(group):
        rows = head_rows(index)
        for part, store, gain in ((0, dq_s, gain_q), (1, dk_s, gain_k)):
            unit = unit_ref[part, rows, :].astype(F32)
            grad = store[rows, :]
            if part == 0:
                grad = grad * 0.125
                sums[0] = sums[0] + jnp.sum(grad * unit, axis=1, keepdims=True)
                sums[1] = sums[1] + jnp.sum(grad, axis=1, keepdims=True)
            else:
                sums[2] = sums[2] + jnp.sum(grad * unit, axis=1, keepdims=True)
            unit_grad = grad * gain
            result = scale_ref[part, index] * (
                unit_grad
                - jnp.mean(unit_grad, axis=0, keepdims=True)
                - unit * jnp.mean(unit_grad * unit, axis=0, keepdims=True)
            )
            result = result.astype(LOW)
            dqkv_ref[part, rows, :] = result
            biases[part].append(jnp.sum(result.astype(F32), axis=1, keepdims=True))
        result = dv_s[rows, :].astype(LOW)
        dqkv_ref[2, rows, :] = result
        biases[2].append(jnp.sum(result.astype(F32), axis=1, keepdims=True))
    for part in range(3):
        bias_ref[part] = to_row(jnp.concatenate(biases[part], axis=0))
    blank = jnp.zeros((HD, 1), F32)
    gains_ref[:, 0:128] += to_row(jnp.concatenate(sums[:2], axis=0))
    gains_ref[:, 128:256] += to_row(jnp.concatenate([sums[2], blank], axis=0))


def attend_back(counts, qkv, attn, log_total, attn_grad, unit, scale, vectors, earlier, half,
                group=2):
    slots = qkv.shape[2]
    steps = HEADS // group // 2
    first = half * steps
    head_block = pl.BlockSpec((group * HD, slots), lambda h, c: (h + first, 0))
    dqkv_block = pl.BlockSpec((3, group * HD, slots), lambda h, c: (0, h + first, 0))
    held = pl.BlockSpec(memory_space=pl.ANY)
    extra = [vectors if earlier is None else earlier]
    return pl.pallas_call(
        functools.partial(attend_back_kernel, group),
        grid_spec=pltpu.PrefetchScalarGridSpec(
            num_scalar_prefetch=1,
            grid=(steps,),
            in_specs=[dqkv_block,
                      head_block,
                      pl.BlockSpec((group, 1, slots), lambda h, c: (h + first, 0, 0)),
                      head_block,
                      pl.BlockSpec((2, group * HD, slots), lambda h, c: (0, h + first, 0)),
                      pl.BlockSpec((2, group, 1, slots), lambda h, c: (0, h + first, 0, 0)),
                      whole(vectors.shape), held],
            out_specs=[dqkv_block,
                       pl.BlockSpec((3, 1, group * HD), lambda h, c: (0, 0, h)),
                       whole((1, 256))],
            scratch_shapes=[pltpu.VMEM((group * HD, slots), F32)] * 3,
        ),
        out_shape=[shape_of((3, D, slots), LOW), shape_of((3, 1, D // 2), F32),
                   shape_of((1, 256), F32)],
        input_output_aliases={} if earlier is None else {8: 0},
        compiler_params=params(60),
        cost_estimate=cost(2.0, 8e6),
        name="attend_back",
    )(counts, qkv, attn, log_total, attn_grad, unit, scale, vectors, *extra)


def segment_picker(counts_ref, first, width):
    images = counts_ref.shape[0]
    slot = first + lax.broadcasted_iota(jnp.int32, (images, width), 1)
    image = lax.broadcasted_iota(jnp.int32, (images, width), 0)
    start = jnp.int32(0)
    picked = jnp.zeros((images, width), jnp.bool_)
    for k in range(images):
        end = start + counts_ref[k]
        picked = picked | ((image == k) & (slot >= start) & (slot < end))
        start = end
    return picked.astype(F32), start


def image_sizes(counts_ref):
    images = counts_ref.shape[0]
    image = lax.broadcasted_iota(jnp.int32, (images, 1), 0)
    sizes = jnp.zeros((images, 1), F32)
    for k in range(images):
        sizes = jnp.where(image == k, jnp.maximum(counts_ref[k], 1).astype(F32), sizes)
    return sizes


def middle_kernel(counts_ref, place_ref, x_ref, attn_ref, w0, w1, w2, w3, vec_ref, cot_ref,
                  image_ref, x2_ref, h_ref, dy_ref, mix_ref, w_s):
    @pl.when(pl.program_id(0) == 0)
    def _():
        place_blocks(place_ref, (w0, w1, w2, w3), w_s)

    x2 = x_ref[...].astype(F32) + mm(attn_ref[...], w_s[...], 0, 1) + vector_row(vec_ref, "bias_out")
    x2_ref[...] = x2
    unit, _ = normalise(x2)
    h_ref[...] = (
        unit * vector_row(vec_ref, "gain_two") + vector_row(vec_ref, "bias_two")
    ).astype(LOW)
    tile = x_ref.shape[0]
    first = pl.program_id(0) * tile
    picker, used = segment_picker(counts_ref, first, tile)
    picker = picker.astype(LOW)
    image_grad = image_ref[...].astype(F32) / image_sizes(counts_ref)
    dy = jnp.zeros(x2.shape, F32)
    rest = image_grad
    for _ in range(3):
        high, rest = split_value32(rest)
        dy = dy + mm(picker, high, 0, 0)
    slot = first + lax.broadcasted_iota(jnp.int32, (tile, 1), 0)
    dy = dy + jnp.where(slot < used, cot_ref[...].astype(F32), 0.0)
    dy_ref[...] = dy
    mix_ref[...] = dy.astype(LOW)


def split_value32(value):
    high = value.astype(LOW)
    return high, value - high.astype(F32)


def middle(counts, place, patches, attn, w_blocks, vectors, patch_cot, image_cot):
    slots = patches.shape[0]
    images = counts.shape[0]
    return pl.pallas_call(
        middle_kernel,
        grid_spec=pltpu.PrefetchScalarGridSpec(
            num_scalar_prefetch=2,
            grid=(slots // TILE,),
            in_specs=[rows_of(D), lanes_of(D)] + [out_part(w_blocks[0])] * 4
            + [whole(vectors.shape), rows_of(D), whole((images, D))],
            out_specs=[rows_of(D)] * 4,
            scratch_shapes=[pltpu.VMEM((D, D), LOW)],
        ),
        out_shape=[shape_of((slots, D), F32), shape_of((slots, D), LOW),
                   shape_of((slots, D), F32), shape_of((slots, D), LOW)],
        compiler_params=params(20),
        cost_estimate=cost(9, 20e6),
        name="middle",
    )(counts, place, patches, attn, *w_blocks, vectors, patch_cot, image_cot)


def feed_kernel(distances, start_y, y_in_ref, dh_in_ref, h_ref, mix_ref, up_a, down_a, up_b,
                down_b, bias_ref, vec_ref,
                y_ref, dh_ref, grad_a, grad_b, bias_grad_a, bias_grad_b):
    @pl.when(pl.program_id(0) == 0)
    def _():
        if start_y:
            y_ref[...] = y_in_ref[...] + vector_row(vec_ref, "bias_down")
            dh_ref[...] = jnp.zeros_like(dh_ref)
        else:
            y_ref[...] = y_in_ref[...]
            dh_ref[...] = dh_in_ref[...]

    slots = h_ref.shape[0]
    for distance, up_ref, down_ref, grad_ref, bias_grad_ref in (
        (distances[0], up_a, down_a, grad_a, bias_grad_a),
        (distances[1], up_b, down_b, grad_b, bias_grad_b),
    ):
        up, down = up_ref[...], down_ref[...]
        h, mix = h_ref[...], mix_ref[...]
        u = mm(up, h, 1, 1) + to_column(bias_ref[distance : distance + 1])
        back = mm(down, mix, 1, 1)
        gate = 0.5 * (1.0 + lax.erf(u * (0.5**0.5)))
        slope = gate + u * (jnp.exp(-0.5 * u * u) * ((0.5 / math.pi) ** 0.5))
        hidden = (u * gate).astype(LOW)
        pre = (back * slope).astype(LOW)
        y_ref[...] += mm(hidden, down, 0, 0)
        dh_ref[...] += mm(pre, up, 0, 0)
        grad_up = mm(pre, h)
        grad_down = mm(hidden, mix)
        bias_grad = to_row(jnp.sum(pre.astype(F32), axis=1, keepdims=True))
        grad_ref[0] = grad_up.astype(LOW)
        grad_ref[1] = grad_down.astype(LOW)
        bias_grad_ref[...] = bias_grad


def feed(distances, y, dh2, h2, mix, pair_a, pair_b, bias_table, vectors, block=256):
    slots = y.shape[0]
    units = pair_a.shape[1]
    start_y = dh2 is None
    if start_y:
        dh2 = y
    up = pl.BlockSpec((None, block, D), lambda i: (0, i, 0))
    down = pl.BlockSpec((None, block, D), lambda i: (1, i, 0))
    bias = pl.BlockSpec((1, block), lambda i: (0, i))
    both = pl.BlockSpec((2, block, D), lambda i: (0, i, 0))
    dh_spec = pl.BlockSpec((8, D), lambda i: (0, 0)) if start_y else once((slots, D))
    return pl.pallas_call(
        functools.partial(feed_kernel, distances, start_y),
        grid=(units // block,),
        in_specs=[once((slots, D)), dh_spec, once((slots, D)), once((slots, D)),
                  up, down, up, down, pl.BlockSpec((bias_table.shape[0], block), lambda i: (0, i)),
                  whole(vectors.shape)],
        out_specs=[once((slots, D)), once((slots, D)), both, both, bias, bias],
        out_shape=[shape_of((slots, D), F32), shape_of((slots, D), F32),
                   shape_of((2, units, D), LOW), shape_of((2, units, D), LOW),
                   shape_of((1, units), F32), shape_of((1, units), F32)],
        compiler_params=params(26),
        cost_estimate=cost(24, 25e6),
        name="feed",
    )(y, dh2, h2, mix, pair_a, pair_a, pair_b, pair_b, bias_table, vectors)


def after_kernel(counts_ref, place_ref, y_ref, x2_ref, dh_ref, dy_ref, attn_ref, w0, w1, w2, w3,
                 vec_ref, out_ref, pooled_ref, dx2_ref, dattn_ref, grad_out_ref, sums_ref,
                 pool_s, grad_s, w_s):
    step = pl.program_id(0)

    @pl.when(step == 0)
    def _():
        pool_s[...] = jnp.zeros_like(pool_s)
        grad_s[...] = jnp.zeros_like(grad_s)
        sums_ref[...] = jnp.zeros_like(sums_ref)
        place_blocks(place_ref, (w0, w1, w2, w3), w_s)

    y = y_ref[...]
    tile = y.shape[0]
    out_ref[...] = y.astype(LOW)
    picker, _ = segment_picker(counts_ref, step * tile, tile)
    picker = picker.astype(LOW)
    rest = y
    pooled = pool_s[...]
    for _ in range(3):
        high, rest = split_value32(rest)
        pooled = pooled + mm(picker, high)
    pool_s[...] = pooled
    pooled_ref[...] = (pooled / image_sizes(counts_ref)).astype(LOW)
    unit, scale = normalise(x2_ref[...])
    dh = dh_ref[...]
    sums_ref[0:1] += column_sum(dh * unit)
    sums_ref[1:2] += column_sum(dh)
    dy = dy_ref[...]
    sums_ref[3:4] += column_sum(dy.astype(LOW).astype(F32))
    dx2 = dy + norm_back(unit, scale, dh * vector_row(vec_ref, "gain_two"))
    dx2_ref[...] = dx2
    da = dx2.astype(LOW)
    sums_ref[2:3] += column_sum(da.astype(F32))
    dattn_ref[...] = mm(w_s[...], da, 0, 1).astype(LOW)
    grad = grad_s[...] + mm(da, attn_ref[...], 0, 1)
    grad_s[...] = grad
    grad_out_ref[...] = grad.astype(LOW)


def after(counts, place, y, x2, dh2, dy, attn, w_blocks, vectors):
    slots = y.shape[0]
    images = counts.shape[0]
    return pl.pallas_call(
        after_kernel,
        grid_spec=pltpu.PrefetchScalarGridSpec(
            num_scalar_prefetch=2,
            grid=(slots // TILE,),
            in_specs=[rows_of(D), rows_of(D), rows_of(D), rows_of(D), lanes_of(D)]
            + [out_part(w_blocks[0])] * 4 + [whole(vectors.shape)],
            out_specs=[rows_of(D), whole((images, D)), rows_of(D), lanes_of(D), whole((D, D)),
                       whole((8, D))],
            scratch_shapes=[pltpu.VMEM((images, D), F32), pltpu.VMEM((D, D), F32),
                            pltpu.VMEM((D, D), LOW)],
        ),
        out_shape=[shape_of((slots, D), LOW), shape_of((images, D), LOW),
                   shape_of((slots, D), F32), shape_of((D, slots), LOW), shape_of((D, D), LOW),
                   shape_of((8, D), F32)],
        compiler_params=params(60),
        cost_estimate=cost(4.0, 25e6),
        name="after",
    )(counts, place, y, x2, dh2, dy, attn, *w_blocks, vectors)


def first_back_kernel(place_ref, x_ref, dqkv_ref, w0, w1, w2, w3, vec_ref, dx2_ref,
                      out_ref, sums_ref, w_s):
    @pl.when(pl.program_id(0) == 0)
    def _():
        sums_ref[...] = jnp.zeros_like(sums_ref)
        place_blocks(place_ref, (w0, w1, w2, w3), w_s)

    dh = mm(dqkv_ref[...], w_s[...], 0, 0)
    unit, scale = normalise(x_ref[...].astype(F32))
    sums_ref[0:1] += column_sum(dh * unit)
    sums_ref[1:2] += column_sum(dh)
    out_ref[...] = dx2_ref[...] + norm_back(unit, scale, dh * vector_row(vec_ref, "gain_one"))


def first_back(place, patches, dqkv, w_blocks, vectors, dx2):
    slots = patches.shape[0]
    return pl.pallas_call(
        first_back_kernel,
        grid_spec=pltpu.PrefetchScalarGridSpec(
            num_scalar_prefetch=1,
            grid=(slots // TILE,),
            in_specs=[rows_of(D), lanes_of(3 * D)] + [qkv_part(w_blocks[0])] * 4
            + [whole(vectors.shape), rows_of(D)],
            out_specs=[rows_of(D), whole((8, D))],
            scratch_shapes=[pltpu.VMEM((3 * D, D), LOW)],
        ),
        out_shape=[shape_of((slots, D), F32), shape_of((8, D), F32)],
        compiler_params=params(22),
        cost_estimate=cost(2.0, 17e6),
        name="first_back",
    )(place, patches, dqkv, *w_blocks, vectors, dx2)


SIDE = 256
GRID_BLOCKS = [(i, j) for i in range(D // SIDE) for j in range(i, D // SIDE)]


def moment_kernel(half_ref, own_ref, other_ref, mom_ref, grad_ref, moment_ref, gram_ref):
    rows = own_ref.shape[0]
    for ref, place in ((own_ref, half_ref[0]), (other_ref, 1 - half_ref[0])):
        span = pl.ds(pl.multiple_of(place * rows, rows), rows)
        grad = ref[...].astype(F32)
        grad_ref[span, :] = grad
        moment_ref[span, :] = MUON_DECAY * mom_ref[span, :] + grad
    moment_low = moment_ref[...].astype(LOW)
    for index, (i, j) in enumerate(GRID_BLOCKS):
        gram_ref[index] = mm(
            moment_low[:, i * SIDE : (i + 1) * SIDE], moment_low[:, j * SIDE : (j + 1) * SIDE], 0, 0
        )


def role_kernel(half_ref, own_ref, other_ref, mom_ref, low_ref, gram_ref):
    rows = own_ref.shape[0]
    for ref, place in ((own_ref, half_ref[0]), (other_ref, 1 - half_ref[0])):
        span = pl.ds(pl.multiple_of(place * rows, rows), rows)
        low_ref[span, :] = (MUON_DECAY * mom_ref[span, :] + ref[...].astype(F32)).astype(LOW)
    moment_low = low_ref[...]
    for index, (i, j) in enumerate(GRID_BLOCKS):
        gram_ref[index] = mm(
            moment_low[:, i * SIDE : (i + 1) * SIDE], moment_low[:, j * SIDE : (j + 1) * SIDE], 0, 0
        )


def role_gram(half, own, other, mom):
    rows = mom.shape[0]
    blocks = len(GRID_BLOCKS)
    out_shape = [shape_of((rows, D), LOW), shape_of((blocks, SIDE, SIDE), F32)]
    return pl.pallas_call(
        role_kernel,
        grid=(1,),
        in_specs=[pl.BlockSpec(memory_space=pltpu.SMEM), once(own.shape), once(other.shape),
                  once((rows, D))],
        out_specs=[once(leaf.shape) for leaf in out_shape],
        out_shape=out_shape,
        compiler_params=params(16),
        cost_estimate=cost(0.5, rows * D * 8 + blocks * SIDE * SIDE * 4),
        name="role_gram",
    )(half, own, other, mom)


def record_kernel(kind, half_ref, own_ref, first_ref, second_ref, mom_ref, grad_ref, moment_ref):
    rows = own_ref.shape[0]

    def put(ref, place):
        span = pl.ds(pl.multiple_of(place * rows, rows), rows)
        grad = ref[...].astype(F32)
        grad_ref[span, :] = grad
        moment_ref[span, :] = MUON_DECAY * mom_ref[span, :] + grad

    put(own_ref, half_ref[0])

    @pl.when(half_ref[0] == kind)
    def _():
        put(first_ref, 1 - half_ref[0])

    @pl.when(half_ref[0] != kind)
    def _():
        put(second_ref, 1 - half_ref[0])


def record(kind, half, own, first, second, mom):
    rows = mom.shape[0]
    out_shape = [shape_of((rows, D), F32), shape_of((rows, D), F32)]
    return pl.pallas_call(
        functools.partial(record_kernel, kind),
        grid=(1,),
        in_specs=[pl.BlockSpec(memory_space=pltpu.SMEM), one_of(own, kind), once(first.shape),
                  once(second.shape), once((rows, D))],
        out_specs=[once(leaf.shape) for leaf in out_shape],
        out_shape=out_shape,
        compiler_params=params(16),
        cost_estimate=cost(0.5, rows * D * 14),
        name="record",
    )(half, own, first, second, mom)


def one_of(stack, index):
    return pl.BlockSpec(
        (None,) + stack.shape[1:],
        lambda i: (index,) + (0,) * (stack.ndim - 1),
        pipeline_mode=pl.Buffered(1),
    )


def moment_and_gram(half, own, other, mom):
    rows = mom.shape[0]
    blocks = len(GRID_BLOCKS)
    out_shape = [shape_of((rows, D), F32), shape_of((rows, D), F32),
                 shape_of((blocks, SIDE, SIDE), F32)]
    (own, own_index), (other, other_index) = own, other
    return pl.pallas_call(
        moment_kernel,
        grid=(1,),
        in_specs=[pl.BlockSpec(memory_space=pltpu.SMEM), one_of(own, own_index),
                  one_of(other, other_index), once((rows, D))],
        out_specs=[once(leaf.shape) for leaf in out_shape],
        out_shape=out_shape,
        compiler_params=params(16),
        cost_estimate=cost(0.5, rows * D * 14 + blocks * SIDE * SIDE * 4),
        name="moment",
    )(half, own, other, mom)


def muon_kernel(step_scale, half_ref, own_ref, other_ref, moment_ref, *refs):
    *refs, gram_s, low_s, rest_s, mix_s, rows_s, gram_ref = refs
    count = own_ref.shape[0]
    for index in range(count):
        gram_ref[half_ref[0] * count + index] = own_ref[index]
        gram_ref[(1 - half_ref[0]) * count + index] = other_ref[index]
    spans = [slice(i * SIDE, (i + 1) * SIDE) for i in range(D // SIDE)]

    def put(refs, i, j, blocks):
        for ref, block in zip(refs, blocks):
            ref[spans[i], spans[j]] = block
            if i != j:
                ref[spans[j], spans[i]] = block.T

    total = jnp.zeros((1, 1), F32)
    row = lax.broadcasted_iota(jnp.int32, (SIDE, SIDE), 0)
    column = lax.broadcasted_iota(jnp.int32, (SIDE, SIDE), 1)
    for index, (i, j) in enumerate(GRID_BLOCKS):
        if i == j:
            kept = jnp.where(row == column, gram_ref[index], 0.0)
            total = total + jnp.sum(jnp.sum(kept, axis=0, keepdims=True), axis=1, keepdims=True)
    scale = 1.0 / (jnp.sqrt(total) + 1e-07)
    square = scale * scale
    for index, (i, j) in enumerate(GRID_BLOCKS):
        block = gram_ref[index] * square
        put((gram_s,), i, j, (block,))
        put((low_s, rest_s), i, j, split_value(block))
    rows_s[...] = moment_ref[...].astype(LOW)
    for iteration in range(ITERS):
        careful = iteration == 0
        for i, j in GRID_BLOCKS:
            squared = mm(low_s[spans[i], :], low_s[:, spans[j]])
            put((mix_s,), i, j, ((NS_B * gram_s[spans[i], spans[j]] + NS_C * squared).astype(LOW),))
        if iteration == ITERS - 1:
            break
        middle_blocks = []
        for i in range(D // SIDE):
            for j in range(0 if careful else i, D // SIDE):
                block = NS_A * gram_s[spans[i], spans[j]] + mm(low_s[spans[i], :], mix_s[:, spans[j]])
                if careful:
                    block = block + mm(rest_s[spans[i], :], mix_s[:, spans[j]])
                middle_blocks.append((i, j, block))
        for i, j, block in middle_blocks:
            gram_s[spans[i], spans[j]] = block
            if careful:
                low_s[spans[i], spans[j]], rest_s[spans[i], spans[j]] = split_value(block)
            else:
                put((low_s,), i, j, (block.astype(LOW),))
        renewed = NS_A * rows_s[...].astype(F32) + mm(rows_s[...], mix_s[...])
        if careful:
            renewed = renewed * scale
        rows_s[...] = renewed.astype(LOW)
        gram_blocks = []
        for i, j in GRID_BLOCKS:
            block = NS_A * gram_s[spans[i], spans[j]] + mm(mix_s[spans[i], :], low_s[:, spans[j]])
            if careful:
                block = block + mm(mix_s[spans[i], :], rest_s[:, spans[j]])
            gram_blocks.append((i, j, block))
        for i, j, block in gram_blocks:
            gram_s[spans[i], spans[j]] = block
            put((low_s,), i, j, (block.astype(LOW),))
    renewed = NS_A * rows_s[...].astype(F32) + mm(rows_s[...], mix_s[...])
    if step_scale is None:
        (ortho_ref,) = refs
        ortho_ref[...] = renewed.astype(LOW)
        return
    master_ref, new_ref, copy_ref = refs
    new = master_ref[...] * (1.0 - MUON_RATE * MUON_SHRINK) - step_scale * renewed
    new_ref[...] = new
    copy_ref[...] = new.astype(LOW)


def muon(half, own, other, moment, master=None, step_scale=None):
    rows = moment.shape[0]
    (own, own_index), (other, other_index) = own, other
    out_shape = [shape_of((rows, D), F32), shape_of((rows, D), LOW)]
    masters = [master]
    if master is None:
        out_shape, masters = out_shape[1:], []
    return pl.pallas_call(
        functools.partial(muon_kernel, step_scale),
        grid=(1,),
        in_specs=[pl.BlockSpec(memory_space=pltpu.SMEM), one_of(own, own_index),
                  one_of(other, other_index), once((rows, D))] + [once((rows, D))] * len(masters),
        out_specs=[once(leaf.shape) for leaf in out_shape],
        out_shape=out_shape,
        scratch_shapes=[pltpu.VMEM((D, D), F32), pltpu.VMEM((D, D), LOW), pltpu.VMEM((D, D), LOW),
                        pltpu.VMEM((D, D), LOW), pltpu.VMEM((rows, D), LOW),
                        pltpu.VMEM((len(GRID_BLOCKS), SIDE, SIDE), F32)],
        compiler_params=params(30),
        cost_estimate=cost(1.0, rows * D * 14),
        name="muon",
    )(half, own, other, moment, *masters)


def per_device(
    patches,
    counts,
    owners,
    pooled_cot,
    patch_cot,
    master_qkv,
    master_out,
    master_up,
    master_down,
    mom_qkv,
    mom_out,
    mom_up,
    mom_down,
    vectors,
    vec_first,
    vec_second,
):
    dp_count = lax.axis_size("dp")
    ns_count = lax.axis_size("ns")
    slot_count = patches.shape[0]
    image_total = counts.shape[1]
    capacity = pooled_cot.shape[0] // dp_count
    low = jnp.bfloat16
    place = lax.axis_index("ns").astype(jnp.int32).reshape(1)
    half_dp = bit_of("dp", 0).astype(jnp.int32).reshape(1)
    half_ns = bit_of("ns", 0).astype(jnp.int32).reshape(1)

    own_first = jnp.concatenate([master_qkv, master_out]).astype(low)
    w_first = (own_first, swap(own_first, "ns", 0), swap(own_first, "ns", 1))
    row = vectors.reshape(1, -1)
    bias_start = STARTS["bias_up"]
    bias_table = jnp.concatenate(
        by_distance(vectors[bias_start : bias_start + FF].reshape(ns_count, -1)), axis=0
    )
    returned = lax.all_to_all(
        pooled_cot.reshape(dp_count, capacity, D), "dp", split_axis=0, concat_axis=0, tiled=True
    ).reshape(dp_count * capacity, D)
    targets = owner_slots(owners[0], capacity)
    routing = (
        jnp.arange(dp_count * capacity, dtype=jnp.int32)[:, None] == targets[None, :]
    ).astype(low)
    image_cot = dot32(routing.T, returned).astype(low)
    sizes = counts[0]
    own_pair = jnp.stack([master_up, master_down]).astype(low)
    role_mom = jnp.where(bit_of("dp", 0) == 0, mom_up, mom_down)
    far_first, (own_pair, image_cot, role_mom) = tie(w_first[2], (own_pair, image_cot, role_mom))
    w_first = (w_first[0], w_first[1], far_first, swap(far_first, "ns", 0))
    own_pair, _ = tie(own_pair, far_first)
    near_pair, next_pair, far_pair = own_pair, swap(own_pair, "ns", 0), swap(own_pair, "ns", 1)
    first_low, qkv, unit, scale = project(place, patches, w_first, row)
    attn, log_total = attend(sizes, qkv)
    x2, second_low, row_grad, mixed_low = middle(
        sizes, place, patches, attn, w_first, row, patch_cot, image_cot
    )
    y, second_grad, grad_1, grad_0, bias_1, bias_0 = feed(
        (1, 0), x2, None, second_low, mixed_low, next_pair, near_pair, bias_table, row
    )
    came_1 = swap(grad_1, "ns", 0)
    y, far_pair = tie(y, far_pair)
    far_next_pair = swap(far_pair, "ns", 0)
    y, second_grad, grad_3, grad_2, bias_3, bias_2 = feed(
        (3, 2), y, second_grad, second_low, mixed_low, far_next_pair, far_pair, bias_table, row
    )
    came_3 = swap(grad_3, "ns", 0)
    kept = add_low(grad_0, came_1)
    came_3, kept = tie(came_3, kept)
    sent = add_low(grad_2, came_3)
    up, down = Chain(sum_up(kept[0], sent[0])), Chain(sum_down(kept[1], sent[1]))
    y, (sent, kept) = tie(y, (sent, kept))
    out_patches, pooled, middle_grad, attn_grad, grad_out, sums_two = after(
        sizes, place, y, x2, second_grad, row_grad, attn, w_first, row
    )
    out = Chain(sum_blocks(grad_out.reshape(ns_count, -1, D), False))
    dqkv, bias_a, gains_a = attend_back(
        sizes, qkv, attn, log_total, attn_grad, unit, scale, row, None, 0
    )
    dqkv = meet(up, down, out, also=dqkv)
    dqkv, bias_b, gains_b = attend_back(
        sizes, qkv, attn, log_total, attn_grad, unit, scale, row, dqkv, 1
    )
    outgoing = dot32(routing, pooled).astype(low).reshape(dp_count, capacity, D)
    dqkv = meet(up, down, out, also=dqkv.reshape(3 * D, slot_count))
    pair = Chain(sum_pair(jnp.stack([up.result, down.result])))
    grad_qkv = dot32(dqkv, first_low).astype(low)
    three = Chain(sum_blocks(grad_qkv.reshape(ns_count, -1, D), True))
    meet(three)
    middle_grad = meet(pair, out, also=middle_grad)
    patch_grad, sums_one = first_back(place, patches, dqkv, w_first, row, middle_grad)
    sums_one, patch_grad = meet(three, also=(sums_one, patch_grad))
    gains = gains_a + gains_b
    up_bias_grad = by_distance(jnp.concatenate([bias_0, bias_1, bias_2, bias_3], axis=0))
    vector_local = jnp.concatenate(
        [
            sums_one[0:1],
            sums_one[1:2],
            jnp.concatenate([bias_a, bias_b], axis=2).reshape(1, 3 * D),
            gains[:, : 3 * HD],
            sums_two[2:3],
            sums_two[0:1],
            sums_two[1:2],
            *up_bias_grad,
            sums_two[3:4],
        ],
        axis=1,
    )
    vector_size = vector_local.shape[1]
    padded = -(-vector_size // 1024) * 1024
    vector = Chain(sum_vector(
        jnp.pad(vector_local, ((0, 0), (0, padded - vector_size))).reshape(-1, 128)
    ))
    moments = (mom_qkv, mom_out, mom_up, mom_down)
    masters = (master_qkv, master_out, master_up, master_down)
    grad_parts, moment_parts = [None] * 4, [None] * 4
    new_masters, copies = [None] * 4, [None] * 4

    def momentum(kind, own, other):
        grad_parts[kind], moment_parts[kind], gram = moment_and_gram(
            half_dp, own, other, moments[kind]
        )
        return Chain(sum_gram(gram))

    def iterate(kind, halves_of_gram):
        rows = moments[kind].shape[0] * ns_count
        step_scale = MUON_RATE * math.sqrt(max(1.0, rows / D))
        new_masters[kind], copies[kind] = muon(
            half_ns, *halves_of_gram, moment_parts[kind], masters[kind], step_scale
        )

    meet(pair, out, vector)
    meet(three)
    meet(pair, out, vector)
    meet(three, also=pair.sent)
    meet(out, vector, also=pair.sent)
    finish(out)
    gram_out = momentum(1, *((half[None], 0) for half in out.result))
    while pair.held != ["first"]:
        meet(pair)
    meet(pair, three, also=gram_out.sent)
    role_low, gram = role_gram(half_dp, *pair.held[0], role_mom)
    gram_role = Chain(sum_gram(gram))
    meet(three, also=gram_role.sent)
    meet(gram_role, also=three.sent)
    outgoing = meet(gram_out, pair, also=(gram_role.sent, outgoing))[1]
    value, first, second = pair.result
    for kind in (2, 3):
        grad_parts[kind], moment_parts[kind] = record(
            kind - 2, half_dp, value, first, second, moments[kind]
        )
    arrived = lax.all_to_all(outgoing, "dp", split_axis=0, concat_axis=0, tiled=True)
    pooled_rows = arrived.reshape(dp_count * capacity, D)
    grad_parts[2], grad_parts[3] = meet(three, also=(grad_parts[2], grad_parts[3]))
    finish(three)
    gram_three = momentum(0, *((half[None], 0) for half in three.result))
    pooled_rows = meet(gram_role, also=(pooled_rows, gram_three.sent))[0]
    meet(gram_three, also=gram_role.sent)
    meet(gram_role, also=gram_three.sent)
    finish(vector)
    (ortho,) = muon(half_ns, *gram_role.result, role_low)
    ortho_came = swap(ortho, "dp", 0)
    meet(gram_out, also=ortho)
    finish(gram_out)
    iterate(1, gram_out.result)
    new_masters[1] = meet(gram_three, also=new_masters[1])
    finish(gram_three)
    iterate(0, gram_three.result)
    ortho_came, new_masters[0] = tie(ortho_came, new_masters[0])
    for kind in (2, 3):
        rows = moments[kind].shape[0] * ns_count
        step_scale = MUON_RATE * math.sqrt(max(1.0, rows / D))
        chosen = jnp.where(bit_of("dp", 0) == kind - 2, ortho, ortho_came).astype(jnp.float32)
        new_masters[kind] = masters[kind] * (1.0 - MUON_RATE * MUON_SHRINK) - step_scale * chosen
        copies[kind] = new_masters[kind].astype(low)
    vector_grad = vector.result.reshape(-1)[:vector_size]
    vector_first = BETA_ONE * vec_first + (1.0 - BETA_ONE) * vector_grad
    vector_second = BETA_TWO * vec_second + (1.0 - BETA_TWO) * vector_grad * vector_grad
    first_hat = vector_first / (1.0 - BETA_ONE**STEP)
    second_hat = vector_second / (1.0 - BETA_TWO**STEP)
    vector_new = vectors - ADAM_RATE * first_hat / (jnp.sqrt(second_hat) + 1e-08)
    return (
        out_patches,
        pooled_rows,
        patch_grad,
        grad_parts[0],
        grad_parts[1],
        grad_parts[2],
        grad_parts[3],
        moment_parts[0],
        moment_parts[1],
        moment_parts[2],
        moment_parts[3],
        new_masters[0],
        new_masters[1],
        new_masters[2],
        new_masters[3],
        *copies,
        vector_grad,
        vector_first,
        vector_second,
        vector_new,
    )


def solution(mesh):
    placed = (
        P(("dp", "ns"), None),
        P(("dp", "ns"), None),
        P(("dp", "ns"), None),
        P(("dp", "ns"), None),
        P(("dp", "ns"), None),
        P("ns", None),
        P("ns", None),
        P("ns", None),
        P("ns", None),
        P("ns", None),
        P("ns", None),
        P("ns", None),
        P("ns", None),
        P(),
        P(),
        P(),
    )
    return jax.shard_map(
        per_device,
        mesh=mesh,
        in_specs=placed,
        out_specs=(
            P(("dp", "ns"), None),
            P(("dp", "ns"), None),
            P(("dp", "ns"), None),
            P("ns", None),
            P("ns", None),
            P("ns", None),
            P("ns", None),
            P("ns", None),
            P("ns", None),
            P("ns", None),
            P("ns", None),
            P("ns", None),
            P("ns", None),
            P("ns", None),
            P("ns", None),
            P("ns", None),
            P("ns", None),
            P("ns", None),
            P("ns", None),
            P(),
            P(),
            P(),
            P(),
        ),
        check_vma=False,
    )
```

```python
import functools
import math

import jax
import jax.numpy as jnp
from jax import lax
from jax.experimental import pallas as pl
from jax.experimental.pallas import tpu as pltpu
from jax.sharding import PartitionSpec as P

D = 768
HD = 64
FF = 3072
ITERS = 4
STEP = 10


NS_A = 3.4445
NS_B = -4.775
NS_C = 2.0315
MUON_RATE = 0.8
MUON_DECAY = 0.5
MUON_SHRINK = 0.01
ADAM_RATE = 0.5
BETA_ONE = 0.9
BETA_TWO = 0.95
MASKED = -1e30


def owner_slots(owners_row, capacity):
    image_total = owners_row.shape[0]
    ordering = jnp.arange(image_total, dtype=jnp.int32)
    earlier = (owners_row[None, :] == owners_row[:, None]) & (ordering[None, :] < ordering[:, None])
    same_before = jnp.sum(earlier.astype(jnp.int32), axis=1)
    return owners_row * capacity + same_before


def exchange(value, axis, mask):
    count = lax.axis_size(axis)
    return lax.ppermute(value, axis, [(index, index ^ mask) for index in range(count)])


def swap(value, axis, bit):
    return exchange(value, axis, 1 << bit)


def step(value, axis, bit):
    return value, axis, (1 << bit,)


def bit_of(axis, bit):
    return (lax.axis_index(axis) >> bit) & 1


def bits_in(axis):
    return (lax.axis_size(axis) - 1).bit_length()


def tie(values, earlier):
    return lax.optimization_barrier((values, earlier))


def add_low(first, second):
    return (first.astype(jnp.float32) + second.astype(jnp.float32)).astype(jnp.bfloat16)


def halves(value, axis, bit, dim=0):
    mine = bit_of(axis, bit)
    shape = value.shape
    pairs = value.reshape(*shape[:dim], 2, shape[dim] // 2, *shape[dim + 1 :])
    keep = lax.dynamic_index_in_dim(pairs, mine, dim, keepdims=False)
    send = lax.dynamic_index_in_dim(pairs, 1 - mine, dim, keepdims=False)
    return keep, send


def joined(value, other, axis, bit, dim=0):
    mine = bit_of(axis, bit)
    low_half = jnp.where(mine == 0, value, other)
    high_half = jnp.where(mine == 0, other, value)
    return jnp.concatenate([low_half, high_half], axis=dim)


class Chain:
    def __init__(self, steps):
        self.steps = steps
        self.result = None
        self.advance(None)

    def advance(self, came):
        try:
            self.sent, axis, masks, *self.held = self.steps.send(came)
            self.pending = tuple(exchange(self.sent, axis, mask) for mask in masks)
        except StopIteration as stop:
            self.sent = self.pending = None
            self.result = stop.value


def meet(*chains, also=()):
    live = [chain for chain in chains if chain.pending is not None]
    cames, also = lax.optimization_barrier((tuple(chain.pending for chain in live), also))
    for chain, came in zip(live, cames):
        chain.advance(came if len(came) > 1 else came[0])
    return also


def finish(*chains):
    while any(chain.pending is not None for chain in chains):
        meet(*chains)


def rest_of_dp(value, dim, split):
    value = yield from rest_summed(value, dim, split)
    other = yield step(value, "dp", 0)
    return value, other


def rest_summed(value, dim, split):
    first = 1
    split = split and bits_in("dp") > 2
    if split:
        keep, send = halves(value, "dp", 1, dim)
        value = add_low(keep, (yield step(send, "dp", 1)))
        first = 2
    for bit in range(first, bits_in("dp")):
        value = add_low(value, (yield step(value, "dp", bit)))
    if split:
        value = joined(value, (yield step(value, "dp", 1)), "dp", 1, dim)
    return value


def swap_roles(up, down):
    first_role = bit_of("dp", 0) == 0
    mine, theirs = jnp.where(first_role, up, down), jnp.where(first_role, down, up)
    first = yield (*step(theirs, "dp", 0), "first")
    held = (mine, first)
    second = yield (*step(tie(mine, first)[0], "dp", 0), held)
    return first, second


def sum_up(kept, sent):
    value = add_low(kept, (yield step(sent, "ns", 1)))
    keep, send = halves(value, "dp", 0)
    return add_low(keep, (yield step(send, "dp", 0)))


def sum_down(kept, sent):
    keep, send = halves(jnp.stack([kept, sent]), "dp", 0, 1)
    value = add_low(keep, (yield step(send, "dp", 0)))
    return add_low(value[0], (yield step(value[1], "ns", 1)))


def sum_blocks(value, split):
    for bit in range(bits_in("ns")):
        mine = bit_of("ns", bit)
        pairs = value.reshape(value.shape[0] // 2, 2, *value.shape[1:])
        keep = lax.dynamic_index_in_dim(pairs, mine, 1, keepdims=False)
        send = lax.dynamic_index_in_dim(pairs, 1 - mine, 1, keepdims=False)
        value = add_low(keep, (yield step(send, "ns", bit)))
    keep, send = halves(value[0], "dp", 0)
    value = add_low(keep, (yield step(send, "dp", 0)))
    return (yield from rest_of_dp(value, 0, split))


def sum_vector(value):
    for axis in ("ns", "dp"):
        for bit in range(0, bits_in(axis), 2):
            masks = [1 << bit]
            if bit + 1 < bits_in(axis):
                masks += [2 << bit, 3 << bit]
            came = yield value, axis, masks
            if len(masks) == 1:
                value = value + came
            else:
                value = (value + came[0]) + (came[1] + came[2])
    return value


def sum_gram(gram):
    gram = gram + (yield step(gram, "ns", 0))
    keep, _ = halves(gram, "ns", 0)
    for bit in range(1, bits_in("ns")):
        keep = keep + (yield step(keep, "ns", bit))
    other = yield step(keep, "ns", 0)
    return (keep[None], 0), (other[None], 0)


def by_distance(table):
    place = lax.axis_index("ns")
    return [
        lax.dynamic_index_in_dim(table, place ^ distance, 0, keepdims=True)
        for distance in range(table.shape[0])
    ]


def dot32(first, second):
    return jnp.dot(first, second, preferred_element_type=jnp.float32)


LOW = jnp.bfloat16
F32 = jnp.float32
HEADS = D // HD
BIG = 576
SMALL = 64
TILE = 256
MIB = 1024 * 1024
COST_SCALE = 1e9


def mm(first, second, first_dim=1, second_dim=0):
    return lax.dot_general(
        first,
        second,
        (((first_dim,), (second_dim,)), ((), ())),
        preferred_element_type=F32,
    )


def split_value(value):
    high = value.astype(LOW)
    return high, (value - high.astype(F32)).astype(LOW)


def normalise(values):
    row_mean = jnp.mean(values, axis=-1, keepdims=True)
    centred = values - row_mean
    scale = lax.rsqrt(jnp.mean(centred * centred, axis=-1, keepdims=True) + 1e-06)
    return centred * scale, scale


def norm_back(unit, scale, unit_grad):
    return scale * (
        unit_grad
        - jnp.mean(unit_grad, axis=-1, keepdims=True)
        - unit * jnp.mean(unit_grad * unit, axis=-1, keepdims=True)
    )


def column_sum(values):
    return jnp.sum(values, axis=0, keepdims=True)


def params(mebibytes):
    return pltpu.CompilerParams(vmem_limit_bytes=mebibytes * MIB)


def cost(micros, nbytes):
    return pl.CostEstimate(flops=int(micros * COST_SCALE), bytes_accessed=int(nbytes * COST_SCALE * 1e-9), transcendentals=0)


def whole(shape):
    return pl.BlockSpec(shape, lambda *_: (0,) * len(shape))


def once(shape):
    return pl.BlockSpec(shape, lambda *_: (0,) * len(shape), pipeline_mode=pl.Buffered(1))


def rows_of(width, tile=TILE):
    return pl.BlockSpec((tile, width), lambda i, *_: (i, 0))


def lanes_of(height, tile=TILE):
    return pl.BlockSpec((height, tile), lambda i, *_: (0, i))


STARTS = {}
WIDTHS = dict(gain_one=D, bias_one=D, bias_qkv=3 * D, gain_query=HD, bias_query=HD, gain_key=HD,
              bias_out=D, gain_two=D, bias_two=D, bias_up=FF, bias_down=D)
for part_name, part_width in WIDTHS.items():
    STARTS[part_name] = sum(WIDTHS[other] for other in STARTS)


def vector_row(ref, name):
    start = STARTS[name]
    return ref[:, start : start + WIDTHS[name]]


def to_column(row):
    return jnp.broadcast_to(row, (8, row.shape[1])).T[:, :1]


def to_row(column):
    return jnp.broadcast_to(column, (column.shape[0], 128)).T[:1]


def qkv_part(block):
    return pl.BlockSpec(
        (block.shape[0] - out_rows(block), D), lambda *_: (0, 0), pipeline_mode=pl.Buffered(1)
    )


def out_part(block):
    return pl.BlockSpec((out_rows(block), D), lambda *_: (3, 0), pipeline_mode=pl.Buffered(1))


def out_rows(block):
    return block.shape[0] // 4


def place_blocks(place_ref, refs, store):
    rows = refs[0].shape[0]
    for distance, ref in enumerate(refs):
        start = pl.multiple_of((place_ref[0] ^ distance) * rows, rows)
        store[pl.ds(start, rows), :] = ref[...]


def shape_of(shape, dtype):
    return jax.ShapeDtypeStruct(shape, dtype)


def project_kernel(place_ref, x_ref, w0, w1, w2, w3, vec_ref,
                   h_ref, qkv_ref, unit_ref, scale_ref, w_s, col_s):
    @pl.when(pl.program_id(0) == 0)
    def _():
        place_blocks(place_ref, (w0, w1, w2, w3), w_s)
        start = STARTS["bias_qkv"]
        row = vec_ref[:, start : start + 3 * D + 256]
        col_s[...] = to_column(row)

    unit, _ = normalise(x_ref[...].astype(F32))
    h_low = (unit * vector_row(vec_ref, "gain_one") + vector_row(vec_ref, "bias_one")).astype(LOW)
    h_ref[...] = h_low
    gain_q = col_s[pl.ds(3 * D, HD), :]
    bias_q = col_s[pl.ds(3 * D + HD, HD), :]
    gain_k = col_s[pl.ds(3 * D + 2 * HD, HD), :]
    for part in range(3):
        rows = pl.ds(part * D, D)
        value = mm(w_s[rows, :], h_low, 1, 1) + col_s[rows, :]
        if part == 2:
            qkv_ref[2] = value.astype(LOW)
            continue
        heads = value.reshape(HEADS, HD, value.shape[1])
        centred = heads - jnp.mean(heads, axis=1, keepdims=True)
        scale = lax.rsqrt(jnp.mean(centred * centred, axis=1, keepdims=True) + 1e-06)
        unit_heads = centred * scale
        scale_ref[part] = scale
        unit_ref[part] = unit_heads.reshape(D, -1).astype(LOW)
        if part == 0:
            result = unit_heads * gain_q[None] + bias_q[None]
            result = result.astype(LOW) * LOW(0.125)
        else:
            result = (unit_heads * gain_k[None]).astype(LOW)
        qkv_ref[part] = result.reshape(D, -1)


def project(place, patches, w_blocks, vectors):
    slots = patches.shape[0]
    return pl.pallas_call(
        project_kernel,
        grid_spec=pltpu.PrefetchScalarGridSpec(
            num_scalar_prefetch=1,
            grid=(slots // TILE,),
            in_specs=[rows_of(D)] + [qkv_part(w_blocks[0])] * 4 + [once(vectors.shape)],
            out_specs=[rows_of(D),
                       pl.BlockSpec((3, D, TILE), lambda i, p: (0, 0, i)),
                       pl.BlockSpec((2, D, TILE), lambda i, p: (0, 0, i)),
                       pl.BlockSpec((2, HEADS, 1, TILE), lambda i, p: (0, 0, 0, i))],
            scratch_shapes=[pltpu.VMEM((3 * D, D), LOW), pltpu.VMEM((3 * D + 256, 1), F32)],
        ),
        out_shape=[shape_of((slots, D), LOW), shape_of((3, D, slots), LOW),
                   shape_of((2, D, slots), LOW), shape_of((2, HEADS, 1, slots), F32)],
        compiler_params=params(24),
        cost_estimate=cost(10, 16e6),
        name="project",
    )(place, patches, *w_blocks, vectors)


def used_slots(counts_ref):
    total = counts_ref[0]
    for k in range(1, counts_ref.shape[0]):
        total = total + counts_ref[k]
    return total


def pair_mask(tile_start, used, has_big):
    same = (has_big & (tile_start + SMALL < BIG)) | (tile_start >= used)
    row_half = lax.broadcasted_iota(jnp.int32, (128, 128), 0) // SMALL
    column_half = lax.broadcasted_iota(jnp.int32, (128, 128), 1) // SMALL
    return (row_half == column_half) | same


def soft_columns(scores):
    peak = jnp.max(scores, axis=0, keepdims=True)
    exponent = jnp.exp(scores - peak)
    total = jnp.sum(exponent, axis=0, keepdims=True)
    return exponent.astype(LOW), total, peak + jnp.log(total)


def pair_mask_row(slots, used, has_big):
    row_half = lax.broadcasted_iota(jnp.int32, (128, slots), 0) // SMALL
    slot = lax.broadcasted_iota(jnp.int32, (128, slots), 1)
    column_half = slot // SMALL % 2
    start = slot // 128 * 128
    same = (has_big & (start + SMALL < BIG)) | (start >= used)
    return (row_half == column_half) | same


def attend_kernel(group, counts_ref, qkv_ref, out_ref, log_ref):
    used = used_slots(counts_ref)
    has_big = counts_ref[0] == BIG
    slots = out_ref.shape[1]
    heads = [pl.ds(index * HD, HD) for index in range(group)]

    def narrow(first, last):
        tiles = [slice(start, start + 128) for start in range(first, last, 128)]
        mask = pair_mask_row(slots, used, has_big)[:, first:last]
        span = slice(first, last)
        all_scores = []
        for rows in heads:
            all_scores.append(jnp.concatenate(
                [mm(qkv_ref[1, rows, tile], qkv_ref[0, rows, tile], 0, 0) for tile in tiles], axis=1
            ))
        for index, rows in enumerate(heads):
            scores = jnp.where(mask, all_scores[index], MASKED)
            weights, total, log_total = soft_columns(scores)
            result = jnp.concatenate(
                [mm(qkv_ref[2, rows, tile], weights[:, tile.start - first : tile.stop - first])
                 for tile in tiles], axis=1
            )
            out_ref[rows, span] = (result / total).astype(LOW)
            log_ref[index, :, span] = log_total

    @pl.when(jnp.logical_not(has_big))
    def _():
        narrow(0, 512)

    narrow(512, slots)

    @pl.when(has_big)
    def _():
        for start, width in ((0, 256), (256, 256), (512, 128)):
            span = pl.ds(start, width)
            all_scores = [
                mm(qkv_ref[1, rows, 0:640], qkv_ref[0, rows, span], 0, 0)[:BIG] for rows in heads
            ]
            for index, rows in enumerate(heads):
                weights, total, log_total = soft_columns(all_scores[index])
                weights = jnp.concatenate([weights, jnp.zeros((640 - BIG, width), LOW)], axis=0)
                result = mm(qkv_ref[2, rows, 0:640], weights) / total
                if width == 128:
                    lane = lax.broadcasted_iota(jnp.int32, (1, width), 1)
                    inside = lane < BIG - start
                    result = jnp.where(inside, result, out_ref[rows, span].astype(F32))
                    log_total = jnp.where(inside, log_total, log_ref[index, :, span])
                out_ref[rows, span] = result.astype(LOW)
                log_ref[index, :, span] = log_total

    for first in range(0, slots - 128, 256):

        @pl.when((used >= first) & (used < first + 256) & (used < slots - 128))
        def _():
            def columns(chunk, carry):
                span = pl.ds(pl.multiple_of(chunk * 256, 256), 256)
                slot = chunk * 256 + lax.broadcasted_iota(jnp.int32, (1, 256), 1)
                inside = slot >= used
                key_slot = first + lax.broadcasted_iota(jnp.int32, (256, 256), 0)
                all_scores = [
                    mm(qkv_ref[1, rows, first:slots], qkv_ref[0, rows, span], 0, 0)
                    for rows in heads
                ]
                for index, rows in enumerate(heads):
                    scores = all_scores[index]
                    top = jnp.where(key_slot >= used, scores[:256], MASKED)
                    if slots - first > 256:
                        top = jnp.concatenate([top, scores[256:]], axis=0)
                    weights, total, log_total = soft_columns(top)
                    result = mm(qkv_ref[2, rows, first:slots], weights) / total
                    old = out_ref[rows, span].astype(F32)
                    out_ref[rows, span] = jnp.where(inside, result, old).astype(LOW)
                    log_ref[index, :, span] = jnp.where(inside, log_total, log_ref[index, :, span])
                return carry

            lax.fori_loop(first // 256, slots // 256, columns, 0)


def attend(counts, qkv, group=6):
    slots = qkv.shape[2]
    return pl.pallas_call(
        functools.partial(attend_kernel, group),
        grid_spec=pltpu.PrefetchScalarGridSpec(
            num_scalar_prefetch=1,
            grid=(HEADS // group,),
            in_specs=[pl.BlockSpec((3, group * HD, slots), lambda h, c: (0, h, 0))],
            out_specs=[pl.BlockSpec((group * HD, slots), lambda h, c: (h, 0)),
                       pl.BlockSpec((group, 1, slots), lambda h, c: (h, 0, 0))],
        ),
        out_shape=[shape_of((D, slots), LOW), shape_of((HEADS, 1, slots), F32)],
        compiler_params=params(16),
        cost_estimate=cost(28, 7000000.0),
        name="attend",
    )(counts, qkv)


def attend_back_kernel(group, counts_ref, qkv_ref, attn_ref, log_ref, grad_ref, unit_ref,
                       scale_ref, vec_ref, h_ref, *refs):
    dqkv_ref, bias_ref, gains_ref, grad_w_ref, dq_s, dk_s, dv_s = refs[-7:]
    used = used_slots(counts_ref)
    has_big = counts_ref[0] == BIG
    slots = attn_ref.shape[1]
    start = STARTS["gain_query"]
    columns = to_column(vec_ref[:, start : start + 256])
    gain_q, gain_k = columns[:HD], columns[2 * HD : 3 * HD]

    @pl.when(pl.program_id(0) == 0)
    def _():
        gains_ref[...] = jnp.zeros_like(gains_ref)

    def head_rows(index):
        return pl.ds(index * HD, HD)

    def delta_of(index, span):
        return column_sum(
            grad_ref[head_rows(index), span].astype(F32)
            * attn_ref[head_rows(index), span].astype(F32)
        )

    def narrow(first, last):
        tiles = [slice(start, start + 128) for start in range(first, last, 128)]
        mask = pair_mask_row(slots, used, has_big)[:, first:last]
        span = slice(first, last)

        def wide(product):
            return jnp.concatenate([product(tile) for tile in tiles], axis=1)

        def inner(tile):
            return slice(tile.start - first, tile.stop - first)

        all_scores, all_grads = [], []
        for index in range(group):
            rows = head_rows(index)
            all_scores.append(wide(
                lambda tile: mm(qkv_ref[1, rows, tile], qkv_ref[0, rows, tile], 0, 0)))
            all_grads.append(wide(
                lambda tile: mm(qkv_ref[2, rows, tile], grad_ref[rows, tile], 0, 0)))
        for index in range(group):
            rows = head_rows(index)
            scores = all_scores[index] - log_ref[index, :, span]
            probs = jnp.exp(jnp.where(mask, scores, MASKED))
            score_low = (probs * (all_grads[index] - delta_of(index, span))).astype(LOW)
            probs_low = probs.astype(LOW)
            dv_s[rows, span] = wide(
                lambda tile: mm(grad_ref[rows, tile], probs_low[:, inner(tile)], 1, 1))
            dk_s[rows, span] = wide(
                lambda tile: mm(qkv_ref[0, rows, tile], score_low[:, inner(tile)], 1, 1))
            dq_s[rows, span] = wide(
                lambda tile: mm(qkv_ref[1, rows, tile], score_low[:, inner(tile)]))

    @pl.when(jnp.logical_not(has_big))
    def _():
        narrow(0, 512)

    @pl.when(used > 512)
    def _():
        narrow(512, slots)

    @pl.when(used <= 512)
    def _():
        for store in (dq_s, dk_s, dv_s):
            store[:, 512:slots] = jnp.zeros((store.shape[0], slots - 512), F32)

    @pl.when(has_big)
    def _():
        wide = pl.ds(0, 640)
        dk = [jnp.zeros((HD, 640), F32)] * group
        dv = [jnp.zeros((HD, 640), F32)] * group
        for start, width in ((0, 256), (256, 256), (512, 128)):
            span = pl.ds(start, width)
            lane = lax.broadcasted_iota(jnp.int32, (1, width), 1)
            all_scores, all_grads = [], []
            for index in range(group):
                rows = head_rows(index)
                all_scores.append(mm(qkv_ref[1, rows, wide], qkv_ref[0, rows, span], 0, 0)[:BIG])
                all_grads.append(mm(qkv_ref[2, rows, wide], grad_ref[rows, span], 0, 0)[:BIG])
            for index in range(group):
                rows = head_rows(index)
                probs = jnp.exp(all_scores[index] - log_ref[index, :, span])
                if width == 128:
                    probs = jnp.where(lane < BIG - start, probs, 0.0)
                score_low = (probs * (all_grads[index] - delta_of(index, span))).astype(LOW)
                blank = jnp.zeros((640 - BIG, width), LOW)
                score_low = jnp.concatenate([score_low, blank], axis=0)
                probs_low = jnp.concatenate([probs.astype(LOW), blank], axis=0)
                dv[index] = dv[index] + mm(grad_ref[rows, span], probs_low, 1, 1)
                dk[index] = dk[index] + mm(qkv_ref[0, rows, span], score_low, 1, 1)
                dq = mm(qkv_ref[1, rows, wide], score_low)
                if width == 128:
                    dq = jnp.where(lane < BIG - start, dq, dq_s[rows, span])
                dq_s[rows, span] = dq
        inside = lax.broadcasted_iota(jnp.int32, (1, 640), 1) < BIG
        for index in range(group):
            rows = head_rows(index)
            dk_s[rows, wide] = jnp.where(inside, dk[index], dk_s[rows, wide])
            dv_s[rows, wide] = jnp.where(inside, dv[index], dv_s[rows, wide])

    sums = [jnp.zeros((HD, 1), F32)] * 3
    biases = [[], [], []]
    for index in range(group):
        rows = head_rows(index)
        for part, store, gain in ((0, dq_s, gain_q), (1, dk_s, gain_k)):
            unit = unit_ref[part, rows, :].astype(F32)
            grad = store[rows, :]
            if part == 0:
                grad = grad * 0.125
                sums[0] = sums[0] + jnp.sum(grad * unit, axis=1, keepdims=True)
                sums[1] = sums[1] + jnp.sum(grad, axis=1, keepdims=True)
            else:
                sums[2] = sums[2] + jnp.sum(grad * unit, axis=1, keepdims=True)
            unit_grad = grad * gain
            result = scale_ref[part, index] * (
                unit_grad
                - jnp.mean(unit_grad, axis=0, keepdims=True)
                - unit * jnp.mean(unit_grad * unit, axis=0, keepdims=True)
            )
            result = result.astype(LOW)
            dqkv_ref[part, rows, :] = result
            biases[part].append(jnp.sum(result.astype(F32), axis=1, keepdims=True))
        result = dv_s[rows, :].astype(LOW)
        dqkv_ref[2, rows, :] = result
        biases[2].append(jnp.sum(result.astype(F32), axis=1, keepdims=True))
    for part in range(3):
        grad_w_ref[part] = mm(dqkv_ref[part], h_ref[...]).astype(LOW)
        bias_ref[part] = to_row(jnp.concatenate(biases[part], axis=0))
    blank = jnp.zeros((HD, 1), F32)
    gains_ref[:, 0:128] += to_row(jnp.concatenate(sums[:2], axis=0))
    gains_ref[:, 128:256] += to_row(jnp.concatenate([sums[2], blank], axis=0))


def attend_back(counts, qkv, attn, log_total, attn_grad, unit, scale, vectors, h, earlier, half,
                group=2):
    slots = qkv.shape[2]
    steps = HEADS // group // 2
    first = half * steps
    head_block = pl.BlockSpec((group * HD, slots), lambda h, c: (h + first, 0))
    dqkv_block = pl.BlockSpec((3, group * HD, slots), lambda h, c: (0, h + first, 0))
    held = pl.BlockSpec(memory_space=pl.ANY)
    grad_block = pl.BlockSpec((3, group * HD, D), lambda h, c: (0, h + first, 0))
    return pl.pallas_call(
        functools.partial(attend_back_kernel, group),
        grid_spec=pltpu.PrefetchScalarGridSpec(
            num_scalar_prefetch=1,
            grid=(steps,),
            in_specs=[dqkv_block,
                      head_block,
                      pl.BlockSpec((group, 1, slots), lambda h, c: (h + first, 0, 0)),
                      head_block,
                      pl.BlockSpec((2, group * HD, slots), lambda h, c: (0, h + first, 0)),
                      pl.BlockSpec((2, group, 1, slots), lambda h, c: (0, h + first, 0, 0)),
                      whole(vectors.shape), once(h.shape)] + [held] * len(earlier),
            out_specs=[dqkv_block,
                       pl.BlockSpec((3, 1, group * HD), lambda h, c: (0, 0, h)),
                       whole((1, 256)), grad_block],
            scratch_shapes=[pltpu.VMEM((group * HD, slots), F32)] * 3,
        ),
        out_shape=[shape_of((3, D, slots), LOW), shape_of((3, 1, D // 2), F32),
                   shape_of((1, 256), F32), shape_of((3, D, D), LOW)],
        input_output_aliases={9: 0, 10: 3} if earlier else {},
        compiler_params=params(60),
        cost_estimate=cost(2.0, 8e6),
        name="attend_back",
    )(counts, qkv, attn, log_total, attn_grad, unit, scale, vectors, h, *earlier)


def segment_picker(counts_ref, first, width):
    images = counts_ref.shape[0]
    slot = first + lax.broadcasted_iota(jnp.int32, (images, width), 1)
    image = lax.broadcasted_iota(jnp.int32, (images, width), 0)
    start = jnp.int32(0)
    picked = jnp.zeros((images, width), jnp.bool_)
    for k in range(images):
        end = start + counts_ref[k]
        picked = picked | ((image == k) & (slot >= start) & (slot < end))
        start = end
    return picked.astype(F32), start


def image_sizes(counts_ref):
    images = counts_ref.shape[0]
    image = lax.broadcasted_iota(jnp.int32, (images, 1), 0)
    sizes = jnp.zeros((images, 1), F32)
    for k in range(images):
        sizes = jnp.where(image == k, jnp.maximum(counts_ref[k], 1).astype(F32), sizes)
    return sizes


def middle_kernel(counts_ref, place_ref, x_ref, attn_ref, w0, w1, w2, w3, vec_ref, cot_ref,
                  image_ref, x2_ref, h_ref, dy_ref, mix_ref, w_s):
    @pl.when(pl.program_id(0) == 0)
    def _():
        place_blocks(place_ref, (w0, w1, w2, w3), w_s)

    x2 = x_ref[...].astype(F32) + mm(attn_ref[...], w_s[...], 0, 1) + vector_row(vec_ref, "bias_out")
    x2_ref[...] = x2
    unit, _ = normalise(x2)
    h_ref[...] = (
        unit * vector_row(vec_ref, "gain_two") + vector_row(vec_ref, "bias_two")
    ).astype(LOW)
    tile = x_ref.shape[0]
    first = pl.program_id(0) * tile
    picker, used = segment_picker(counts_ref, first, tile)
    picker = picker.astype(LOW)
    image_grad = image_ref[...].astype(F32) / image_sizes(counts_ref)
    dy = jnp.zeros(x2.shape, F32)
    rest = image_grad
    for _ in range(3):
        high, rest = split_value32(rest)
        dy = dy + mm(picker, high, 0, 0)
    slot = first + lax.broadcasted_iota(jnp.int32, (tile, 1), 0)
    dy = dy + jnp.where(slot < used, cot_ref[...].astype(F32), 0.0)
    dy_ref[...] = dy
    mix_ref[...] = dy.astype(LOW)


def split_value32(value):
    high = value.astype(LOW)
    return high, value - high.astype(F32)


def middle(counts, place, patches, attn, w_blocks, vectors, patch_cot, image_cot):
    slots = patches.shape[0]
    images = counts.shape[0]
    return pl.pallas_call(
        middle_kernel,
        grid_spec=pltpu.PrefetchScalarGridSpec(
            num_scalar_prefetch=2,
            grid=(slots // TILE,),
            in_specs=[rows_of(D), lanes_of(D)] + [out_part(w_blocks[0])] * 4
            + [whole(vectors.shape), rows_of(D), whole((images, D))],
            out_specs=[rows_of(D)] * 4,
            scratch_shapes=[pltpu.VMEM((D, D), LOW)],
        ),
        out_shape=[shape_of((slots, D), F32), shape_of((slots, D), LOW),
                   shape_of((slots, D), F32), shape_of((slots, D), LOW)],
        compiler_params=params(20),
        cost_estimate=cost(9, 20e6),
        name="middle",
    )(counts, place, patches, attn, *w_blocks, vectors, patch_cot, image_cot)


def feed_kernel(distances, start_y, y_in_ref, dh_in_ref, h_ref, mix_ref, up_a, down_a, up_b,
                down_b, bias_ref, vec_ref,
                y_ref, dh_ref, grad_a, grad_b, bias_grad_a, bias_grad_b):
    @pl.when(pl.program_id(0) == 0)
    def _():
        if start_y:
            y_ref[...] = y_in_ref[...] + vector_row(vec_ref, "bias_down")
            dh_ref[...] = jnp.zeros_like(dh_ref)
        else:
            y_ref[...] = y_in_ref[...]
            dh_ref[...] = dh_in_ref[...]

    slots = h_ref.shape[0]
    for distance, up_ref, down_ref, grad_ref, bias_grad_ref in (
        (distances[0], up_a, down_a, grad_a, bias_grad_a),
        (distances[1], up_b, down_b, grad_b, bias_grad_b),
    ):
        up, down = up_ref[...], down_ref[...]
        h, mix = h_ref[...], mix_ref[...]
        u = mm(up, h, 1, 1) + to_column(bias_ref[distance : distance + 1])
        back = mm(down, mix, 1, 1)
        gate = 0.5 * (1.0 + lax.erf(u * (0.5**0.5)))
        slope = gate + u * (jnp.exp(-0.5 * u * u) * ((0.5 / math.pi) ** 0.5))
        hidden = (u * gate).astype(LOW)
        pre = (back * slope).astype(LOW)
        y_ref[...] += mm(hidden, down, 0, 0)
        dh_ref[...] += mm(pre, up, 0, 0)
        grad_up = mm(pre, h)
        grad_down = mm(hidden, mix)
        bias_grad = to_row(jnp.sum(pre.astype(F32), axis=1, keepdims=True))
        grad_ref[0] = grad_up.astype(LOW)
        grad_ref[1] = grad_down.astype(LOW)
        bias_grad_ref[...] = bias_grad


def feed(distances, y, dh2, h2, mix, pair_a, pair_b, bias_table, vectors, block=256):
    slots = y.shape[0]
    units = pair_a.shape[1]
    start_y = dh2 is None
    if start_y:
        dh2 = y
    up = pl.BlockSpec((None, block, D), lambda i: (0, i, 0))
    down = pl.BlockSpec((None, block, D), lambda i: (1, i, 0))
    bias = pl.BlockSpec((1, block), lambda i: (0, i))
    both = pl.BlockSpec((2, block, D), lambda i: (0, i, 0))
    dh_spec = pl.BlockSpec((8, D), lambda i: (0, 0)) if start_y else once((slots, D))
    return pl.pallas_call(
        functools.partial(feed_kernel, distances, start_y),
        grid=(units // block,),
        in_specs=[once((slots, D)), dh_spec, once((slots, D)), once((slots, D)),
                  up, down, up, down, pl.BlockSpec((bias_table.shape[0], block), lambda i: (0, i)),
                  whole(vectors.shape)],
        out_specs=[once((slots, D)), once((slots, D)), both, both, bias, bias],
        out_shape=[shape_of((slots, D), F32), shape_of((slots, D), F32),
                   shape_of((2, units, D), LOW), shape_of((2, units, D), LOW),
                   shape_of((1, units), F32), shape_of((1, units), F32)],
        compiler_params=params(26),
        cost_estimate=cost(24, 25e6),
        name="feed",
    )(y, dh2, h2, mix, pair_a, pair_a, pair_b, pair_b, bias_table, vectors)


def after_kernel(counts_ref, place_ref, y_ref, x2_ref, dh_ref, dy_ref, attn_ref, w0, w1, w2, w3,
                 vec_ref, out_ref, pooled_ref, dx2_ref, dattn_ref, grad_out_ref, sums_ref,
                 pool_s, grad_s, w_s):
    step = pl.program_id(0)

    @pl.when(step == 0)
    def _():
        pool_s[...] = jnp.zeros_like(pool_s)
        grad_s[...] = jnp.zeros_like(grad_s)
        sums_ref[...] = jnp.zeros_like(sums_ref)
        place_blocks(place_ref, (w0, w1, w2, w3), w_s)

    y = y_ref[...]
    tile = y.shape[0]
    out_ref[...] = y.astype(LOW)
    picker, _ = segment_picker(counts_ref, step * tile, tile)
    picker = picker.astype(LOW)
    rest = y
    pooled = pool_s[...]
    for _ in range(3):
        high, rest = split_value32(rest)
        pooled = pooled + mm(picker, high)
    pool_s[...] = pooled
    pooled_ref[...] = (pooled / image_sizes(counts_ref)).astype(LOW)
    unit, scale = normalise(x2_ref[...])
    dh = dh_ref[...]
    sums_ref[0:1] += column_sum(dh * unit)
    sums_ref[1:2] += column_sum(dh)
    dy = dy_ref[...]
    sums_ref[3:4] += column_sum(dy.astype(LOW).astype(F32))
    dx2 = dy + norm_back(unit, scale, dh * vector_row(vec_ref, "gain_two"))
    dx2_ref[...] = dx2
    da = dx2.astype(LOW)
    sums_ref[2:3] += column_sum(da.astype(F32))
    dattn_ref[...] = mm(w_s[...], da, 0, 1).astype(LOW)
    grad = grad_s[...] + mm(da, attn_ref[...], 0, 1)
    grad_s[...] = grad
    grad_out_ref[...] = grad.astype(LOW)


def after(counts, place, y, x2, dh2, dy, attn, w_blocks, vectors):
    slots = y.shape[0]
    images = counts.shape[0]
    return pl.pallas_call(
        after_kernel,
        grid_spec=pltpu.PrefetchScalarGridSpec(
            num_scalar_prefetch=2,
            grid=(slots // TILE,),
            in_specs=[rows_of(D), rows_of(D), rows_of(D), rows_of(D), lanes_of(D)]
            + [out_part(w_blocks[0])] * 4 + [whole(vectors.shape)],
            out_specs=[rows_of(D), whole((images, D)), rows_of(D), lanes_of(D), whole((D, D)),
                       whole((8, D))],
            scratch_shapes=[pltpu.VMEM((images, D), F32), pltpu.VMEM((D, D), F32),
                            pltpu.VMEM((D, D), LOW)],
        ),
        out_shape=[shape_of((slots, D), LOW), shape_of((images, D), LOW),
                   shape_of((slots, D), F32), shape_of((D, slots), LOW), shape_of((D, D), LOW),
                   shape_of((8, D), F32)],
        compiler_params=params(60),
        cost_estimate=cost(4.0, 25e6),
        name="after",
    )(counts, place, y, x2, dh2, dy, attn, *w_blocks, vectors)


def first_back_kernel(place_ref, x_ref, dqkv_ref, w0, w1, w2, w3, vec_ref, dx2_ref,
                      out_ref, sums_ref, w_s):
    @pl.when(pl.program_id(0) == 0)
    def _():
        sums_ref[...] = jnp.zeros_like(sums_ref)
        place_blocks(place_ref, (w0, w1, w2, w3), w_s)

    dh = mm(dqkv_ref[...], w_s[...], 0, 0)
    unit, scale = normalise(x_ref[...].astype(F32))
    sums_ref[0:1] += column_sum(dh * unit)
    sums_ref[1:2] += column_sum(dh)
    out_ref[...] = dx2_ref[...] + norm_back(unit, scale, dh * vector_row(vec_ref, "gain_one"))


def first_back(place, patches, dqkv, w_blocks, vectors, dx2):
    slots = patches.shape[0]
    return pl.pallas_call(
        first_back_kernel,
        grid_spec=pltpu.PrefetchScalarGridSpec(
            num_scalar_prefetch=1,
            grid=(slots // TILE,),
            in_specs=[rows_of(D), lanes_of(3 * D)] + [qkv_part(w_blocks[0])] * 4
            + [whole(vectors.shape), rows_of(D)],
            out_specs=[rows_of(D), whole((8, D))],
            scratch_shapes=[pltpu.VMEM((3 * D, D), LOW)],
        ),
        out_shape=[shape_of((slots, D), F32), shape_of((8, D), F32)],
        compiler_params=params(22),
        cost_estimate=cost(0.2, 17e6),
        name="first_back",
    )(place, patches, dqkv, *w_blocks, vectors, dx2)


SIDE = 256
GRID_BLOCKS = [(i, j) for i in range(D // SIDE) for j in range(i, D // SIDE)]


def moment_kernel(half_ref, own_ref, other_ref, mom_ref, grad_ref, moment_ref, gram_ref):
    rows = own_ref.shape[0]
    for ref, place in ((own_ref, half_ref[0]), (other_ref, 1 - half_ref[0])):
        span = pl.ds(pl.multiple_of(place * rows, rows), rows)
        grad = ref[...].astype(F32)
        grad_ref[span, :] = grad
        moment_ref[span, :] = MUON_DECAY * mom_ref[span, :] + grad
    moment_low = moment_ref[...].astype(LOW)
    for index, (i, j) in enumerate(GRID_BLOCKS):
        gram_ref[index] = mm(
            moment_low[:, i * SIDE : (i + 1) * SIDE], moment_low[:, j * SIDE : (j + 1) * SIDE], 0, 0
        )


def role_kernel(half_ref, own_ref, other_ref, mom_ref, low_ref, gram_ref):
    rows = own_ref.shape[0]
    for ref, place in ((own_ref, half_ref[0]), (other_ref, 1 - half_ref[0])):
        span = pl.ds(pl.multiple_of(place * rows, rows), rows)
        low_ref[span, :] = (MUON_DECAY * mom_ref[span, :] + ref[...].astype(F32)).astype(LOW)
    moment_low = low_ref[...]
    for index, (i, j) in enumerate(GRID_BLOCKS):
        gram_ref[index] = mm(
            moment_low[:, i * SIDE : (i + 1) * SIDE], moment_low[:, j * SIDE : (j + 1) * SIDE], 0, 0
        )


def role_gram(half, own, other, mom):
    rows = mom.shape[0]
    blocks = len(GRID_BLOCKS)
    out_shape = [shape_of((rows, D), LOW), shape_of((blocks, SIDE, SIDE), F32)]
    return pl.pallas_call(
        role_kernel,
        grid=(1,),
        in_specs=[pl.BlockSpec(memory_space=pltpu.SMEM), once(own.shape), once(other.shape),
                  once((rows, D))],
        out_specs=[once(leaf.shape) for leaf in out_shape],
        out_shape=out_shape,
        compiler_params=params(16),
        cost_estimate=cost(0.5, rows * D * 8 + blocks * SIDE * SIDE * 4),
        name="role_gram",
    )(half, own, other, mom)


def record_kernel(kind, half_ref, own_ref, first_ref, second_ref, mom_ref, grad_ref, moment_ref):
    rows = own_ref.shape[0]

    def put(ref, place):
        span = pl.ds(pl.multiple_of(place * rows, rows), rows)
        grad = ref[...].astype(F32)
        grad_ref[span, :] = grad
        moment_ref[span, :] = MUON_DECAY * mom_ref[span, :] + grad

    put(own_ref, half_ref[0])

    @pl.when(half_ref[0] == kind)
    def _():
        put(first_ref, 1 - half_ref[0])

    @pl.when(half_ref[0] != kind)
    def _():
        put(second_ref, 1 - half_ref[0])


def record(kind, half, own, first, second, mom):
    rows = mom.shape[0]
    out_shape = [shape_of((rows, D), F32), shape_of((rows, D), F32)]
    return pl.pallas_call(
        functools.partial(record_kernel, kind),
        grid=(1,),
        in_specs=[pl.BlockSpec(memory_space=pltpu.SMEM), once(own.shape), once(first.shape),
                  once(second.shape), once((rows, D))],
        out_specs=[once(leaf.shape) for leaf in out_shape],
        out_shape=out_shape,
        compiler_params=params(16),
        cost_estimate=cost(0.5, rows * D * 14),
        name="record",
    )(half, own, first, second, mom)


def one_of(stack, index):
    return pl.BlockSpec(
        (None,) + stack.shape[1:],
        lambda i: (index,) + (0,) * (stack.ndim - 1),
        pipeline_mode=pl.Buffered(1),
    )


def moment_and_gram(half, own, other, mom):
    rows = mom.shape[0]
    blocks = len(GRID_BLOCKS)
    out_shape = [shape_of((rows, D), F32), shape_of((rows, D), F32),
                 shape_of((blocks, SIDE, SIDE), F32)]
    (own, own_index), (other, other_index) = own, other
    return pl.pallas_call(
        moment_kernel,
        grid=(1,),
        in_specs=[pl.BlockSpec(memory_space=pltpu.SMEM), one_of(own, own_index),
                  one_of(other, other_index), once((rows, D))],
        out_specs=[once(leaf.shape) for leaf in out_shape],
        out_shape=out_shape,
        compiler_params=params(16),
        cost_estimate=cost(0.5, rows * D * 14 + blocks * SIDE * SIDE * 4),
        name="moment",
    )(half, own, other, mom)


def muon_kernel(step_scale, half_ref, own_ref, other_ref, moment_ref, *refs):
    *refs, gram_s, low_s, rest_s, mix_s, rows_s, gram_ref = refs
    count = own_ref.shape[0]
    for index in range(count):
        gram_ref[half_ref[0] * count + index] = own_ref[index]
        gram_ref[(1 - half_ref[0]) * count + index] = other_ref[index]
    spans = [slice(i * SIDE, (i + 1) * SIDE) for i in range(D // SIDE)]

    def put(refs, i, j, blocks):
        for ref, block in zip(refs, blocks):
            ref[spans[i], spans[j]] = block
            if i != j:
                ref[spans[j], spans[i]] = block.T

    total = jnp.zeros((1, 1), F32)
    row = lax.broadcasted_iota(jnp.int32, (SIDE, SIDE), 0)
    column = lax.broadcasted_iota(jnp.int32, (SIDE, SIDE), 1)
    for index, (i, j) in enumerate(GRID_BLOCKS):
        if i == j:
            kept = jnp.where(row == column, gram_ref[index], 0.0)
            total = total + jnp.sum(jnp.sum(kept, axis=0, keepdims=True), axis=1, keepdims=True)
    scale = 1.0 / (jnp.sqrt(total) + 1e-07)
    square = scale * scale
    for index, (i, j) in enumerate(GRID_BLOCKS):
        block = gram_ref[index] * square
        put((gram_s,), i, j, (block,))
        put((low_s, rest_s), i, j, split_value(block))
    rows_s[...] = moment_ref[...].astype(LOW)
    for iteration in range(ITERS):
        careful = iteration == 0
        for i, j in GRID_BLOCKS:
            squared = mm(low_s[spans[i], :], low_s[:, spans[j]])
            put((mix_s,), i, j, ((NS_B * gram_s[spans[i], spans[j]] + NS_C * squared).astype(LOW),))
        if iteration == ITERS - 1:
            break
        middle_blocks = []
        for i in range(D // SIDE):
            for j in range(0 if careful else i, D // SIDE):
                block = NS_A * gram_s[spans[i], spans[j]] + mm(low_s[spans[i], :], mix_s[:, spans[j]])
                if careful:
                    block = block + mm(rest_s[spans[i], :], mix_s[:, spans[j]])
                middle_blocks.append((i, j, block))
        for i, j, block in middle_blocks:
            gram_s[spans[i], spans[j]] = block
            if careful:
                low_s[spans[i], spans[j]], rest_s[spans[i], spans[j]] = split_value(block)
            else:
                put((low_s,), i, j, (block.astype(LOW),))
        renewed = NS_A * rows_s[...].astype(F32) + mm(rows_s[...], mix_s[...])
        if careful:
            renewed = renewed * scale
        rows_s[...] = renewed.astype(LOW)
        gram_blocks = []
        for i, j in GRID_BLOCKS:
            block = NS_A * gram_s[spans[i], spans[j]] + mm(mix_s[spans[i], :], low_s[:, spans[j]])
            if careful:
                block = block + mm(mix_s[spans[i], :], rest_s[:, spans[j]])
            gram_blocks.append((i, j, block))
        for i, j, block in gram_blocks:
            gram_s[spans[i], spans[j]] = block
            put((low_s,), i, j, (block.astype(LOW),))
    renewed = NS_A * rows_s[...].astype(F32) + mm(rows_s[...], mix_s[...])
    if step_scale is None:
        (ortho_ref,) = refs
        ortho_ref[...] = renewed.astype(LOW)
        return
    master_ref, new_ref, copy_ref = refs
    new = master_ref[...] * (1.0 - MUON_RATE * MUON_SHRINK) - step_scale * renewed
    new_ref[...] = new
    copy_ref[...] = new.astype(LOW)


def muon(half, own, other, moment, master=None, step_scale=None):
    rows = moment.shape[0]
    (own, own_index), (other, other_index) = own, other
    out_shape = [shape_of((rows, D), F32), shape_of((rows, D), LOW)]
    masters = [master]
    if master is None:
        out_shape, masters = out_shape[1:], []
    return pl.pallas_call(
        functools.partial(muon_kernel, step_scale),
        grid=(1,),
        in_specs=[pl.BlockSpec(memory_space=pltpu.SMEM), one_of(own, own_index),
                  one_of(other, other_index), once((rows, D))] + [once((rows, D))] * len(masters),
        out_specs=[once(leaf.shape) for leaf in out_shape],
        out_shape=out_shape,
        scratch_shapes=[pltpu.VMEM((D, D), F32), pltpu.VMEM((D, D), LOW), pltpu.VMEM((D, D), LOW),
                        pltpu.VMEM((D, D), LOW), pltpu.VMEM((rows, D), LOW),
                        pltpu.VMEM((len(GRID_BLOCKS), SIDE, SIDE), F32)],
        compiler_params=params(30),
        cost_estimate=cost(1.0, rows * D * 14),
        name="muon",
    )(half, own, other, moment, *masters)


def per_device(
    patches,
    counts,
    owners,
    pooled_cot,
    patch_cot,
    master_qkv,
    master_out,
    master_up,
    master_down,
    mom_qkv,
    mom_out,
    mom_up,
    mom_down,
    vectors,
    vec_first,
    vec_second,
):
    dp_count = lax.axis_size("dp")
    ns_count = lax.axis_size("ns")
    slot_count = patches.shape[0]
    image_total = counts.shape[1]
    capacity = pooled_cot.shape[0] // dp_count
    low = jnp.bfloat16
    place = lax.axis_index("ns").astype(jnp.int32).reshape(1)
    half_dp = bit_of("dp", 0).astype(jnp.int32).reshape(1)
    half_ns = bit_of("ns", 0).astype(jnp.int32).reshape(1)

    own_first = jnp.concatenate([master_qkv, master_out]).astype(low)
    w_first = (own_first, swap(own_first, "ns", 0), swap(own_first, "ns", 1))
    row = vectors.reshape(1, -1)
    bias_start = STARTS["bias_up"]
    bias_table = jnp.concatenate(
        by_distance(vectors[bias_start : bias_start + FF].reshape(ns_count, -1)), axis=0
    )
    returned = lax.all_to_all(
        pooled_cot.reshape(dp_count, capacity, D), "dp", split_axis=0, concat_axis=0, tiled=True
    ).reshape(dp_count * capacity, D)
    targets = owner_slots(owners[0], capacity)
    routing = (
        jnp.arange(dp_count * capacity, dtype=jnp.int32)[:, None] == targets[None, :]
    ).astype(low)
    image_cot = dot32(routing.T, returned).astype(low)
    sizes = counts[0]
    own_pair = jnp.stack([master_up, master_down]).astype(low)
    role_mom = jnp.where(bit_of("dp", 0) == 0, mom_up, mom_down)
    far_first, (own_pair, image_cot, role_mom) = tie(w_first[2], (own_pair, image_cot, role_mom))
    w_first = (w_first[0], w_first[1], far_first, swap(far_first, "ns", 0))
    own_pair, _ = tie(own_pair, far_first)
    near_pair, next_pair, far_pair = own_pair, swap(own_pair, "ns", 0), swap(own_pair, "ns", 1)
    first_low, qkv, unit, scale = project(place, patches, w_first, row)
    attn, log_total = attend(sizes, qkv)
    x2, second_low, row_grad, mixed_low = middle(
        sizes, place, patches, attn, w_first, row, patch_cot, image_cot
    )
    y, second_grad, grad_1, grad_0, bias_1, bias_0 = feed(
        (1, 0), x2, None, second_low, mixed_low, next_pair, near_pair, bias_table, row
    )
    came_1 = swap(grad_1, "ns", 0)
    y, far_pair = tie(y, far_pair)
    far_next_pair = swap(far_pair, "ns", 0)
    y, second_grad, grad_3, grad_2, bias_3, bias_2 = feed(
        (3, 2), y, second_grad, second_low, mixed_low, far_next_pair, far_pair, bias_table, row
    )
    came_3 = swap(grad_3, "ns", 0)
    kept = add_low(grad_0, came_1)
    came_3, kept = tie(came_3, kept)
    sent = add_low(grad_2, came_3)
    up, down = Chain(sum_up(kept[0], sent[0])), Chain(sum_down(kept[1], sent[1]))
    y, (sent, kept) = tie(y, (sent, kept))
    out_patches, pooled, middle_grad, attn_grad, grad_out, sums_two = after(
        sizes, place, y, x2, second_grad, row_grad, attn, w_first, row
    )
    out = Chain(sum_blocks(grad_out.reshape(ns_count, -1, D), False))
    dqkv, bias_a, gains_a, grad_qkv = attend_back(
        sizes, qkv, attn, log_total, attn_grad, unit, scale, row, first_low, (), 0
    )
    earlier = meet(up, down, out, also=(dqkv, grad_qkv))
    dqkv, bias_b, gains_b, grad_qkv = attend_back(
        sizes, qkv, attn, log_total, attn_grad, unit, scale, row, first_low, earlier, 1
    )
    outgoing = dot32(routing, pooled).astype(low).reshape(dp_count, capacity, D)
    dqkv, grad_qkv = meet(up, down, out, also=(dqkv.reshape(3 * D, slot_count), grad_qkv))
    up = Chain(rest_summed(up.result, 0, True))
    down = Chain(rest_summed(down.result, 0, True))
    three = Chain(sum_blocks(grad_qkv.reshape(ns_count, -1, D), True))
    meet(three)
    meet(up, also=three.sent)
    middle_grad = meet(down, out, also=(middle_grad, up.sent))[0]
    patch_grad, sums_one = first_back(place, patches, dqkv, w_first, row, middle_grad)
    sums_one, patch_grad = meet(three, also=(sums_one, patch_grad))
    gains = gains_a + gains_b
    up_bias_grad = by_distance(jnp.concatenate([bias_0, bias_1, bias_2, bias_3], axis=0))
    vector_local = jnp.concatenate(
        [
            sums_one[0:1],
            sums_one[1:2],
            jnp.concatenate([bias_a, bias_b], axis=2).reshape(1, 3 * D),
            gains[:, : 3 * HD],
            sums_two[2:3],
            sums_two[0:1],
            sums_two[1:2],
            *up_bias_grad,
            sums_two[3:4],
        ],
        axis=1,
    )
    vector_size = vector_local.shape[1]
    padded = -(-vector_size // 1024) * 1024
    vector = Chain(sum_vector(
        jnp.pad(vector_local, ((0, 0), (0, padded - vector_size))).reshape(-1, 128)
    ))
    moments = (mom_qkv, mom_out, mom_up, mom_down)
    masters = (master_qkv, master_out, master_up, master_down)
    grad_parts, moment_parts = [None] * 4, [None] * 4
    new_masters, copies = [None] * 4, [None] * 4

    def momentum(kind, own, other):
        grad_parts[kind], moment_parts[kind], gram = moment_and_gram(
            half_dp, own, other, moments[kind]
        )
        return Chain(sum_gram(gram))

    def iterate(kind, halves_of_gram):
        rows = moments[kind].shape[0] * ns_count
        step_scale = MUON_RATE * math.sqrt(max(1.0, rows / D))
        new_masters[kind], copies[kind] = muon(
            half_ns, *halves_of_gram, moment_parts[kind], masters[kind], step_scale
        )

    outgoing = meet(up, out, vector, also=outgoing)
    meet(three, also=up.sent)
    meet(down, also=three.sent)
    arrived = lax.all_to_all(outgoing, "dp", split_axis=0, concat_axis=0, tiled=True)
    pooled_rows = arrived.reshape(dp_count * capacity, D)
    finish(up)
    pooled_rows = meet(down, out, vector, also=(pooled_rows, up.result))[0]
    finish(down)
    pair = Chain(swap_roles(up.result, down.result))
    meet(out, vector, also=pair.sent)
    finish(out)
    gram_out = momentum(1, *((half[None], 0) for half in out.result))
    meet(gram_out)
    meet(three, also=(pair.sent, gram_out.sent))
    while pair.held != ["first"]:
        meet(pair)
    meet(pair, three, gram_out)
    role_low, gram = role_gram(half_dp, *pair.held[0], role_mom)
    gram_role = Chain(sum_gram(gram))
    meet(gram_role, three, gram_out)
    gram_own = tie(gram_out.result[0][0], (three.sent, gram_role.sent))[0]
    iterate(1, ((gram_own, 0), gram_out.result[1]))
    meet(pair, also=(gram_role.sent, new_masters[1]))
    first, second = pair.result
    for kind, own in ((2, up.result), (3, down.result)):
        grad_parts[kind], moment_parts[kind] = record(
            kind - 2, half_dp, own, first, second, moments[kind]
        )
    new_masters[1], grad_parts[2], grad_parts[3] = meet(
        gram_role, also=(new_masters[1], grad_parts[2], grad_parts[3])
    )
    meet(three, also=gram_role.sent)
    finish(three)
    gram_three = momentum(0, *((half[None], 0) for half in three.result))
    meet(gram_three, also=gram_role.sent)
    meet(gram_role, also=gram_three.sent)
    finish(vector)
    (ortho,) = muon(half_ns, *gram_role.result, role_low)
    ortho_came = swap(ortho, "dp", 0)
    meet(gram_three, also=ortho)
    finish(gram_three)
    iterate(0, gram_three.result)
    ortho_came, new_masters[0] = tie(ortho_came, new_masters[0])
    for kind in (2, 3):
        rows = moments[kind].shape[0] * ns_count
        step_scale = MUON_RATE * math.sqrt(max(1.0, rows / D))
        chosen = jnp.where(bit_of("dp", 0) == kind - 2, ortho, ortho_came).astype(jnp.float32)
        new_masters[kind] = masters[kind] * (1.0 - MUON_RATE * MUON_SHRINK) - step_scale * chosen
        copies[kind] = new_masters[kind].astype(low)
    vector_grad = vector.result.reshape(-1)[:vector_size]
    vector_first = BETA_ONE * vec_first + (1.0 - BETA_ONE) * vector_grad
    vector_second = BETA_TWO * vec_second + (1.0 - BETA_TWO) * vector_grad * vector_grad
    first_hat = vector_first / (1.0 - BETA_ONE**STEP)
    second_hat = vector_second / (1.0 - BETA_TWO**STEP)
    vector_new = vectors - ADAM_RATE * first_hat / (jnp.sqrt(second_hat) + 1e-08)
    return (
        out_patches,
        pooled_rows,
        patch_grad,
        grad_parts[0],
        grad_parts[1],
        grad_parts[2],
        grad_parts[3],
        moment_parts[0],
        moment_parts[1],
        moment_parts[2],
        moment_parts[3],
        new_masters[0],
        new_masters[1],
        new_masters[2],
        new_masters[3],
        *copies,
        vector_grad,
        vector_first,
        vector_second,
        vector_new,
    )


def solution(mesh):
    placed = (
        P(("dp", "ns"), None),
        P(("dp", "ns"), None),
        P(("dp", "ns"), None),
        P(("dp", "ns"), None),
        P(("dp", "ns"), None),
        P("ns", None),
        P("ns", None),
        P("ns", None),
        P("ns", None),
        P("ns", None),
        P("ns", None),
        P("ns", None),
        P("ns", None),
        P(),
        P(),
        P(),
    )
    return jax.shard_map(
        per_device,
        mesh=mesh,
        in_specs=placed,
        out_specs=(
            P(("dp", "ns"), None),
            P(("dp", "ns"), None),
            P(("dp", "ns"), None),
            P("ns", None),
            P("ns", None),
            P("ns", None),
            P("ns", None),
            P("ns", None),
            P("ns", None),
            P("ns", None),
            P("ns", None),
            P("ns", None),
            P("ns", None),
            P("ns", None),
            P("ns", None),
            P("ns", None),
            P("ns", None),
            P("ns", None),
            P("ns", None),
            P(),
            P(),
            P(),
            P(),
        ),
        check_vma=False,
    )
```

```python
import functools
import math

import jax
import jax.numpy as jnp
from jax import lax
from jax.experimental import pallas as pl
from jax.experimental.pallas import tpu as pltpu
from jax.sharding import PartitionSpec as P

D = 768
HD = 64
FF = 3072
ITERS = 4
STEP = 10


NS_A = 3.4445
NS_B = -4.775
NS_C = 2.0315
MUON_RATE = 0.8
MUON_DECAY = 0.5
MUON_SHRINK = 0.01
ADAM_RATE = 0.5
BETA_ONE = 0.9
BETA_TWO = 0.95
MASKED = -1e30


def owner_slots(owners_row, capacity):
    image_total = owners_row.shape[0]
    ordering = jnp.arange(image_total, dtype=jnp.int32)
    earlier = (owners_row[None, :] == owners_row[:, None]) & (ordering[None, :] < ordering[:, None])
    same_before = jnp.sum(earlier.astype(jnp.int32), axis=1)
    return owners_row * capacity + same_before


def exchange(value, axis, mask):
    count = lax.axis_size(axis)
    return lax.ppermute(value, axis, [(index, index ^ mask) for index in range(count)])


def swap(value, axis, bit):
    return exchange(value, axis, 1 << bit)


def step(value, axis, bit):
    return value, axis, (1 << bit,)


def bit_of(axis, bit):
    return (lax.axis_index(axis) >> bit) & 1


def bits_in(axis):
    return (lax.axis_size(axis) - 1).bit_length()


def tie(values, earlier):
    return lax.optimization_barrier((values, earlier))


def add_low(first, second):
    return (first.astype(jnp.float32) + second.astype(jnp.float32)).astype(jnp.bfloat16)


def halves(value, axis, bit, dim=0):
    mine = bit_of(axis, bit)
    shape = value.shape
    pairs = value.reshape(*shape[:dim], 2, shape[dim] // 2, *shape[dim + 1 :])
    keep = lax.dynamic_index_in_dim(pairs, mine, dim, keepdims=False)
    send = lax.dynamic_index_in_dim(pairs, 1 - mine, dim, keepdims=False)
    return keep, send


def joined(value, other, axis, bit, dim=0):
    mine = bit_of(axis, bit)
    low_half = jnp.where(mine == 0, value, other)
    high_half = jnp.where(mine == 0, other, value)
    return jnp.concatenate([low_half, high_half], axis=dim)


class Chain:
    def __init__(self, steps):
        self.steps = steps
        self.result = None
        self.advance(None)

    def advance(self, came):
        try:
            self.sent, axis, masks, *self.held = self.steps.send(came)
            self.pending = tuple(exchange(self.sent, axis, mask) for mask in masks)
        except StopIteration as stop:
            self.sent = self.pending = None
            self.result = stop.value


def meet(*chains, also=()):
    live = [chain for chain in chains if chain.pending is not None]
    cames, also = lax.optimization_barrier((tuple(chain.pending for chain in live), also))
    for chain, came in zip(live, cames):
        chain.advance(came if len(came) > 1 else came[0])
    return also


def finish(*chains):
    while any(chain.pending is not None for chain in chains):
        meet(*chains)


def rest_of_dp(value, dim, split):
    value = yield from rest_summed(value, dim, split)
    other = yield step(value, "dp", 0)
    return value, other


def rest_summed(value, dim, split):
    first = 1
    split = split and bits_in("dp") > 2
    if split:
        keep, send = halves(value, "dp", 1, dim)
        value = add_low(keep, (yield step(send, "dp", 1)))
        first = 2
    for bit in range(first, bits_in("dp")):
        value = add_low(value, (yield step(value, "dp", bit)))
    if split:
        value = joined(value, (yield step(value, "dp", 1)), "dp", 1, dim)
    return value


def swap_roles(up, down):
    first_role = bit_of("dp", 0) == 0
    mine, theirs = jnp.where(first_role, up, down), jnp.where(first_role, down, up)
    first = yield (*step(theirs, "dp", 0), "first")
    held = (mine, first)
    second = yield (*step(tie(mine, first)[0], "dp", 0), held)
    return first, second


def sum_up(kept, sent):
    value = add_low(kept, (yield step(sent, "ns", 1)))
    keep, send = halves(value, "dp", 0)
    return add_low(keep, (yield step(send, "dp", 0)))


def sum_down(kept, sent):
    keep, send = halves(jnp.stack([kept, sent]), "dp", 0, 1)
    value = add_low(keep, (yield step(send, "dp", 0)))
    return add_low(value[0], (yield step(value[1], "ns", 1)))


def sum_blocks(value, split):
    for bit in range(bits_in("ns")):
        mine = bit_of("ns", bit)
        pairs = value.reshape(value.shape[0] // 2, 2, *value.shape[1:])
        keep = lax.dynamic_index_in_dim(pairs, mine, 1, keepdims=False)
        send = lax.dynamic_index_in_dim(pairs, 1 - mine, 1, keepdims=False)
        value = add_low(keep, (yield step(send, "ns", bit)))
    keep, send = halves(value[0], "dp", 0)
    value = add_low(keep, (yield step(send, "dp", 0)))
    return (yield from rest_of_dp(value, 0, split))


def sum_vector(value):
    for axis in ("ns", "dp"):
        for bit in range(0, bits_in(axis), 2):
            masks = [1 << bit]
            if bit + 1 < bits_in(axis):
                masks += [2 << bit, 3 << bit]
            came = yield value, axis, masks
            if len(masks) == 1:
                value = value + came
            else:
                value = (value + came[0]) + (came[1] + came[2])
    return value


def sum_gram(gram):
    gram = gram + (yield step(gram, "ns", 0))
    keep, _ = halves(gram, "ns", 0)
    for bit in range(1, bits_in("ns")):
        keep = keep + (yield step(keep, "ns", bit))
    other = yield step(keep, "ns", 0)
    return (keep[None], 0), (other[None], 0)


def by_distance(table):
    place = lax.axis_index("ns")
    return [
        lax.dynamic_index_in_dim(table, place ^ distance, 0, keepdims=True)
        for distance in range(table.shape[0])
    ]


def dot32(first, second):
    return jnp.dot(first, second, preferred_element_type=jnp.float32)


LOW = jnp.bfloat16
F32 = jnp.float32
HEADS = D // HD
BIG = 576
SMALL = 64
TILE = 256
MIB = 1024 * 1024
COST_SCALE = 1e9


def mm(first, second, first_dim=1, second_dim=0):
    return lax.dot_general(
        first,
        second,
        (((first_dim,), (second_dim,)), ((), ())),
        preferred_element_type=F32,
    )


def split_value(value):
    high = value.astype(LOW)
    return high, (value - high.astype(F32)).astype(LOW)


def normalise(values):
    row_mean = jnp.mean(values, axis=-1, keepdims=True)
    centred = values - row_mean
    scale = lax.rsqrt(jnp.mean(centred * centred, axis=-1, keepdims=True) + 1e-06)
    return centred * scale, scale


def norm_back(unit, scale, unit_grad):
    return scale * (
        unit_grad
        - jnp.mean(unit_grad, axis=-1, keepdims=True)
        - unit * jnp.mean(unit_grad * unit, axis=-1, keepdims=True)
    )


def column_sum(values):
    return jnp.sum(values, axis=0, keepdims=True)


def params(mebibytes):
    return pltpu.CompilerParams(vmem_limit_bytes=mebibytes * MIB)


def cost(micros, nbytes):
    return pl.CostEstimate(flops=int(micros * COST_SCALE), bytes_accessed=int(nbytes * COST_SCALE * 1e-9), transcendentals=0)


def whole(shape):
    return pl.BlockSpec(shape, lambda *_: (0,) * len(shape))


def once(shape):
    return pl.BlockSpec(shape, lambda *_: (0,) * len(shape), pipeline_mode=pl.Buffered(1))


def rows_of(width, tile=TILE):
    return pl.BlockSpec((tile, width), lambda i, *_: (i, 0))


def lanes_of(height, tile=TILE):
    return pl.BlockSpec((height, tile), lambda i, *_: (0, i))


STARTS = {}
WIDTHS = dict(gain_one=D, bias_one=D, bias_qkv=3 * D, gain_query=HD, bias_query=HD, gain_key=HD,
              bias_out=D, gain_two=D, bias_two=D, bias_up=FF, bias_down=D)
for part_name, part_width in WIDTHS.items():
    STARTS[part_name] = sum(WIDTHS[other] for other in STARTS)


def vector_row(ref, name):
    start = STARTS[name]
    return ref[:, start : start + WIDTHS[name]]


def to_column(row):
    return jnp.broadcast_to(row, (8, row.shape[1])).T[:, :1]


def to_row(column):
    return jnp.broadcast_to(column, (column.shape[0], 128)).T[:1]


def qkv_part(block):
    return pl.BlockSpec(
        (block.shape[0] - out_rows(block), D), lambda *_: (0, 0), pipeline_mode=pl.Buffered(1)
    )


def out_part(block):
    return pl.BlockSpec((out_rows(block), D), lambda *_: (3, 0), pipeline_mode=pl.Buffered(1))


def out_rows(block):
    return block.shape[0] // 4


def place_blocks(place_ref, refs, store):
    rows = refs[0].shape[0]
    for distance, ref in enumerate(refs):
        start = pl.multiple_of((place_ref[0] ^ distance) * rows, rows)
        store[pl.ds(start, rows), :] = ref[...]


def shape_of(shape, dtype):
    return jax.ShapeDtypeStruct(shape, dtype)


def project_kernel(place_ref, x_ref, w0, w1, w2, w3, vec_ref,
                   h_ref, qkv_ref, unit_ref, scale_ref, w_s, col_s):
    @pl.when(pl.program_id(0) == 0)
    def _():
        place_blocks(place_ref, (w0, w1, w2, w3), w_s)
        start = STARTS["bias_qkv"]
        row = vec_ref[:, start : start + 3 * D + 256]
        col_s[...] = to_column(row)

    unit, _ = normalise(x_ref[...].astype(F32))
    h_low = (unit * vector_row(vec_ref, "gain_one") + vector_row(vec_ref, "bias_one")).astype(LOW)
    h_ref[...] = h_low
    gain_q = col_s[pl.ds(3 * D, HD), :]
    bias_q = col_s[pl.ds(3 * D + HD, HD), :]
    gain_k = col_s[pl.ds(3 * D + 2 * HD, HD), :]
    for part in range(3):
        rows = pl.ds(part * D, D)
        value = mm(w_s[rows, :], h_low, 1, 1) + col_s[rows, :]
        if part == 2:
            qkv_ref[2] = value.astype(LOW)
            continue
        heads = value.reshape(HEADS, HD, value.shape[1])
        centred = heads - jnp.mean(heads, axis=1, keepdims=True)
        scale = lax.rsqrt(jnp.mean(centred * centred, axis=1, keepdims=True) + 1e-06)
        unit_heads = centred * scale
        scale_ref[part] = scale
        unit_ref[part] = unit_heads.reshape(D, -1).astype(LOW)
        if part == 0:
            result = unit_heads * gain_q[None] + bias_q[None]
            result = result.astype(LOW) * LOW(0.125)
        else:
            result = (unit_heads * gain_k[None]).astype(LOW)
        qkv_ref[part] = result.reshape(D, -1)


def project(place, patches, w_blocks, vectors):
    slots = patches.shape[0]
    return pl.pallas_call(
        project_kernel,
        grid_spec=pltpu.PrefetchScalarGridSpec(
            num_scalar_prefetch=1,
            grid=(slots // TILE,),
            in_specs=[rows_of(D)] + [qkv_part(w_blocks[0])] * 4 + [once(vectors.shape)],
            out_specs=[rows_of(D),
                       pl.BlockSpec((3, D, TILE), lambda i, p: (0, 0, i)),
                       pl.BlockSpec((2, D, TILE), lambda i, p: (0, 0, i)),
                       pl.BlockSpec((2, HEADS, 1, TILE), lambda i, p: (0, 0, 0, i))],
            scratch_shapes=[pltpu.VMEM((3 * D, D), LOW), pltpu.VMEM((3 * D + 256, 1), F32)],
        ),
        out_shape=[shape_of((slots, D), LOW), shape_of((3, D, slots), LOW),
                   shape_of((2, D, slots), LOW), shape_of((2, HEADS, 1, slots), F32)],
        compiler_params=params(24),
        cost_estimate=cost(10, 16e6),
        name="project",
    )(place, patches, *w_blocks, vectors)


def used_slots(counts_ref):
    total = counts_ref[0]
    for k in range(1, counts_ref.shape[0]):
        total = total + counts_ref[k]
    return total


def pair_mask(tile_start, used, has_big):
    same = (has_big & (tile_start + SMALL < BIG)) | (tile_start >= used)
    row_half = lax.broadcasted_iota(jnp.int32, (128, 128), 0) // SMALL
    column_half = lax.broadcasted_iota(jnp.int32, (128, 128), 1) // SMALL
    return (row_half == column_half) | same


def soft_columns(scores):
    peak = jnp.max(scores, axis=0, keepdims=True)
    exponent = jnp.exp(scores - peak)
    total = jnp.sum(exponent, axis=0, keepdims=True)
    return exponent.astype(LOW), total, peak + jnp.log(total)


def pair_mask_row(slots, used, has_big):
    row_half = lax.broadcasted_iota(jnp.int32, (128, slots), 0) // SMALL
    slot = lax.broadcasted_iota(jnp.int32, (128, slots), 1)
    column_half = slot // SMALL % 2
    start = slot // 128 * 128
    same = (has_big & (start + SMALL < BIG)) | (start >= used)
    return (row_half == column_half) | same


def attend_kernel(group, counts_ref, qkv_ref, out_ref, log_ref):
    used = used_slots(counts_ref)
    has_big = counts_ref[0] == BIG
    slots = out_ref.shape[1]
    heads = [pl.ds(index * HD, HD) for index in range(group)]

    def narrow(first, last):
        tiles = [slice(start, start + 128) for start in range(first, last, 128)]
        mask = pair_mask_row(slots, used, has_big)[:, first:last]
        span = slice(first, last)
        all_scores = []
        for rows in heads:
            all_scores.append(jnp.concatenate(
                [mm(qkv_ref[1, rows, tile], qkv_ref[0, rows, tile], 0, 0) for tile in tiles], axis=1
            ))
        for index, rows in enumerate(heads):
            scores = jnp.where(mask, all_scores[index], MASKED)
            weights, total, log_total = soft_columns(scores)
            result = jnp.concatenate(
                [mm(qkv_ref[2, rows, tile], weights[:, tile.start - first : tile.stop - first])
                 for tile in tiles], axis=1
            )
            out_ref[rows, span] = (result / total).astype(LOW)
            log_ref[index, :, span] = log_total

    @pl.when(jnp.logical_not(has_big))
    def _():
        narrow(0, 512)

    narrow(512, slots)

    @pl.when(has_big)
    def _():
        for start, width in ((0, 256), (256, 256), (512, 128)):
            span = pl.ds(start, width)
            all_scores = [
                mm(qkv_ref[1, rows, 0:640], qkv_ref[0, rows, span], 0, 0)[:BIG] for rows in heads
            ]
            for index, rows in enumerate(heads):
                weights, total, log_total = soft_columns(all_scores[index])
                weights = jnp.concatenate([weights, jnp.zeros((640 - BIG, width), LOW)], axis=0)
                result = mm(qkv_ref[2, rows, 0:640], weights) / total
                if width == 128:
                    lane = lax.broadcasted_iota(jnp.int32, (1, width), 1)
                    inside = lane < BIG - start
                    result = jnp.where(inside, result, out_ref[rows, span].astype(F32))
                    log_total = jnp.where(inside, log_total, log_ref[index, :, span])
                out_ref[rows, span] = result.astype(LOW)
                log_ref[index, :, span] = log_total

    for first in range(0, slots - 128, 256):

        @pl.when((used >= first) & (used < first + 256) & (used < slots - 128))
        def _():
            def columns(chunk, carry):
                span = pl.ds(pl.multiple_of(chunk * 256, 256), 256)
                slot = chunk * 256 + lax.broadcasted_iota(jnp.int32, (1, 256), 1)
                inside = slot >= used
                key_slot = first + lax.broadcasted_iota(jnp.int32, (256, 256), 0)
                all_scores = [
                    mm(qkv_ref[1, rows, first:slots], qkv_ref[0, rows, span], 0, 0)
                    for rows in heads
                ]
                for index, rows in enumerate(heads):
                    scores = all_scores[index]
                    top = jnp.where(key_slot >= used, scores[:256], MASKED)
                    if slots - first > 256:
                        top = jnp.concatenate([top, scores[256:]], axis=0)
                    weights, total, log_total = soft_columns(top)
                    result = mm(qkv_ref[2, rows, first:slots], weights) / total
                    old = out_ref[rows, span].astype(F32)
                    out_ref[rows, span] = jnp.where(inside, result, old).astype(LOW)
                    log_ref[index, :, span] = jnp.where(inside, log_total, log_ref[index, :, span])
                return carry

            lax.fori_loop(first // 256, slots // 256, columns, 0)


def attend(counts, qkv, group=12):
    slots = qkv.shape[2]
    return pl.pallas_call(
        functools.partial(attend_kernel, group),
        grid_spec=pltpu.PrefetchScalarGridSpec(
            num_scalar_prefetch=1,
            grid=(HEADS // group,),
            in_specs=[pl.BlockSpec((3, group * HD, slots), lambda h, c: (0, h, 0))],
            out_specs=[pl.BlockSpec((group * HD, slots), lambda h, c: (h, 0)),
                       pl.BlockSpec((group, 1, slots), lambda h, c: (h, 0, 0))],
        ),
        out_shape=[shape_of((D, slots), LOW), shape_of((HEADS, 1, slots), F32)],
        compiler_params=params(46),
        cost_estimate=cost(28, 7000000.0),
        name="attend",
    )(counts, qkv)


def attend_back_kernel(group, counts_ref, qkv_ref, attn_ref, log_ref, grad_ref, unit_ref,
                       scale_ref, vec_ref, h_ref, *refs):
    dqkv_ref, bias_ref, gains_ref, grad_w_ref, dq_s, dk_s, dv_s = refs[-7:]
    used = used_slots(counts_ref)
    has_big = counts_ref[0] == BIG
    slots = attn_ref.shape[1]
    start = STARTS["gain_query"]
    columns = to_column(vec_ref[:, start : start + 256])
    gain_q, gain_k = columns[:HD], columns[2 * HD : 3 * HD]

    @pl.when(pl.program_id(0) == 0)
    def _():
        gains_ref[...] = jnp.zeros_like(gains_ref)

    def head_rows(index):
        return pl.ds(index * HD, HD)

    def delta_of(index, span):
        return column_sum(
            grad_ref[head_rows(index), span].astype(F32)
            * attn_ref[head_rows(index), span].astype(F32)
        )

    def narrow(first, last):
        tiles = [slice(start, start + 128) for start in range(first, last, 128)]
        mask = pair_mask_row(slots, used, has_big)[:, first:last]
        span = slice(first, last)

        def wide(product):
            return jnp.concatenate([product(tile) for tile in tiles], axis=1)

        def inner(tile):
            return slice(tile.start - first, tile.stop - first)

        all_scores, all_grads = [], []
        for index in range(group):
            rows = head_rows(index)
            all_scores.append(wide(
                lambda tile: mm(qkv_ref[1, rows, tile], qkv_ref[0, rows, tile], 0, 0)))
            all_grads.append(wide(
                lambda tile: mm(qkv_ref[2, rows, tile], grad_ref[rows, tile], 0, 0)))
        for index in range(group):
            rows = head_rows(index)
            scores = all_scores[index] - log_ref[index, :, span]
            probs = jnp.exp(jnp.where(mask, scores, MASKED))
            score_low = (probs * (all_grads[index] - delta_of(index, span))).astype(LOW)
            probs_low = probs.astype(LOW)
            dv_s[rows, span] = wide(
                lambda tile: mm(grad_ref[rows, tile], probs_low[:, inner(tile)], 1, 1))
            dk_s[rows, span] = wide(
                lambda tile: mm(qkv_ref[0, rows, tile], score_low[:, inner(tile)], 1, 1))
            dq_s[rows, span] = wide(
                lambda tile: mm(qkv_ref[1, rows, tile], score_low[:, inner(tile)]))

    @pl.when(jnp.logical_not(has_big))
    def _():
        narrow(0, 512)

    @pl.when(used > 512)
    def _():
        narrow(512, slots)

    @pl.when(used <= 512)
    def _():
        for store in (dq_s, dk_s, dv_s):
            store[:, 512:slots] = jnp.zeros((store.shape[0], slots - 512), F32)

    @pl.when(has_big)
    def _():
        wide = pl.ds(0, 640)
        dk = [jnp.zeros((HD, 640), F32)] * group
        dv = [jnp.zeros((HD, 640), F32)] * group
        for start, width in ((0, 256), (256, 256), (512, 128)):
            span = pl.ds(start, width)
            lane = lax.broadcasted_iota(jnp.int32, (1, width), 1)
            all_scores, all_grads = [], []
            for index in range(group):
                rows = head_rows(index)
                all_scores.append(mm(qkv_ref[1, rows, wide], qkv_ref[0, rows, span], 0, 0)[:BIG])
                all_grads.append(mm(qkv_ref[2, rows, wide], grad_ref[rows, span], 0, 0)[:BIG])
            for index in range(group):
                rows = head_rows(index)
                probs = jnp.exp(all_scores[index] - log_ref[index, :, span])
                if width == 128:
                    probs = jnp.where(lane < BIG - start, probs, 0.0)
                score_low = (probs * (all_grads[index] - delta_of(index, span))).astype(LOW)
                blank = jnp.zeros((640 - BIG, width), LOW)
                score_low = jnp.concatenate([score_low, blank], axis=0)
                probs_low = jnp.concatenate([probs.astype(LOW), blank], axis=0)
                dv[index] = dv[index] + mm(grad_ref[rows, span], probs_low, 1, 1)
                dk[index] = dk[index] + mm(qkv_ref[0, rows, span], score_low, 1, 1)
                dq = mm(qkv_ref[1, rows, wide], score_low)
                if width == 128:
                    dq = jnp.where(lane < BIG - start, dq, dq_s[rows, span])
                dq_s[rows, span] = dq
        inside = lax.broadcasted_iota(jnp.int32, (1, 640), 1) < BIG
        for index in range(group):
            rows = head_rows(index)
            dk_s[rows, wide] = jnp.where(inside, dk[index], dk_s[rows, wide])
            dv_s[rows, wide] = jnp.where(inside, dv[index], dv_s[rows, wide])

    sums = [jnp.zeros((HD, 1), F32)] * 3
    biases = [[], [], []]
    for index in range(group):
        rows = head_rows(index)
        for part, store, gain in ((0, dq_s, gain_q), (1, dk_s, gain_k)):
            unit = unit_ref[part, rows, :].astype(F32)
            grad = store[rows, :]
            if part == 0:
                grad = grad * 0.125
                sums[0] = sums[0] + jnp.sum(grad * unit, axis=1, keepdims=True)
                sums[1] = sums[1] + jnp.sum(grad, axis=1, keepdims=True)
            else:
                sums[2] = sums[2] + jnp.sum(grad * unit, axis=1, keepdims=True)
            unit_grad = grad * gain
            result = scale_ref[part, index] * (
                unit_grad
                - jnp.mean(unit_grad, axis=0, keepdims=True)
                - unit * jnp.mean(unit_grad * unit, axis=0, keepdims=True)
            )
            result = result.astype(LOW)
            dqkv_ref[part, rows, :] = result
            biases[part].append(jnp.sum(result.astype(F32), axis=1, keepdims=True))
        result = dv_s[rows, :].astype(LOW)
        dqkv_ref[2, rows, :] = result
        biases[2].append(jnp.sum(result.astype(F32), axis=1, keepdims=True))
    for part in range(3):
        grad_w_ref[part] = mm(dqkv_ref[part], h_ref[...]).astype(LOW)
        bias_ref[part] = to_row(jnp.concatenate(biases[part], axis=0))
    blank = jnp.zeros((HD, 1), F32)
    gains_ref[:, 0:128] += to_row(jnp.concatenate(sums[:2], axis=0))
    gains_ref[:, 128:256] += to_row(jnp.concatenate([sums[2], blank], axis=0))


def attend_back(counts, qkv, attn, log_total, attn_grad, unit, scale, vectors, h, earlier, half,
                group=2):
    slots = qkv.shape[2]
    steps = HEADS // group // 2
    first = half * steps
    head_block = pl.BlockSpec((group * HD, slots), lambda h, c: (h + first, 0))
    dqkv_block = pl.BlockSpec((3, group * HD, slots), lambda h, c: (0, h + first, 0))
    held = pl.BlockSpec(memory_space=pl.ANY)
    grad_block = pl.BlockSpec((3, group * HD, D), lambda h, c: (0, h + first, 0))
    return pl.pallas_call(
        functools.partial(attend_back_kernel, group),
        grid_spec=pltpu.PrefetchScalarGridSpec(
            num_scalar_prefetch=1,
            grid=(steps,),
            in_specs=[dqkv_block,
                      head_block,
                      pl.BlockSpec((group, 1, slots), lambda h, c: (h + first, 0, 0)),
                      head_block,
                      pl.BlockSpec((2, group * HD, slots), lambda h, c: (0, h + first, 0)),
                      pl.BlockSpec((2, group, 1, slots), lambda h, c: (0, h + first, 0, 0)),
                      whole(vectors.shape), once(h.shape)] + [held] * len(earlier),
            out_specs=[dqkv_block,
                       pl.BlockSpec((3, 1, group * HD), lambda h, c: (0, 0, h)),
                       whole((1, 256)), grad_block],
            scratch_shapes=[pltpu.VMEM((group * HD, slots), F32)] * 3,
        ),
        out_shape=[shape_of((3, D, slots), LOW), shape_of((3, 1, D // 2), F32),
                   shape_of((1, 256), F32), shape_of((3, D, D), LOW)],
        input_output_aliases={9: 0, 10: 3} if earlier else {},
        compiler_params=params(60),
        cost_estimate=cost(2.0, 8e6),
        name="attend_back",
    )(counts, qkv, attn, log_total, attn_grad, unit, scale, vectors, h, *earlier)


def segment_picker(counts_ref, first, width):
    images = counts_ref.shape[0]
    slot = first + lax.broadcasted_iota(jnp.int32, (images, width), 1)
    image = lax.broadcasted_iota(jnp.int32, (images, width), 0)
    start = jnp.int32(0)
    picked = jnp.zeros((images, width), jnp.bool_)
    for k in range(images):
        end = start + counts_ref[k]
        picked = picked | ((image == k) & (slot >= start) & (slot < end))
        start = end
    return picked.astype(F32), start


def image_sizes(counts_ref):
    images = counts_ref.shape[0]
    image = lax.broadcasted_iota(jnp.int32, (images, 1), 0)
    sizes = jnp.zeros((images, 1), F32)
    for k in range(images):
        sizes = jnp.where(image == k, jnp.maximum(counts_ref[k], 1).astype(F32), sizes)
    return sizes


def middle_kernel(counts_ref, place_ref, x_ref, attn_ref, w0, w1, w2, w3, vec_ref, cot_ref,
                  image_ref, x2_ref, h_ref, dy_ref, mix_ref, w_s):
    @pl.when(pl.program_id(0) == 0)
    def _():
        place_blocks(place_ref, (w0, w1, w2, w3), w_s)

    x2 = x_ref[...].astype(F32) + mm(attn_ref[...], w_s[...], 0, 1) + vector_row(vec_ref, "bias_out")
    x2_ref[...] = x2
    unit, _ = normalise(x2)
    h_ref[...] = (
        unit * vector_row(vec_ref, "gain_two") + vector_row(vec_ref, "bias_two")
    ).astype(LOW)
    tile = x_ref.shape[0]
    first = pl.program_id(0) * tile
    picker, used = segment_picker(counts_ref, first, tile)
    picker = picker.astype(LOW)
    image_grad = image_ref[...].astype(F32) / image_sizes(counts_ref)
    dy = jnp.zeros(x2.shape, F32)
    rest = image_grad
    for _ in range(3):
        high, rest = split_value32(rest)
        dy = dy + mm(picker, high, 0, 0)
    slot = first + lax.broadcasted_iota(jnp.int32, (tile, 1), 0)
    dy = dy + jnp.where(slot < used, cot_ref[...].astype(F32), 0.0)
    dy_ref[...] = dy
    mix_ref[...] = dy.astype(LOW)


def split_value32(value):
    high = value.astype(LOW)
    return high, value - high.astype(F32)


def middle(counts, place, patches, attn, w_blocks, vectors, patch_cot, image_cot):
    slots = patches.shape[0]
    images = counts.shape[0]
    return pl.pallas_call(
        middle_kernel,
        grid_spec=pltpu.PrefetchScalarGridSpec(
            num_scalar_prefetch=2,
            grid=(slots // TILE,),
            in_specs=[rows_of(D), lanes_of(D)] + [out_part(w_blocks[0])] * 4
            + [whole(vectors.shape), rows_of(D), whole((images, D))],
            out_specs=[rows_of(D)] * 4,
            scratch_shapes=[pltpu.VMEM((D, D), LOW)],
        ),
        out_shape=[shape_of((slots, D), F32), shape_of((slots, D), LOW),
                   shape_of((slots, D), F32), shape_of((slots, D), LOW)],
        compiler_params=params(20),
        cost_estimate=cost(9, 20e6),
        name="middle",
    )(counts, place, patches, attn, *w_blocks, vectors, patch_cot, image_cot)


def feed_kernel(distances, start_y, y_in_ref, dh_in_ref, h_ref, mix_ref, up_a, down_a, up_b,
                down_b, bias_ref, vec_ref,
                y_ref, dh_ref, grad_a, grad_b, bias_grad_a, bias_grad_b):
    @pl.when(pl.program_id(0) == 0)
    def _():
        if start_y:
            y_ref[...] = y_in_ref[...] + vector_row(vec_ref, "bias_down")
            dh_ref[...] = jnp.zeros_like(dh_ref)
        else:
            y_ref[...] = y_in_ref[...]
            dh_ref[...] = dh_in_ref[...]

    slots = h_ref.shape[0]
    for distance, up_ref, down_ref, grad_ref, bias_grad_ref in (
        (distances[0], up_a, down_a, grad_a, bias_grad_a),
        (distances[1], up_b, down_b, grad_b, bias_grad_b),
    ):
        up, down = up_ref[...], down_ref[...]
        h, mix = h_ref[...], mix_ref[...]
        u = mm(up, h, 1, 1) + to_column(bias_ref[distance : distance + 1])
        back = mm(down, mix, 1, 1)
        gate = 0.5 * (1.0 + lax.erf(u * (0.5**0.5)))
        slope = gate + u * (jnp.exp(-0.5 * u * u) * ((0.5 / math.pi) ** 0.5))
        hidden = (u * gate).astype(LOW)
        pre = (back * slope).astype(LOW)
        y_ref[...] += mm(hidden, down, 0, 0)
        dh_ref[...] += mm(pre, up, 0, 0)
        grad_up = mm(pre, h)
        grad_down = mm(hidden, mix)
        bias_grad = to_row(jnp.sum(pre.astype(F32), axis=1, keepdims=True))
        grad_ref[0] = grad_up.astype(LOW)
        grad_ref[1] = grad_down.astype(LOW)
        bias_grad_ref[...] = bias_grad


def feed(distances, y, dh2, h2, mix, pair_a, pair_b, bias_table, vectors, block=256):
    slots = y.shape[0]
    units = pair_a.shape[1]
    start_y = dh2 is None
    if start_y:
        dh2 = y
    up = pl.BlockSpec((None, block, D), lambda i: (0, i, 0))
    down = pl.BlockSpec((None, block, D), lambda i: (1, i, 0))
    bias = pl.BlockSpec((1, block), lambda i: (0, i))
    both = pl.BlockSpec((2, block, D), lambda i: (0, i, 0))
    dh_spec = pl.BlockSpec((8, D), lambda i: (0, 0)) if start_y else once((slots, D))
    return pl.pallas_call(
        functools.partial(feed_kernel, distances, start_y),
        grid=(units // block,),
        in_specs=[once((slots, D)), dh_spec, once((slots, D)), once((slots, D)),
                  up, down, up, down, pl.BlockSpec((bias_table.shape[0], block), lambda i: (0, i)),
                  whole(vectors.shape)],
        out_specs=[once((slots, D)), once((slots, D)), both, both, bias, bias],
        out_shape=[shape_of((slots, D), F32), shape_of((slots, D), F32),
                   shape_of((2, units, D), LOW), shape_of((2, units, D), LOW),
                   shape_of((1, units), F32), shape_of((1, units), F32)],
        compiler_params=params(26),
        cost_estimate=cost(24, 25e6),
        name="feed",
    )(y, dh2, h2, mix, pair_a, pair_a, pair_b, pair_b, bias_table, vectors)


def after_kernel(counts_ref, place_ref, y_ref, x2_ref, dh_ref, dy_ref, attn_ref, w0, w1, w2, w3,
                 vec_ref, out_ref, pooled_ref, dx2_ref, dattn_ref, grad_out_ref, sums_ref,
                 pool_s, grad_s, w_s):
    step = pl.program_id(0)

    @pl.when(step == 0)
    def _():
        pool_s[...] = jnp.zeros_like(pool_s)
        grad_s[...] = jnp.zeros_like(grad_s)
        sums_ref[...] = jnp.zeros_like(sums_ref)
        place_blocks(place_ref, (w0, w1, w2, w3), w_s)

    y = y_ref[...]
    tile = y.shape[0]
    out_ref[...] = y.astype(LOW)
    picker, _ = segment_picker(counts_ref, step * tile, tile)
    picker = picker.astype(LOW)
    rest = y
    pooled = pool_s[...]
    for _ in range(3):
        high, rest = split_value32(rest)
        pooled = pooled + mm(picker, high)
    pool_s[...] = pooled
    pooled_ref[...] = (pooled / image_sizes(counts_ref)).astype(LOW)
    unit, scale = normalise(x2_ref[...])
    dh = dh_ref[...]
    sums_ref[0:1] += column_sum(dh * unit)
    sums_ref[1:2] += column_sum(dh)
    dy = dy_ref[...]
    sums_ref[3:4] += column_sum(dy.astype(LOW).astype(F32))
    dx2 = dy + norm_back(unit, scale, dh * vector_row(vec_ref, "gain_two"))
    dx2_ref[...] = dx2
    da = dx2.astype(LOW)
    sums_ref[2:3] += column_sum(da.astype(F32))
    dattn_ref[...] = mm(w_s[...], da, 0, 1).astype(LOW)
    grad = grad_s[...] + mm(da, attn_ref[...], 0, 1)
    grad_s[...] = grad
    grad_out_ref[...] = grad.astype(LOW)


def after(counts, place, y, x2, dh2, dy, attn, w_blocks, vectors):
    slots = y.shape[0]
    images = counts.shape[0]
    return pl.pallas_call(
        after_kernel,
        grid_spec=pltpu.PrefetchScalarGridSpec(
            num_scalar_prefetch=2,
            grid=(slots // TILE,),
            in_specs=[rows_of(D), rows_of(D), rows_of(D), rows_of(D), lanes_of(D)]
            + [out_part(w_blocks[0])] * 4 + [whole(vectors.shape)],
            out_specs=[rows_of(D), whole((images, D)), rows_of(D), lanes_of(D), whole((D, D)),
                       whole((8, D))],
            scratch_shapes=[pltpu.VMEM((images, D), F32), pltpu.VMEM((D, D), F32),
                            pltpu.VMEM((D, D), LOW)],
        ),
        out_shape=[shape_of((slots, D), LOW), shape_of((images, D), LOW),
                   shape_of((slots, D), F32), shape_of((D, slots), LOW), shape_of((D, D), LOW),
                   shape_of((8, D), F32)],
        compiler_params=params(60),
        cost_estimate=cost(4.0, 25e6),
        name="after",
    )(counts, place, y, x2, dh2, dy, attn, *w_blocks, vectors)


def first_back_kernel(place_ref, x_ref, dqkv_ref, w0, w1, w2, w3, vec_ref, dx2_ref,
                      out_ref, sums_ref, w_s):
    @pl.when(pl.program_id(0) == 0)
    def _():
        sums_ref[...] = jnp.zeros_like(sums_ref)
        place_blocks(place_ref, (w0, w1, w2, w3), w_s)

    dh = mm(dqkv_ref[...], w_s[...], 0, 0)
    unit, scale = normalise(x_ref[...].astype(F32))
    sums_ref[0:1] += column_sum(dh * unit)
    sums_ref[1:2] += column_sum(dh)
    out_ref[...] = dx2_ref[...] + norm_back(unit, scale, dh * vector_row(vec_ref, "gain_one"))


def first_back(place, patches, dqkv, w_blocks, vectors, dx2):
    slots = patches.shape[0]
    return pl.pallas_call(
        first_back_kernel,
        grid_spec=pltpu.PrefetchScalarGridSpec(
            num_scalar_prefetch=1,
            grid=(slots // TILE,),
            in_specs=[rows_of(D), lanes_of(3 * D)] + [qkv_part(w_blocks[0])] * 4
            + [whole(vectors.shape), rows_of(D)],
            out_specs=[rows_of(D), whole((8, D))],
            scratch_shapes=[pltpu.VMEM((3 * D, D), LOW)],
        ),
        out_shape=[shape_of((slots, D), F32), shape_of((8, D), F32)],
        compiler_params=params(22),
        cost_estimate=cost(0.2, 17e6),
        name="first_back",
    )(place, patches, dqkv, *w_blocks, vectors, dx2)


SIDE = 256
GRID_BLOCKS = [(i, j) for i in range(D // SIDE) for j in range(i, D // SIDE)]


def moment_kernel(half_ref, own_ref, other_ref, mom_ref, grad_ref, moment_ref, gram_ref):
    rows = own_ref.shape[0]
    for ref, place in ((own_ref, half_ref[0]), (other_ref, 1 - half_ref[0])):
        span = pl.ds(pl.multiple_of(place * rows, rows), rows)
        grad = ref[...].astype(F32)
        grad_ref[span, :] = grad
        moment_ref[span, :] = MUON_DECAY * mom_ref[span, :] + grad
    moment_low = moment_ref[...].astype(LOW)
    for index, (i, j) in enumerate(GRID_BLOCKS):
        gram_ref[index] = mm(
            moment_low[:, i * SIDE : (i + 1) * SIDE], moment_low[:, j * SIDE : (j + 1) * SIDE], 0, 0
        )


def role_kernel(half_ref, own_ref, other_ref, mom_ref, low_ref, gram_ref):
    rows = own_ref.shape[0]
    for ref, place in ((own_ref, half_ref[0]), (other_ref, 1 - half_ref[0])):
        span = pl.ds(pl.multiple_of(place * rows, rows), rows)
        low_ref[span, :] = (MUON_DECAY * mom_ref[span, :] + ref[...].astype(F32)).astype(LOW)
    moment_low = low_ref[...]
    for index, (i, j) in enumerate(GRID_BLOCKS):
        gram_ref[index] = mm(
            moment_low[:, i * SIDE : (i + 1) * SIDE], moment_low[:, j * SIDE : (j + 1) * SIDE], 0, 0
        )


def role_gram(half, own, other, mom):
    rows = mom.shape[0]
    blocks = len(GRID_BLOCKS)
    out_shape = [shape_of((rows, D), LOW), shape_of((blocks, SIDE, SIDE), F32)]
    return pl.pallas_call(
        role_kernel,
        grid=(1,),
        in_specs=[pl.BlockSpec(memory_space=pltpu.SMEM), once(own.shape), once(other.shape),
                  once((rows, D))],
        out_specs=[once(leaf.shape) for leaf in out_shape],
        out_shape=out_shape,
        compiler_params=params(16),
        cost_estimate=cost(0.5, rows * D * 8 + blocks * SIDE * SIDE * 4),
        name="role_gram",
    )(half, own, other, mom)


def record_kernel(kind, half_ref, own_ref, first_ref, second_ref, mom_ref, grad_ref, moment_ref):
    rows = own_ref.shape[0]

    def put(ref, place):
        span = pl.ds(pl.multiple_of(place * rows, rows), rows)
        grad = ref[...].astype(F32)
        grad_ref[span, :] = grad
        moment_ref[span, :] = MUON_DECAY * mom_ref[span, :] + grad

    put(own_ref, half_ref[0])

    @pl.when(half_ref[0] == kind)
    def _():
        put(first_ref, 1 - half_ref[0])

    @pl.when(half_ref[0] != kind)
    def _():
        put(second_ref, 1 - half_ref[0])


def record(kind, half, own, first, second, mom):
    rows = mom.shape[0]
    out_shape = [shape_of((rows, D), F32), shape_of((rows, D), F32)]
    return pl.pallas_call(
        functools.partial(record_kernel, kind),
        grid=(1,),
        in_specs=[pl.BlockSpec(memory_space=pltpu.SMEM), once(own.shape), once(first.shape),
                  once(second.shape), once((rows, D))],
        out_specs=[once(leaf.shape) for leaf in out_shape],
        out_shape=out_shape,
        compiler_params=params(16),
        cost_estimate=cost(0.5, rows * D * 14),
        name="record",
    )(half, own, first, second, mom)


def one_of(stack, index):
    return pl.BlockSpec(
        (None,) + stack.shape[1:],
        lambda i: (index,) + (0,) * (stack.ndim - 1),
        pipeline_mode=pl.Buffered(1),
    )


def moment_and_gram(half, own, other, mom):
    rows = mom.shape[0]
    blocks = len(GRID_BLOCKS)
    out_shape = [shape_of((rows, D), F32), shape_of((rows, D), F32),
                 shape_of((blocks, SIDE, SIDE), F32)]
    (own, own_index), (other, other_index) = own, other
    return pl.pallas_call(
        moment_kernel,
        grid=(1,),
        in_specs=[pl.BlockSpec(memory_space=pltpu.SMEM), one_of(own, own_index),
                  one_of(other, other_index), once((rows, D))],
        out_specs=[once(leaf.shape) for leaf in out_shape],
        out_shape=out_shape,
        compiler_params=params(16),
        cost_estimate=cost(0.5, rows * D * 14 + blocks * SIDE * SIDE * 4),
        name="moment",
    )(half, own, other, mom)


def muon_kernel(step_scale, half_ref, own_ref, other_ref, moment_ref, *refs):
    *refs, gram_s, low_s, rest_s, mix_s, rows_s, gram_ref = refs
    count = own_ref.shape[0]
    for index in range(count):
        gram_ref[half_ref[0] * count + index] = own_ref[index]
        gram_ref[(1 - half_ref[0]) * count + index] = other_ref[index]
    spans = [slice(i * SIDE, (i + 1) * SIDE) for i in range(D // SIDE)]

    def put(refs, i, j, blocks):
        for ref, block in zip(refs, blocks):
            ref[spans[i], spans[j]] = block
            if i != j:
                ref[spans[j], spans[i]] = block.T

    total = jnp.zeros((1, 1), F32)
    row = lax.broadcasted_iota(jnp.int32, (SIDE, SIDE), 0)
    column = lax.broadcasted_iota(jnp.int32, (SIDE, SIDE), 1)
    for index, (i, j) in enumerate(GRID_BLOCKS):
        if i == j:
            kept = jnp.where(row == column, gram_ref[index], 0.0)
            total = total + jnp.sum(jnp.sum(kept, axis=0, keepdims=True), axis=1, keepdims=True)
    scale = 1.0 / (jnp.sqrt(total) + 1e-07)
    square = scale * scale
    for index, (i, j) in enumerate(GRID_BLOCKS):
        block = gram_ref[index] * square
        put((gram_s,), i, j, (block,))
        put((low_s, rest_s), i, j, split_value(block))
    rows_s[...] = moment_ref[...].astype(LOW)
    for iteration in range(ITERS):
        careful = iteration == 0
        for i, j in GRID_BLOCKS:
            squared = mm(low_s[spans[i], :], low_s[:, spans[j]])
            put((mix_s,), i, j, ((NS_B * gram_s[spans[i], spans[j]] + NS_C * squared).astype(LOW),))
        if iteration == ITERS - 1:
            break
        middle_blocks = []
        for i in range(D // SIDE):
            for j in range(0 if careful else i, D // SIDE):
                block = NS_A * gram_s[spans[i], spans[j]] + mm(low_s[spans[i], :], mix_s[:, spans[j]])
                if careful:
                    block = block + mm(rest_s[spans[i], :], mix_s[:, spans[j]])
                middle_blocks.append((i, j, block))
        for i, j, block in middle_blocks:
            gram_s[spans[i], spans[j]] = block
            if careful:
                low_s[spans[i], spans[j]], rest_s[spans[i], spans[j]] = split_value(block)
            else:
                put((low_s,), i, j, (block.astype(LOW),))
        renewed = NS_A * rows_s[...].astype(F32) + mm(rows_s[...], mix_s[...])
        if careful:
            renewed = renewed * scale
        rows_s[...] = renewed.astype(LOW)
        gram_blocks = []
        for i, j in GRID_BLOCKS:
            block = NS_A * gram_s[spans[i], spans[j]] + mm(mix_s[spans[i], :], low_s[:, spans[j]])
            if careful:
                block = block + mm(mix_s[spans[i], :], rest_s[:, spans[j]])
            gram_blocks.append((i, j, block))
        for i, j, block in gram_blocks:
            gram_s[spans[i], spans[j]] = block
            put((low_s,), i, j, (block.astype(LOW),))
    renewed = NS_A * rows_s[...].astype(F32) + mm(rows_s[...], mix_s[...])
    if step_scale is None:
        (ortho_ref,) = refs
        ortho_ref[...] = renewed.astype(LOW)
        return
    master_ref, new_ref, copy_ref = refs
    new = master_ref[...] * (1.0 - MUON_RATE * MUON_SHRINK) - step_scale * renewed
    new_ref[...] = new
    copy_ref[...] = new.astype(LOW)


def muon(half, own, other, moment, master=None, step_scale=None):
    rows = moment.shape[0]
    (own, own_index), (other, other_index) = own, other
    out_shape = [shape_of((rows, D), F32), shape_of((rows, D), LOW)]
    masters = [master]
    if master is None:
        out_shape, masters = out_shape[1:], []
    return pl.pallas_call(
        functools.partial(muon_kernel, step_scale),
        grid=(1,),
        in_specs=[pl.BlockSpec(memory_space=pltpu.SMEM), one_of(own, own_index),
                  one_of(other, other_index), once((rows, D))] + [once((rows, D))] * len(masters),
        out_specs=[once(leaf.shape) for leaf in out_shape],
        out_shape=out_shape,
        scratch_shapes=[pltpu.VMEM((D, D), F32), pltpu.VMEM((D, D), LOW), pltpu.VMEM((D, D), LOW),
                        pltpu.VMEM((D, D), LOW), pltpu.VMEM((rows, D), LOW),
                        pltpu.VMEM((len(GRID_BLOCKS), SIDE, SIDE), F32)],
        compiler_params=params(30),
        cost_estimate=cost(1.0, rows * D * 14),
        name="muon",
    )(half, own, other, moment, *masters)


def per_device(
    patches,
    counts,
    owners,
    pooled_cot,
    patch_cot,
    master_qkv,
    master_out,
    master_up,
    master_down,
    mom_qkv,
    mom_out,
    mom_up,
    mom_down,
    vectors,
    vec_first,
    vec_second,
):
    dp_count = lax.axis_size("dp")
    ns_count = lax.axis_size("ns")
    slot_count = patches.shape[0]
    image_total = counts.shape[1]
    capacity = pooled_cot.shape[0] // dp_count
    low = jnp.bfloat16
    place = lax.axis_index("ns").astype(jnp.int32).reshape(1)
    half_dp = bit_of("dp", 0).astype(jnp.int32).reshape(1)
    half_ns = bit_of("ns", 0).astype(jnp.int32).reshape(1)

    own_first = jnp.concatenate([master_qkv, master_out]).astype(low)
    w_first = (own_first, swap(own_first, "ns", 0), swap(own_first, "ns", 1))
    row = vectors.reshape(1, -1)
    bias_start = STARTS["bias_up"]
    bias_table = jnp.concatenate(
        by_distance(vectors[bias_start : bias_start + FF].reshape(ns_count, -1)), axis=0
    )
    returned = lax.all_to_all(
        pooled_cot.reshape(dp_count, capacity, D), "dp", split_axis=0, concat_axis=0, tiled=True
    ).reshape(dp_count * capacity, D)
    targets = owner_slots(owners[0], capacity)
    routing = (
        jnp.arange(dp_count * capacity, dtype=jnp.int32)[:, None] == targets[None, :]
    ).astype(low)
    image_cot = dot32(routing.T, returned).astype(low)
    sizes = counts[0]
    own_pair = jnp.stack([master_up, master_down]).astype(low)
    role_mom = jnp.where(bit_of("dp", 0) == 0, mom_up, mom_down)
    far_first, (own_pair, image_cot, role_mom) = tie(w_first[2], (own_pair, image_cot, role_mom))
    w_first = (w_first[0], w_first[1], far_first, swap(far_first, "ns", 0))
    own_pair, _ = tie(own_pair, far_first)
    near_pair, next_pair, far_pair = own_pair, swap(own_pair, "ns", 0), swap(own_pair, "ns", 1)
    first_low, qkv, unit, scale = project(place, patches, w_first, row)
    attn, log_total = attend(sizes, qkv)
    x2, second_low, row_grad, mixed_low = middle(
        sizes, place, patches, attn, w_first, row, patch_cot, image_cot
    )
    y, second_grad, grad_1, grad_0, bias_1, bias_0 = feed(
        (1, 0), x2, None, second_low, mixed_low, next_pair, near_pair, bias_table, row
    )
    came_1 = swap(grad_1, "ns", 0)
    y, far_pair = tie(y, far_pair)
    far_next_pair = swap(far_pair, "ns", 0)
    y, second_grad, grad_3, grad_2, bias_3, bias_2 = feed(
        (3, 2), y, second_grad, second_low, mixed_low, far_next_pair, far_pair, bias_table, row
    )
    came_3 = swap(grad_3, "ns", 0)
    kept = add_low(grad_0, came_1)
    came_3, kept = tie(came_3, kept)
    sent = add_low(grad_2, came_3)
    up, down = Chain(sum_up(kept[0], sent[0])), Chain(sum_down(kept[1], sent[1]))
    y, (sent, kept) = tie(y, (sent, kept))
    out_patches, pooled, middle_grad, attn_grad, grad_out, sums_two = after(
        sizes, place, y, x2, second_grad, row_grad, attn, w_first, row
    )
    out = Chain(sum_blocks(grad_out.reshape(ns_count, -1, D), False))
    dqkv, bias_a, gains_a, grad_qkv = attend_back(
        sizes, qkv, attn, log_total, attn_grad, unit, scale, row, first_low, (), 0
    )
    earlier = meet(up, down, out, also=(dqkv, grad_qkv))
    dqkv, bias_b, gains_b, grad_qkv = attend_back(
        sizes, qkv, attn, log_total, attn_grad, unit, scale, row, first_low, earlier, 1
    )
    outgoing = dot32(routing, pooled).astype(low).reshape(dp_count, capacity, D)
    dqkv, grad_qkv = meet(up, down, out, also=(dqkv.reshape(3 * D, slot_count), grad_qkv))
    up = Chain(rest_summed(up.result, 0, True))
    down = Chain(rest_summed(down.result, 0, True))
    three = Chain(sum_blocks(grad_qkv.reshape(ns_count, -1, D), True))
    meet(three)
    meet(up, also=three.sent)
    middle_grad = meet(down, out, also=(middle_grad, up.sent))[0]
    patch_grad, sums_one = first_back(place, patches, dqkv, w_first, row, middle_grad)
    sums_one, patch_grad = meet(three, also=(sums_one, patch_grad))
    gains = gains_a + gains_b
    up_bias_grad = by_distance(jnp.concatenate([bias_0, bias_1, bias_2, bias_3], axis=0))
    vector_local = jnp.concatenate(
        [
            sums_one[0:1],
            sums_one[1:2],
            jnp.concatenate([bias_a, bias_b], axis=2).reshape(1, 3 * D),
            gains[:, : 3 * HD],
            sums_two[2:3],
            sums_two[0:1],
            sums_two[1:2],
            *up_bias_grad,
            sums_two[3:4],
        ],
        axis=1,
    )
    vector_size = vector_local.shape[1]
    padded = -(-vector_size // 1024) * 1024
    vector = Chain(sum_vector(
        jnp.pad(vector_local, ((0, 0), (0, padded - vector_size))).reshape(-1, 128)
    ))
    moments = (mom_qkv, mom_out, mom_up, mom_down)
    masters = (master_qkv, master_out, master_up, master_down)
    grad_parts, moment_parts = [None] * 4, [None] * 4
    new_masters, copies = [None] * 4, [None] * 4

    def momentum(kind, own, other):
        grad_parts[kind], moment_parts[kind], gram = moment_and_gram(
            half_dp, own, other, moments[kind]
        )
        return Chain(sum_gram(gram))

    def iterate(kind, halves_of_gram):
        rows = moments[kind].shape[0] * ns_count
        step_scale = MUON_RATE * math.sqrt(max(1.0, rows / D))
        new_masters[kind], copies[kind] = muon(
            half_ns, *halves_of_gram, moment_parts[kind], masters[kind], step_scale
        )

    outgoing = meet(up, out, vector, also=outgoing)
    meet(three, also=up.sent)
    meet(down, also=three.sent)
    arrived = lax.all_to_all(outgoing, "dp", split_axis=0, concat_axis=0, tiled=True)
    pooled_rows = arrived.reshape(dp_count * capacity, D)
    finish(up)
    pooled_rows = meet(down, out, vector, also=(pooled_rows, up.result))[0]
    finish(down)
    pair = Chain(swap_roles(up.result, down.result))
    meet(out, vector, also=pair.sent)
    finish(out)
    gram_out = momentum(1, *((half[None], 0) for half in out.result))
    meet(gram_out)
    meet(three, also=(pair.sent, gram_out.sent))
    while pair.held != ["first"]:
        meet(pair)
    meet(pair, three, gram_out)
    role_low, gram = role_gram(half_dp, *pair.held[0], role_mom)
    gram_role = Chain(sum_gram(gram))
    meet(gram_role, three, gram_out)
    gram_own = tie(gram_out.result[0][0], (three.sent, gram_role.sent))[0]
    iterate(1, ((gram_own, 0), gram_out.result[1]))
    meet(pair, also=(gram_role.sent, new_masters[1]))
    first, second = pair.result
    for kind, own in ((2, up.result), (3, down.result)):
        grad_parts[kind], moment_parts[kind] = record(
            kind - 2, half_dp, own, first, second, moments[kind]
        )
    new_masters[1], grad_parts[2], grad_parts[3] = meet(
        gram_role, also=(new_masters[1], grad_parts[2], grad_parts[3])
    )
    meet(three, also=gram_role.sent)
    finish(three)
    gram_three = momentum(0, *((half[None], 0) for half in three.result))
    meet(gram_three, also=gram_role.sent)
    meet(gram_role, also=gram_three.sent)
    finish(vector)
    (ortho,) = muon(half_ns, *gram_role.result, role_low)
    ortho_came = swap(ortho, "dp", 0)
    meet(gram_three, also=ortho)
    finish(gram_three)
    iterate(0, gram_three.result)
    ortho_came, new_masters[0] = tie(ortho_came, new_masters[0])
    for kind in (2, 3):
        rows = moments[kind].shape[0] * ns_count
        step_scale = MUON_RATE * math.sqrt(max(1.0, rows / D))
        chosen = jnp.where(bit_of("dp", 0) == kind - 2, ortho, ortho_came).astype(jnp.float32)
        new_masters[kind] = masters[kind] * (1.0 - MUON_RATE * MUON_SHRINK) - step_scale * chosen
        copies[kind] = new_masters[kind].astype(low)
    vector_grad = vector.result.reshape(-1)[:vector_size]
    vector_first = BETA_ONE * vec_first + (1.0 - BETA_ONE) * vector_grad
    vector_second = BETA_TWO * vec_second + (1.0 - BETA_TWO) * vector_grad * vector_grad
    first_hat = vector_first / (1.0 - BETA_ONE**STEP)
    second_hat = vector_second / (1.0 - BETA_TWO**STEP)
    vector_new = vectors - ADAM_RATE * first_hat / (jnp.sqrt(second_hat) + 1e-08)
    return (
        out_patches,
        pooled_rows,
        patch_grad,
        grad_parts[0],
        grad_parts[1],
        grad_parts[2],
        grad_parts[3],
        moment_parts[0],
        moment_parts[1],
        moment_parts[2],
        moment_parts[3],
        new_masters[0],
        new_masters[1],
        new_masters[2],
        new_masters[3],
        *copies,
        vector_grad,
        vector_first,
        vector_second,
        vector_new,
    )


def solution(mesh):
    placed = (
        P(("dp", "ns"), None),
        P(("dp", "ns"), None),
        P(("dp", "ns"), None),
        P(("dp", "ns"), None),
        P(("dp", "ns"), None),
        P("ns", None),
        P("ns", None),
        P("ns", None),
        P("ns", None),
        P("ns", None),
        P("ns", None),
        P("ns", None),
        P("ns", None),
        P(),
        P(),
        P(),
    )
    return jax.shard_map(
        per_device,
        mesh=mesh,
        in_specs=placed,
        out_specs=(
            P(("dp", "ns"), None),
            P(("dp", "ns"), None),
            P(("dp", "ns"), None),
            P("ns", None),
            P("ns", None),
            P("ns", None),
            P("ns", None),
            P("ns", None),
            P("ns", None),
            P("ns", None),
            P("ns", None),
            P("ns", None),
            P("ns", None),
            P("ns", None),
            P("ns", None),
            P("ns", None),
            P("ns", None),
            P("ns", None),
            P("ns", None),
            P(),
            P(),
            P(),
            P(),
        ),
        check_vma=False,
    )
```
